128 devices in a mesh: dp: 128 (over x, z, y, core).
Axes of the slice: x: 4, y: 4, z: 4, core: 2. Of those that a mesh axis runs over, the one named last changes fastest.
Arguments:
- gradients: bfloat16 [128, 8192, 256], P('dp'), may hold values from -6 to 6
- error_memory: float32 [128, 8192, 256], P('dp'), may hold values from -4 to 4
- block_lists: int32 [128, 8, 1024], P('dp'), may hold values from 0 to 8191, as said below
- master: float32 [8192, 256], P('dp'), may hold values from -0.18 to 0.18
- first_moment: float32 [8192, 256], P('dp'), may hold values from -24 to 24
- second_moment: float32 [8192, 256], P('dp'), may hold values from 1 to 4
Outputs:
- new_errors: float32 [128, 8192, 256], P('dp')
- new_master: float32 [8192, 256], P('dp')
- new_first: float32 [8192, 256], P('dp')
- new_second: float32 [8192, 256], P('dp')
- weights: bfloat16 [8192, 256], replicated
The draws below stay inside these ranges and needn't reach their ends.
Inputs may be any that keep to these rules, and one draw needn't show every extreme that they name: block_lists[d, 0] names the 1024 distinct blocks that replica d sends; for r >= 1, block_lists[d, r] names 1024 distinct blocks, the same set for all replicas whose indices agree with d above the lowest r bits; block_lists[d, 7] is the same on every replica.
All inputs are finite; a program needn't handle non-finite values.
Results may differ from the reference program's by a relative error of at most 0.0014.
Values may be sent and summed in bfloat16 or wider, within the bound.
A program may use at most 128 MiB of HBM per device.

```python
import math
import jax
import jax.numpy as jnp
from jax import lax

BLOCK = 256
BLK_DEV = 64
LOGN = 7
NB = 8192
KEEP = 1024
N_DP = 128


def draw_block_lists(key, part):
    key = jax.random.fold_in(key, 11)
    keys = jax.random.split(key, 5)
    blocks = jnp.arange(NB, dtype=jnp.int32)
    heat = jax.random.randint(keys[0], (N_DP,), 0, 4)
    noise = jax.random.randint(keys[1], (NB,), 0, 4096)
    score = (noise + heat[blocks // BLK_DEV] * 1024) * NB + blocks
    order = jnp.argsort(-score)
    root = order[:KEEP]
    spares = order[KEEP:]
    level_ids = jnp.arange(LOGN + 1, dtype=jnp.int32)[:, None]
    groups = jnp.right_shift(jnp.arange(N_DP, dtype=jnp.int32)[None, :], level_ids)
    flags = jax.random.randint(keys[2], (LOGN + 1, N_DP, KEEP), 0, 8)
    offsets = jax.random.randint(keys[3], (LOGN + 1, N_DP), 0, NB - KEEP)
    shuffles = jax.random.randint(keys[4], (LOGN + 1, N_DP, KEEP), 0, 1 << 20)
    group_flags = flags[level_ids, groups]
    group_offsets = offsets[level_ids, groups]
    group_shuffles = shuffles[level_ids, groups]
    limit = jnp.where(level_ids == 0, 2, jnp.where(level_ids == LOGN, 0, 1))
    spots = jnp.arange(KEEP, dtype=jnp.int32)
    replaced = spares[(spots[None, None, :] + group_offsets[:, :, None]) % (NB - KEEP)]
    chosen = jnp.where(group_flags < limit[:, :, None], replaced, root[None, None, :])
    arrange = jnp.argsort(group_shuffles * KEEP + spots[None, None, :], axis=-1)
    chosen = jnp.take_along_axis(chosen, arrange, axis=-1)
    return jnp.transpose(chosen, (1, 0, 2)).astype(jnp.int32)


def level_of(own_key, extent, shards, smallest, high):
    level, own = 1.0, jax.random.fold_in(own_key, 6)
    for position, shards_of in shards:
        steps = jnp.exp(jax.random.uniform(jax.random.fold_in(own, position), (shards_of,), jnp.float32, smallest / len(shards), high / len(shards)))
        level = level * jnp.repeat(steps, extent[position] // shards_of).reshape([-1 if axis == position else 1 for axis in range(len(extent))])
    return level


def centred(own_key, shape, width, reach, shards=(), kind=jnp.bfloat16):
    entries = width * jax.random.normal(own_key, shape, jnp.float32)
    if shards:
        entries = entries * level_of(own_key, shape, shards, -0.22, 0.18)
    return jnp.clip(entries, -reach, reach).astype(kind)


def setup_inputs(seed: int = 0) -> dict:
    key_of = jax.random.split(jax.random.key(seed), 7)
    gradients = centred(key_of[0], (N_DP, NB, BLOCK), 1.0, 6.0, ((0, 128),))
    error_memory = centred(key_of[1], (N_DP, NB, BLOCK), 0.5, 4.0, ((0, 128),), jnp.float32)
    block_lists = draw_block_lists(jax.random.fold_in(key_of[6], 71), 0)
    master = centred(key_of[3], (NB, BLOCK), 0.03, 0.18, ((0, 128),), jnp.float32)
    first_moment = centred(key_of[4], (NB, BLOCK), 4.0, 24.0, ((0, 128),), jnp.float32)
    second_moment = jnp.clip(jnp.exp(math.log(4.0) - 1.3862944 * jax.random.uniform(key_of[5], (NB, BLOCK), jnp.float32) ** level_of(key_of[5], (NB, BLOCK), ((0, 128),), -0.2, 0.2)), 1.0, 4.0)
    return {"gradients": gradients, "error_memory": error_memory, "block_lists": block_lists, "master": master, "first_moment": first_moment, "second_moment": second_moment}


first_bias = 0.9999734386011124
second_bias = 0.09520785288629036

def membership(indices):
    return jnp.zeros((NB,), jnp.float32).at[indices.astype(jnp.int32)].set(1.0)

def reference(gradients, error_memory, block_lists, master, first_moment, second_moment):

    def replica(total, items):
        grad_rows, memory_rows, chain = items
        compressed = grad_rows.astype(jnp.float32) + memory_rows
        keeping = membership(chain[0])
        sent_mask = keeping
        for level in range(1, LOGN + 1):
            keeping = keeping * membership(chain[level])
        total = total + compressed * keeping[:, None]
        return (total, compressed * (1.0 - sent_mask)[:, None])
    summed, new_errors = lax.scan(replica, jnp.zeros((NB, BLOCK), jnp.float32), (gradients, error_memory, block_lists))
    new_first = 0.9 * first_moment + 0.1 * summed
    new_second = 0.999 * second_moment + 0.001 * summed * summed
    first_hat = new_first / first_bias
    second_hat = new_second / second_bias
    new_master = master - 0.001 * (first_hat / (jnp.sqrt(second_hat) + 1e-08) + 0.1 * master)
    weights = new_master.astype(jnp.bfloat16)
    return (new_errors, new_master, new_first, new_second, weights)
```

```python
import functools

import jax
import jax.numpy as jnp
from jax import lax
from jax.experimental import pallas as pl
from jax.experimental.pallas import tpu as pltpu
from jax.sharding import PartitionSpec as P

FIRST_BIAS = 0.9999734386011124
SECOND_BIAS = 0.09520785288629036
MESH = pl.DeviceIdType.MESH
F32 = jnp.float32
BF16 = jnp.bfloat16
MIB = 1 << 20

GROUP = 128
CHUNK = 512


def iota(shape, dim):
    return lax.broadcasted_iota(jnp.int32, shape, dim)


def onehot(hits):
    return jnp.where(hits, 1.0, 0.0).astype(BF16)


def adamw(master, first, second, summed):
    new_first = 0.9 * first + 0.1 * summed
    new_second = 0.999 * second + 0.001 * summed * summed
    first_hat = new_first / FIRST_BIAS
    second_hat = new_second / SECOND_BIAS
    new_master = master - 0.001 * (
        first_hat / (jnp.sqrt(second_hat) + 1e-08) + 0.1 * master
    )
    return new_master, new_first, new_second


def pack_kernel(
    grad_hbm, err_hbm, lists, out_hbm, packed, expand,
    grad, err, acc, sent, kept, starts_v, rooted, column, starts,
    grad_sem, err_sem, out_sem, starts_sem,
):
    rows = grad.shape[0]
    groups = rows // GROUP
    keep_n = lists.shape[1]
    chunks = rows // CHUNK

    def loads(i):
        span = pl.ds(i * CHUNK, CHUNK)
        return (
            pltpu.make_async_copy(grad_hbm.at[0, span], grad.at[span], grad_sem.at[i]),
            pltpu.make_async_copy(err_hbm.at[0, span], err.at[span], err_sem.at[i]),
        )

    def store(i):
        span = pl.ds(i * CHUNK, CHUNK)
        return pltpu.make_async_copy(err.at[span], out_hbm.at[0, span], out_sem.at[i])

    for i in range(chunks):
        for copy in loads(i):
            copy.start()

    acc[...] = jnp.zeros_like(acc)

    def member(r):
        ids = lists[r : r + 1, :]
        high = onehot(iota((groups, keep_n), 0) == ids // GROUP)
        low = onehot(iota((GROUP, keep_n), 0) == ids % GROUP)
        return lax.dot_general(
            high, low, (((1,), (1,)), ((), ())), preferred_element_type=F32
        )

    levels = lists.shape[0]
    first = member(0)
    sent[...] = first
    keep = first
    for r in range(1, levels - 1):
        keep = keep * member(r)
    root = member(levels - 1)
    keep = keep * root

    root_b = root.astype(BF16)
    before = onehot(iota((GROUP, GROUP), 0) < iota((GROUP, GROUP), 1))
    inside = jnp.dot(root_b, before, preferred_element_type=F32)
    total = jnp.dot(root_b, jnp.ones((GROUP, GROUP), BF16), preferred_element_type=F32)
    above = onehot(iota((groups, groups), 1) < iota((groups, groups), 0))
    start = jnp.dot(above, total.astype(BF16), preferred_element_type=F32)
    rank = (start + inside).astype(jnp.int32)
    starts_v[...] = start.astype(jnp.int32)
    to_smem = pltpu.make_async_copy(starts_v, starts, starts_sem)
    to_smem.start()
    kept[...] = jnp.where(keep > 0.5, rank, -1)
    rooted[...] = jnp.where(root > 0.5, rank, -1)

    me = lax.axis_index("dp")
    own = rooted[pl.ds(me // 2, 1), :].astype(F32)
    column[...] = jnp.transpose(jnp.broadcast_to(own, (GROUP, GROUP)))
    half = column[pl.ds((me % 2) * 64, 64), :]
    for k in range(keep_n // GROUP):
        lanes = (iota((64, GROUP), 1) + k * GROUP).astype(F32)
        expand[:, k * GROUP : (k + 1) * GROUP] = onehot(half == lanes)
    to_smem.wait()

    diagonal = iota((GROUP, GROUP), 0) == iota((GROUP, GROUP), 1)
    window = GROUP + 8

    def step(i, _):
        for copy in loads(i):
            copy.wait()
        for j in range(CHUNK // GROUP):
            g = i * (CHUNK // GROUP) + j
            span = pl.ds(pl.multiple_of(g * GROUP, GROUP), GROUP)
            value = grad[span, :].astype(F32) + err[span, :]
            stays = 1.0 - sent[pl.ds(g, 1), :]
            spread = jnp.dot(
                jnp.where(diagonal, stays, 0.0).astype(BF16),
                jnp.ones((GROUP, value.shape[1]), BF16),
                preferred_element_type=F32,
            )
            err[span, :] = value * spread
            base = pl.multiple_of((starts[g, 0] // 8) * 8, 8)
            place = kept[pl.ds(g, 1), :] - base
            hits = onehot(iota((window, GROUP), 0) == place)
            acc[pl.ds(base, window), :] += jnp.dot(
                hits, value.astype(BF16), preferred_element_type=F32
            )
        store(i).start()
        return 0

    lax.fori_loop(0, chunks, step, 0)
    for c in range(2):
        part = acc[0:keep_n, c * 128 : (c + 1) * 128].astype(BF16)
        packed[c] = part.reshape(packed.shape[1:])
    lax.fori_loop(0, chunks, lambda i, _: (store(i).wait(), 0)[1], 0)


def merge_kernel(
    packed, expand, master, first, second, weights, summed,
    from_core, part, sum1, part1, sum2, part2, got1, got2, got3, sums,
    core_send, core_recv, rs_send, rs_recv, ag_send, ag_recv,
    half_send, half_recv, w_send, w_recv, f_send, f_recv,
):
    me = lax.axis_index("dp")
    c = me % 2
    y = (me // 2) % 4
    z = (me // 8) % 4
    x = me // 32
    sibling = me + 1 - 2 * c

    def along(coord, stride, k):
        return me + ((coord + k) % 4 - coord) * stride

    def copy(src, dst, send, recv, peer):
        return pltpu.make_async_remote_copy(
            src_ref=src, dst_ref=dst, send_sem=send, recv_sem=recv,
            device_id=(peer,), device_id_type=MESH,
        )

    barrier = pltpu.get_barrier_semaphore()
    peers = [sibling]
    for coord, stride in ((x, 32), (z, 8), (y, 2)):
        peers += [along(coord, stride, k) for k in (1, 2, 3)]
    for peer in peers:
        pl.semaphore_signal(barrier, inc=1, device_id=(peer,), device_id_type=MESH)
    pl.semaphore_wait(barrier, len(peers))

    pending = []

    d = 1 - c
    a1, s1 = d * x + c * z, d * 32 + c * 8
    a2, s2 = d * z + c * y, d * 8 + c * 2
    a3, s3 = d * y + c * x, d * 2 + c * 32

    swap = copy(packed.at[d], from_core, core_send, core_recv, sibling)
    swap.start()
    swap.wait_recv()
    pending.append(swap)
    part[...] = (packed[c].astype(F32) + from_core[...].astype(F32)).astype(BF16)

    def reduce(phase, source, coord, stride, got, own):
        sends = []
        for k in (1, 2, 3):
            go = copy(
                source.at[(coord + k) % 4], got.at[k - 1],
                rs_send.at[phase, k - 1], rs_recv.at[phase, k - 1],
                along(coord, stride, k),
            )
            go.start()
            sends.append(go)
        pending.extend(sends)
        total = own
        for k in (1, 2, 3):
            sends[k - 1].wait_recv()
            total = total + got[k - 1].astype(F32)
        return total

    sum1[...] = reduce(
        0, part, a1, s1, got1, packed[c, a1].astype(F32) + from_core[a1].astype(F32)
    )
    part1[...] = sum1[...].astype(BF16)
    sum2[...] = reduce(1, part1, a2, s2, got2, sum1[a2])
    part2[...] = sum2[...].astype(BF16)
    sums[c, a1, a2, a3] = reduce(2, part2, a3, s3, got3, sum2[a3]).astype(BF16)

    def gather(phase, block, coord, stride):
        sends = []
        for k in (1, 2, 3):
            go = copy(
                block, block, ag_send.at[phase, k - 1], ag_recv.at[phase, k - 1],
                along(coord, stride, k),
            )
            go.start()
            sends.append(go)
        pending.extend(sends)
        return sends

    for go in gather(0, sums.at[c, a1, a2, a3], a3, s3):
        go.wait_recv()
    for go in gather(1, sums.at[c, a1, a2], a2, s2):
        go.wait_recv()
    last = gather(2, sums.at[c, a1], a1, s1)
    halves = []
    for k in range(4):
        if k:
            last[k - 1].wait_recv()
        block = sums.at[c, (a1 - k + 4) % 4]
        go = copy(block, block, half_send.at[k], half_recv.at[k], sibling)
        go.start()
        halves.append(go)
    for go in halves:
        go.wait_recv()
    pending.extend(halves)

    for h in range(2):
        lanes = slice(h * 128, (h + 1) * 128)
        total = jnp.dot(
            expand[...], sums[h].reshape(-1, 128), preferred_element_type=F32
        )
        summed[:, lanes] = total
        new_master, _, _ = adamw(
            master[:, lanes], first[:, lanes], second[:, lanes], total
        )
        weights[x, z, y, c, h] = new_master.astype(BF16)

    def blocks(ref, taken, half, rows):
        index = tuple(
            pl.ds(0, 4) if axis in taken else coord
            for axis, coord in (("x", x), ("z", z), ("y", y))
        )
        return ref.at[(*index, c, *half, rows)]

    where = {"x": (x, 32), "z": (z, 8), "y": (y, 2)}
    streams = (
        ("xzy", (0,), pl.ds(0, 48)),
        ("zyx", (1,), pl.ds(0, 48)),
        ("yxz", (pl.ds(0, 2),), pl.ds(48, 16)),
    )

    def forward(block, sem):
        go = copy(block, block, f_send.at[sem], f_recv.at[sem], sibling)
        go.start()
        pending.append(go)
        return go

    forwards = []
    mine = weights.at[x, z, y, c]
    waiting = [[] for _ in streams]
    for phase in range(3):
        for s, (order, half, rows) in enumerate(streams):
            for go, _ in waiting[s]:
                go.wait_recv()
            taken = order[:phase]
            coord, stride = where[order[phase]]
            block = blocks(weights, taken, half, rows)
            arrived = waiting[s]
            waiting[s] = []
            for k in (1, 2, 3):
                n = (s * 3 + phase) * 3 + k - 1
                go = copy(block, block, w_send.at[n], w_recv.at[n], along(coord, stride, k))
                go.start()
                pending.append(go)
                origin = tuple(
                    pl.ds(0, 4) if axis in taken
                    else ((at - k + 4) % 4 if axis == order[phase] else at)
                    for axis, at in (("x", x), ("z", z), ("y", y))
                )
                waiting[s].append((go, (weights.at[(*origin, c, *half, rows)], n)))
            for _, (came, n) in arrived:
                forwards.append(forward(came, n))
        if phase == 0:
            forwards.append(forward(mine, 27))
    for k in range(3):
        for s in range(3):
            go, (came, n) = waiting[s][k]
            go.wait_recv()
            forwards.append(forward(came, n))
    for go in forwards:
        go.wait_recv()
    for go in pending:
        go.wait_send()


def finish_kernel(
    weights, summed, master, first, second,
    out_hbm, new_master, new_first, new_second, sems,
):
    copies = []
    for h in range(2):
        go = pltpu.make_async_copy(
            weights.at[:, h], out_hbm.at[:, :, pl.ds(h * 128, 128)], sems.at[h]
        )
        go.start()
        copies.append(go)
    new_master[...], new_first[...], new_second[...] = adamw(
        master[...], first[...], second[...], summed[...]
    )
    for go in copies:
        go.wait()


def body(gradients, error_memory, block_lists, master, first_moment, second_moment):
    _, rows, width = gradients.shape
    owned = master.shape[0]
    devices = lax.axis_size("dp")
    levels, keep_n = block_lists.shape[1:]
    groups = rows // GROUP
    chunks = rows // CHUNK
    vmem = pl.BlockSpec(memory_space=pltpu.VMEM)
    anywhere = pl.BlockSpec(memory_space=pl.ANY)
    dma = pltpu.SemaphoreType.DMA

    new_errors, packed, expand = pl.pallas_call(
        pack_kernel,
        out_shape=(
            jax.ShapeDtypeStruct((1, rows, width), F32),
            jax.ShapeDtypeStruct((2, 4, 4, 4, 16, 128), BF16),
            jax.ShapeDtypeStruct((owned, keep_n), BF16),
        ),
        in_specs=[anywhere, anywhere, vmem],
        out_specs=(anywhere, vmem, vmem),
        scratch_shapes=[
            pltpu.VMEM((rows, width), BF16),
            pltpu.VMEM((rows, width), F32),
            pltpu.VMEM((keep_n + GROUP + 8, width), F32),
            pltpu.VMEM((groups, GROUP), F32),
            pltpu.VMEM((groups, GROUP), jnp.int32),
            pltpu.VMEM((groups, GROUP), jnp.int32),
            pltpu.VMEM((groups, GROUP), jnp.int32),
            pltpu.VMEM((GROUP, GROUP), F32),
            pltpu.SMEM((groups, GROUP), jnp.int32),
            dma((chunks,)),
            dma((chunks,)),
            dma((chunks,)),
            dma,
        ],
        compiler_params=pltpu.CompilerParams(vmem_limit_bytes=32 * MIB),
        name="pack",
    )(gradients, error_memory, block_lists[0])

    weights, summed = pl.pallas_call(
        merge_kernel,
        out_shape=(
            pltpu.VMEM((4, 4, 4, 2, 2, owned, 128), BF16),
            jax.ShapeDtypeStruct((owned, width), F32),
        ),
        in_specs=[vmem] * 5,
        out_specs=(vmem, vmem),
        scratch_shapes=[
            pltpu.VMEM((4, 4, 4, 16, 128), BF16),
            pltpu.VMEM((4, 4, 4, 16, 128), BF16),
            pltpu.VMEM((4, 4, 16, 128), F32),
            pltpu.VMEM((4, 4, 16, 128), BF16),
            pltpu.VMEM((4, 16, 128), F32),
            pltpu.VMEM((4, 16, 128), BF16),
            pltpu.VMEM((3, 4, 4, 16, 128), BF16),
            pltpu.VMEM((3, 4, 16, 128), BF16),
            pltpu.VMEM((3, 16, 128), BF16),
            pltpu.VMEM((2, 4, 4, 4, 16, 128), BF16),
            dma, dma,
            dma((3, 3)), dma((3, 3)),
            dma((3, 3)), dma((3, 3)),
            dma((4,)), dma((4,)),
            dma((27,)), dma((27,)),
            dma((28,)), dma((28,)),
        ],
        compiler_params=pltpu.CompilerParams(
            collective_id=0, has_side_effects=True, vmem_limit_bytes=24 * MIB
        ),
        name="merge",
    )(packed, expand, master, first_moment, second_moment)

    weights = weights.reshape(devices, 2, owned, 128)
    out, new_master, new_first, new_second = pl.pallas_call(
        finish_kernel,
        out_shape=(
            jax.ShapeDtypeStruct((devices, owned, width), BF16),
            jax.ShapeDtypeStruct((owned, width), F32),
            jax.ShapeDtypeStruct((owned, width), F32),
            jax.ShapeDtypeStruct((owned, width), F32),
        ),
        in_specs=[vmem] * 5,
        out_specs=(anywhere, vmem, vmem, vmem),
        scratch_shapes=[dma((2,))],
        compiler_params=pltpu.CompilerParams(vmem_limit_bytes=24 * MIB),
        name="finish",
    )(weights, summed, master, first_moment, second_moment)
    return new_errors, new_master, new_first, new_second, out.reshape(rows, width)


def solution(mesh):
    in_specs = (
        P("dp", None, None),
        P("dp", None, None),
        P("dp", None, None),
        P("dp", None),
        P("dp", None),
        P("dp", None),
    )
    out_specs = (P("dp", None, None), P("dp", None), P("dp", None), P("dp", None), P())
    return jax.shard_map(
        body, mesh=mesh, in_specs=in_specs, out_specs=out_specs, check_vma=False
    )
```

```python
import functools

import jax
import jax.numpy as jnp
from jax import lax
from jax.experimental import pallas as pl
from jax.experimental.pallas import tpu as pltpu
from jax.sharding import PartitionSpec as P

FIRST_BIAS = 0.9999734386011124
SECOND_BIAS = 0.09520785288629036
MESH = pl.DeviceIdType.MESH
F32 = jnp.float32
BF16 = jnp.bfloat16
MIB = 1 << 20

GROUP = 128
CHUNK = 512


def iota(shape, dim):
    return lax.broadcasted_iota(jnp.int32, shape, dim)


def onehot(hits):
    return jnp.where(hits, 1.0, 0.0).astype(BF16)


def adamw(master, first, second, summed):
    new_first = 0.9 * first + 0.1 * summed
    new_second = 0.999 * second + 0.001 * summed * summed
    first_hat = new_first / FIRST_BIAS
    second_hat = new_second / SECOND_BIAS
    new_master = master - 0.001 * (
        first_hat / (jnp.sqrt(second_hat) + 1e-08) + 0.1 * master
    )
    return new_master, new_first, new_second


def pack_kernel(
    grad_hbm, err_hbm, lists, out_hbm, packed, expand,
    grad, err, acc, sent, kept, starts_v, rooted, column, starts,
    grad_sem, err_sem, out_sem, starts_sem,
):
    rows = grad.shape[0]
    groups = rows // GROUP
    keep_n = lists.shape[1]
    chunks = rows // CHUNK

    def loads(i):
        span = pl.ds(i * CHUNK, CHUNK)
        return (
            pltpu.make_async_copy(grad_hbm.at[0, span], grad.at[span], grad_sem.at[i]),
            pltpu.make_async_copy(err_hbm.at[0, span], err.at[span], err_sem.at[i]),
        )

    def store(i):
        span = pl.ds(i * CHUNK, CHUNK)
        return pltpu.make_async_copy(err.at[span], out_hbm.at[0, span], out_sem.at[i])

    for i in range(chunks):
        for copy in loads(i):
            copy.start()

    acc[...] = jnp.zeros_like(acc)

    def member(r):
        ids = lists[r : r + 1, :]
        high = onehot(iota((groups, keep_n), 0) == ids // GROUP)
        low = onehot(iota((GROUP, keep_n), 0) == ids % GROUP)
        return lax.dot_general(
            high, low, (((1,), (1,)), ((), ())), preferred_element_type=F32
        )

    levels = lists.shape[0]
    first = member(0)
    sent[...] = first
    keep = first
    for r in range(1, levels - 1):
        keep = keep * member(r)
    root = member(levels - 1)
    keep = keep * root

    root_b = root.astype(BF16)
    before = onehot(iota((GROUP, GROUP), 0) < iota((GROUP, GROUP), 1))
    inside = jnp.dot(root_b, before, preferred_element_type=F32)
    total = jnp.dot(root_b, jnp.ones((GROUP, GROUP), BF16), preferred_element_type=F32)
    above = onehot(iota((groups, groups), 1) < iota((groups, groups), 0))
    start = jnp.dot(above, total.astype(BF16), preferred_element_type=F32)
    rank = (start + inside).astype(jnp.int32)
    starts_v[...] = start.astype(jnp.int32)
    to_smem = pltpu.make_async_copy(starts_v, starts, starts_sem)
    to_smem.start()
    kept[...] = jnp.where(keep > 0.5, rank, -1)
    rooted[...] = jnp.where(root > 0.5, rank, -1)

    me = lax.axis_index("dp")
    own = rooted[pl.ds(me // 2, 1), :].astype(F32)
    column[...] = jnp.transpose(jnp.broadcast_to(own, (GROUP, GROUP)))
    half = column[pl.ds((me % 2) * 64, 64), :]
    for k in range(keep_n // GROUP):
        lanes = (iota((64, GROUP), 1) + k * GROUP).astype(F32)
        expand[:, k * GROUP : (k + 1) * GROUP] = onehot(half == lanes)
    to_smem.wait()

    diagonal = iota((GROUP, GROUP), 0) == iota((GROUP, GROUP), 1)
    window = GROUP + 8

    def step(i, _):
        for copy in loads(i):
            copy.wait()
        for j in range(CHUNK // GROUP):
            g = i * (CHUNK // GROUP) + j
            span = pl.ds(pl.multiple_of(g * GROUP, GROUP), GROUP)
            value = grad[span, :].astype(F32) + err[span, :]
            stays = 1.0 - sent[pl.ds(g, 1), :]
            spread = jnp.dot(
                jnp.where(diagonal, stays, 0.0).astype(BF16),
                jnp.ones((GROUP, value.shape[1]), BF16),
                preferred_element_type=F32,
            )
            err[span, :] = value * spread
            base = pl.multiple_of((starts[g, 0] // 8) * 8, 8)
            place = kept[pl.ds(g, 1), :] - base
            hits = onehot(iota((window, GROUP), 0) == place)
            acc[pl.ds(base, window), :] += jnp.dot(
                hits, value.astype(BF16), preferred_element_type=F32
            )
        store(i).start()
        return 0

    lax.fori_loop(0, chunks, step, 0)
    for c in range(2):
        part = acc[0:keep_n, c * 128 : (c + 1) * 128].astype(BF16)
        packed[c] = part.reshape(packed.shape[1:])
    lax.fori_loop(0, chunks, lambda i, _: (store(i).wait(), 0)[1], 0)


def merge_kernel(
    packed, expand, master, first, second, weights, summed,
    from_core, part, got, sums,
    core_send, core_recv, rs_send, rs_recv, ag_send, ag_recv,
    half_send, half_recv, w_send, w_recv, f_send, f_recv,
):
    me = lax.axis_index("dp")
    c = me % 2
    y = (me // 2) % 4
    z = (me // 8) % 4
    x = me // 32
    sibling = me + 1 - 2 * c

    def along(coord, stride, k):
        return me + ((coord + k) % 4 - coord) * stride

    def copy(src, dst, send, recv, peer):
        return pltpu.make_async_remote_copy(
            src_ref=src, dst_ref=dst, send_sem=send, recv_sem=recv,
            device_id=(peer,), device_id_type=MESH,
        )

    chip = me // 2
    chips = packed.shape[1]

    def far(k):
        other = (chip + k) % chips
        return other, 2 * other + c

    barrier = pltpu.get_barrier_semaphore()

    def greet(k, _):
        pl.semaphore_signal(
            barrier, inc=1, device_id=(far(k)[1],), device_id_type=MESH
        )
        return 0

    pl.semaphore_signal(barrier, inc=1, device_id=(sibling,), device_id_type=MESH)
    lax.fori_loop(1, chips, greet, 0)
    pl.semaphore_wait(barrier, chips)

    pending = []
    swap = copy(packed.at[1 - c], from_core, core_send, core_recv, sibling)
    swap.start()
    swap.wait_recv()
    part[...] = (packed[c].astype(F32) + from_core[...].astype(F32)).astype(BF16)

    def scatter(k):
        other, peer = far(k)
        return copy(part.at[other], got.at[k - 1], rs_send.at[k], rs_recv.at[k], peer)

    def gather(k):
        unit = sums.at[c, chip]
        return copy(unit, unit, ag_send.at[k], ag_recv.at[k], far(k)[1])

    def each(act):
        lax.fori_loop(1, chips, lambda k, _: (act(k), 0)[1], 0)

    each(lambda k: scatter(k).start())
    own = packed[c, chip].astype(F32) + from_core[chip].astype(F32)
    each(lambda k: scatter(k).wait_recv())
    sums[c, chip] = (own + jnp.sum(got[...].astype(F32), axis=0)).astype(BF16)
    each(lambda k: gather(k).start())
    each(lambda k: gather(k).wait_recv())
    block = sums.at[c]
    halves = copy(block, block, half_send, half_recv, sibling)
    halves.start()
    each(lambda k: scatter(k).wait_send())
    each(lambda k: gather(k).wait_send())
    swap.wait_send()
    halves.wait_recv()
    pending.append(halves)

    for h in range(2):
        lanes = slice(h * 128, (h + 1) * 128)
        total = jnp.dot(
            expand[...], sums[h].reshape(-1, 128), preferred_element_type=F32
        )
        summed[:, lanes] = total
        new_master, _, _ = adamw(
            master[:, lanes], first[:, lanes], second[:, lanes], total
        )
        weights[x, z, y, c, h] = new_master.astype(BF16)

    def blocks(ref, taken, half, rows):
        index = tuple(
            pl.ds(0, 4) if axis in taken else coord
            for axis, coord in (("x", x), ("z", z), ("y", y))
        )
        return ref.at[(*index, c, *half, rows)]

    where = {"x": (x, 32), "z": (z, 8), "y": (y, 2)}
    streams = (
        ("xzy", (0,), pl.ds(0, 48)),
        ("zyx", (1,), pl.ds(0, 48)),
        ("yxz", (pl.ds(0, 2),), pl.ds(48, 16)),
    )

    def forward(block, sem):
        go = copy(block, block, f_send.at[sem], f_recv.at[sem], sibling)
        go.start()
        pending.append(go)
        return go

    forwards = []
    mine = weights.at[x, z, y, c]
    waiting = [[] for _ in streams]
    for phase in range(3):
        for s, (order, half, rows) in enumerate(streams):
            for go, _ in waiting[s]:
                go.wait_recv()
            taken = order[:phase]
            coord, stride = where[order[phase]]
            block = blocks(weights, taken, half, rows)
            arrived = waiting[s]
            waiting[s] = []
            for k in (1, 2, 3):
                n = (s * 3 + phase) * 3 + k - 1
                go = copy(block, block, w_send.at[n], w_recv.at[n], along(coord, stride, k))
                go.start()
                pending.append(go)
                origin = tuple(
                    pl.ds(0, 4) if axis in taken
                    else ((at - k + 4) % 4 if axis == order[phase] else at)
                    for axis, at in (("x", x), ("z", z), ("y", y))
                )
                waiting[s].append((go, (weights.at[(*origin, c, *half, rows)], n)))
            for _, (came, n) in arrived:
                forwards.append(forward(came, n))
        if phase == 0:
            forwards.append(forward(mine, 27))
    for k in range(3):
        for s in range(3):
            go, (came, n) = waiting[s][k]
            go.wait_recv()
            forwards.append(forward(came, n))
    for go in forwards:
        go.wait_recv()
    for go in pending:
        go.wait_send()


def finish_kernel(
    weights, summed, master, first, second,
    out_hbm, new_master, new_first, new_second, sems,
):
    copies = []
    for h in range(2):
        go = pltpu.make_async_copy(
            weights.at[:, h], out_hbm.at[:, :, pl.ds(h * 128, 128)], sems.at[h]
        )
        go.start()
        copies.append(go)
    new_master[...], new_first[...], new_second[...] = adamw(
        master[...], first[...], second[...], summed[...]
    )
    for go in copies:
        go.wait()


def body(gradients, error_memory, block_lists, master, first_moment, second_moment):
    _, rows, width = gradients.shape
    owned = master.shape[0]
    devices = lax.axis_size("dp")
    levels, keep_n = block_lists.shape[1:]
    groups = rows // GROUP
    chunks = rows // CHUNK
    vmem = pl.BlockSpec(memory_space=pltpu.VMEM)
    anywhere = pl.BlockSpec(memory_space=pl.ANY)
    hbm = pl.BlockSpec(memory_space=pltpu.HBM)
    dma = pltpu.SemaphoreType.DMA

    new_errors, packed, expand = pl.pallas_call(
        pack_kernel,
        out_shape=(
            jax.ShapeDtypeStruct((1, rows, width), F32),
            jax.ShapeDtypeStruct((2, 64, 16, 128), BF16),
            jax.ShapeDtypeStruct((owned, keep_n), BF16),
        ),
        in_specs=[hbm, hbm, vmem],
        out_specs=(anywhere, vmem, vmem),
        scratch_shapes=[
            pltpu.VMEM((rows, width), BF16),
            pltpu.VMEM((rows, width), F32),
            pltpu.VMEM((keep_n + GROUP + 8, width), F32),
            pltpu.VMEM((groups, GROUP), F32),
            pltpu.VMEM((groups, GROUP), jnp.int32),
            pltpu.VMEM((groups, GROUP), jnp.int32),
            pltpu.VMEM((groups, GROUP), jnp.int32),
            pltpu.VMEM((GROUP, GROUP), F32),
            pltpu.SMEM((groups, GROUP), jnp.int32),
            dma((chunks,)),
            dma((chunks,)),
            dma((chunks,)),
            dma,
        ],
        compiler_params=pltpu.CompilerParams(vmem_limit_bytes=32 * MIB),
        name="pack",
    )(gradients, error_memory, block_lists[0])

    weights, summed = pl.pallas_call(
        merge_kernel,
        out_shape=(
            pltpu.VMEM((4, 4, 4, 2, 2, owned, 128), BF16),
            jax.ShapeDtypeStruct((owned, width), F32),
        ),
        in_specs=[vmem] * 5,
        out_specs=(vmem, vmem),
        scratch_shapes=[
            pltpu.VMEM((64, 16, 128), BF16),
            pltpu.VMEM((64, 16, 128), BF16),
            pltpu.VMEM((63, 16, 128), BF16),
            pltpu.VMEM((2, 64, 16, 128), BF16),
            dma, dma,
            dma((64,)), dma((64,)),
            dma((64,)), dma((64,)),
            dma, dma,
            dma((27,)), dma((27,)),
            dma((28,)), dma((28,)),
        ],
        compiler_params=pltpu.CompilerParams(
            collective_id=0, has_side_effects=True, vmem_limit_bytes=24 * MIB
        ),
        name="merge",
    )(packed, expand, master, first_moment, second_moment)

    weights = weights.reshape(devices, 2, owned, 128)
    out, new_master, new_first, new_second = pl.pallas_call(
        finish_kernel,
        out_shape=(
            jax.ShapeDtypeStruct((devices, owned, width), BF16),
            jax.ShapeDtypeStruct((owned, width), F32),
            jax.ShapeDtypeStruct((owned, width), F32),
            jax.ShapeDtypeStruct((owned, width), F32),
        ),
        in_specs=[vmem] * 5,
        out_specs=(anywhere, vmem, vmem, vmem),
        scratch_shapes=[dma((2,))],
        compiler_params=pltpu.CompilerParams(vmem_limit_bytes=24 * MIB),
        name="finish",
    )(weights, summed, master, first_moment, second_moment)
    return new_errors, new_master, new_first, new_second, out.reshape(rows, width)


def solution(mesh):
    in_specs = (
        P("dp", None, None),
        P("dp", None, None),
        P("dp", None, None),
        P("dp", None),
        P("dp", None),
        P("dp", None),
    )
    out_specs = (P("dp", None, None), P("dp", None), P("dp", None), P("dp", None), P())
    return jax.shard_map(
        body, mesh=mesh, in_specs=in_specs, out_specs=out_specs, check_vma=False
    )
```

```python
import jax
import jax.numpy as jnp
from jax import lax
from jax.experimental import pallas as pl
from jax.experimental.pallas import tpu as pltpu
from jax.sharding import PartitionSpec as P

FIRST_BIAS = 0.9999734386011124
SECOND_BIAS = 0.09520785288629036
MESH = pl.DeviceIdType.MESH
F32 = jnp.float32
BF16 = jnp.bfloat16
MIB = 1 << 20

GROUP = 128
CHUNK = 512
UNIT = 16
SPAN = 256

ORDERS = ("xzy", "zyx", "yxz")


def iota(shape, dim):
    return lax.broadcasted_iota(jnp.int32, shape, dim)


def onehot(hits):
    return jnp.where(hits, 1.0, 0.0).astype(BF16)


def adamw(master, first, second, summed):
    new_first = 0.9 * first + 0.1 * summed
    new_second = 0.999 * second + 0.001 * summed * summed
    first_hat = new_first / FIRST_BIAS
    second_hat = new_second / SECOND_BIAS
    new_master = master - 0.001 * (
        first_hat / (jnp.sqrt(second_hat) + 1e-08) + 0.1 * master
    )
    return new_master, new_first, new_second


def merge_kernel(
    grad_hbm, err_hbm, lists_hbm, master_hbm, first_hbm, second_hbm,
    err, weights, result, expand, rooted, starts,
    grad, lists, raw, state_rows, acc, sent, kept, column, value_b,
    packed, from_core, part, got,
    state, state1, state2, state3, sgot1, sgot2, sgot3,
    grad_sem, err_sem, list_sem, raw_sem,
    core_send, core_recv, raw_send, raw_recv,
    rs_send, rs_recv, ag_send, ag_recv, half_send, half_recv,
    s_send, s_recv, w_send, w_recv, f_send, f_recv,
):
    rows = grad.shape[0]
    groups = rows // GROUP
    chunks = rows // CHUNK
    levels, keep_n = lists.shape
    me = lax.axis_index("dp")
    c = me % 2
    y = (me // 2) % 4
    z = (me // 8) % 4
    x = me // 32
    chip = me // 2
    chips = groups
    sibling = me + 1 - 2 * c
    at = {"x": x, "z": z, "y": y}
    strides = {"x": 32, "z": 8, "y": 2}

    def far(k):
        other = (chip + k) % chips
        return other, 2 * other + c

    def along(axis, k):
        return me + ((at[axis] + k) % 4 - at[axis]) * strides[axis]

    def copy(src, dst, send, recv, peer):
        return pltpu.make_async_remote_copy(
            src_ref=src, dst_ref=dst, send_sem=send, recv_sem=recv,
            device_id=(peer,), device_id_type=MESH,
        )

    def each(act, first=1):
        lax.fori_loop(first, chips, lambda k, _: (act(k), 0)[1], 0)

    list_load = pltpu.make_async_copy(lists_hbm.at[0], lists, list_sem)
    list_load.start()
    raw_loads = []
    for a, source in enumerate((master_hbm, first_hbm, second_hbm)):
        for h in range(2):
            go = pltpu.make_async_copy(
                source.at[:, pl.ds(h * 128, 128)], raw.at[h, a], raw_sem.at[h, a]
            )
            go.start()
            raw_loads.append(go)

    def loads(i):
        span = pl.ds(pl.multiple_of(i * CHUNK, CHUNK), CHUNK)
        return (
            pltpu.make_async_copy(grad_hbm.at[0, span], grad.at[span], grad_sem.at[i]),
            pltpu.make_async_copy(err_hbm.at[0, span], err.at[0, span], err_sem.at[i]),
        )

    def load(i, _):
        for go in loads(i):
            go.start()
        return 0

    lax.fori_loop(0, chunks, load, 0)

    barrier = pltpu.get_barrier_semaphore()
    pl.semaphore_signal(barrier, inc=1, device_id=(sibling,), device_id_type=MESH)
    each(
        lambda k: pl.semaphore_signal(
            barrier, inc=1, device_id=(far(k)[1],), device_id_type=MESH
        )
    )

    list_load.wait()

    def member(r):
        ids = lists[r : r + 1, :]
        high = onehot(iota((groups, keep_n), 0) == ids // GROUP)
        low = onehot(iota((GROUP, keep_n), 0) == ids % GROUP)
        return lax.dot_general(
            high, low, (((1,), (1,)), ((), ())), preferred_element_type=F32
        )

    root = member(levels - 1)
    root_b = root.astype(BF16)
    before = onehot(iota((GROUP, GROUP), 0) < iota((GROUP, GROUP), 1))
    inside = jnp.dot(root_b, before, preferred_element_type=F32)
    total = jnp.dot(root_b, jnp.ones((GROUP, GROUP), BF16), preferred_element_type=F32)
    above = onehot(iota((groups, groups), 1) < iota((groups, groups), 0))
    start = jnp.dot(above, total.astype(BF16), preferred_element_type=F32)
    rank = start + inside
    starts[...] = start.astype(jnp.int32)
    rooted[...] = jnp.where(root > 0.5, rank, -1.0)

    keep = member(0)
    sent[...] = keep
    for r in range(1, levels - 1):
        keep = keep * member(r)
    kept[...] = jnp.where(keep * root > 0.5, rank, -1.0)

    chip_ranks = rooted[pl.ds(chip, 1), :]
    column[...] = jnp.transpose(jnp.broadcast_to(chip_ranks, (GROUP, GROUP)))
    half = column[pl.ds(pl.multiple_of(c * 64, 64), 64), :]
    for k in range(keep_n // GROUP):
        lanes = (iota((64, GROUP), 1) + k * GROUP).astype(F32)
        expand[:, k * GROUP : (k + 1) * GROUP] = onehot(half == lanes)

    for go in raw_loads:
        go.wait()
    for h in range(2):
        new_master, _, _ = adamw(raw[h, 0], raw[h, 1], raw[h, 2], 0.0)
        weights[x, z, y, c, h] = jnp.where(half < 0.0, new_master, 0.0).astype(BF16)
    own_rows = pl.ds(pl.multiple_of(c * 64, 64), 64)
    state_rows[:, own_rows, :] = raw[c]

    pl.semaphore_wait(barrier, chips)

    raw_swap = copy(
        raw.at[1 - c], state_rows.at[:, own_rows], raw_send, raw_recv, sibling
    )
    raw_swap.start()

    pending = [raw_swap]

    parts = (
        ((0,), pl.ds(0, 48)),
        ((1,), pl.ds(0, 48)),
        ((pl.ds(0, 2),), pl.ds(48, 16)),
    )

    def region(s, taken, place):
        cols, span = parts[s]
        index = tuple(pl.ds(0, 4) if axis in taken else place[axis] for axis in "xzy")
        return weights.at[(*index, c, *cols, span)]

    def spread(phase):
        out = []
        for s, order in enumerate(ORDERS):
            axis = order[phase]
            block = region(s, order[:phase], at)
            for k in (1, 2, 3):
                n = (s * 3 + phase) * 3 + k - 1
                go = copy(block, block, w_send.at[n], w_recv.at[n], along(axis, k))
                go.start()
                pending.append(go)
                origin = {**at, axis: (at[axis] - k + 4) % 4}
                out.append((go, region(s, order[:phase], origin), n))
        return out

    forwards = []

    def forward(block, n):
        go = copy(block, block, f_send.at[n], f_recv.at[n], sibling)
        go.start()
        pending.append(go)
        forwards.append(go)

    def arrive(sends):
        for go, _, _ in sends:
            go.wait_recv()

    wave = spread(0)
    forward(weights.at[x, z, y, c], 27)

    acc[...] = jnp.zeros_like(acc)
    diagonal = iota((GROUP, GROUP), 0) == iota((GROUP, GROUP), 1)
    inner = iota((SPAN // 16, 16, GROUP), 0) * 16 + iota((SPAN // 16, 16, GROUP), 1)
    inner = inner.astype(F32).astype(BF16)
    one = jnp.ones((SPAN // 16, 16, GROUP), BF16)
    zero = jnp.zeros((SPAN // 16, 16, GROUP), BF16)

    def pack(i, _):
        for go in loads(i):
            go.wait()
        each_row = []
        for j in range(CHUNK // GROUP):
            g = i * (CHUNK // GROUP) + j
            span = pl.ds(pl.multiple_of(g * GROUP, GROUP), GROUP)
            value = grad[span, :].astype(F32) + err[0, span, :]
            stays = 1.0 - sent[pl.ds(g, 1), :]
            mask = jnp.dot(
                jnp.where(diagonal, stays, 0.0).astype(BF16),
                jnp.ones((GROUP, value.shape[1]), BF16),
                preferred_element_type=F32,
            )
            err[0, span, :] = value * mask
            value_b[j * GROUP : (j + 1) * GROUP, :] = value.astype(BF16)
            each_row.append(kept[pl.ds(g, 1), :])
        for q in range(keep_n // SPAN):
            hits = []
            for row in each_row:
                near = jnp.clip(row - q * SPAN, -1.0, SPAN)
                near = jnp.broadcast_to(near, (16, GROUP)).astype(BF16)
                hit = jnp.where(inner == near[None], one, zero)
                hits.append(hit.reshape(SPAN, GROUP))
            acc[q * SPAN : (q + 1) * SPAN, :] += jnp.dot(
                jnp.concatenate(hits, axis=1), value_b[...], preferred_element_type=F32
            )
        return 0

    lax.fori_loop(0, chunks // 4, pack, 0)

    raw_swap.wait_recv()
    split = []
    for a in range(3):
        whole = state_rows[a]
        high = whole.astype(BF16)
        rest = whole - high.astype(F32)
        middle = rest.astype(BF16)
        low = (rest - middle.astype(F32)).astype(BF16)
        split += [high, middle, low]
    split = jnp.concatenate(split, axis=1)

    def place(i, _):
        hits = onehot(chip_ranks == (iota((128, GROUP), 0) + i * 128).astype(F32))
        moved = jnp.dot(hits, split, preferred_element_type=F32)
        for a, order in enumerate(ORDERS):
            high, middle, low = (
                moved[:, (3 * a + p) * 128 : (3 * a + p + 1) * 128] for p in range(3)
            )
            exact = ((high + middle) + low).reshape(8, UNIT, 128)
            for u in range(8):
                spot = {"x": i // 2, "z": (i % 2) * 2 + u // 4, "y": u % 4}
                state[a, spot[order[0]], spot[order[1]], spot[order[2]]] = exact[u]
        return 0

    lax.fori_loop(0, keep_n // 128, place, 0)

    def state_phase(phase, source, target):
        out = []
        for a, order in enumerate(ORDERS):
            axis = order[phase]
            for k in (1, 2, 3):
                go = copy(
                    source.at[a, (at[axis] + k) % 4], target.at[a, k - 1],
                    s_send.at[phase, a, k - 1], s_recv.at[phase, a, k - 1],
                    along(axis, k),
                )
                go.start()
                pending.append(go)
                out.append(go)
        return out

    def state_sum(phase, sends, source, target, result_ref):
        for go in sends:
            go.wait_recv()
        for a, order in enumerate(ORDERS):
            value = source[a, at[order[phase]]]
            for k in range(3):
                value = value + target[a, k]
            result_ref[a] = value

    sends1 = state_phase(0, state, sgot1)

    arrive(wave)
    next_wave = spread(1)
    for _, block, n in wave:
        forward(block, n)
    wave = next_wave

    lax.fori_loop(chunks // 4, chunks, pack, 0)

    for h in range(2):
        packed[h] = (
            acc[:, h * 128 : (h + 1) * 128].astype(BF16).reshape(packed.shape[1:])
        )
    swap = copy(packed.at[1 - c], from_core, core_send, core_recv, sibling)
    swap.start()
    pending.append(swap)

    state_sum(0, sends1, state, sgot1, state1)
    sends2 = state_phase(1, state1, sgot2)

    swap.wait_recv()
    part[...] = (packed[c].astype(F32) + from_core[...].astype(F32)).astype(BF16)

    def scatter(k):
        other, peer = far(k)
        return copy(part.at[other], got.at[k - 1], rs_send.at[k], rs_recv.at[k], peer)

    each(lambda k: scatter(k).start())
    own = packed[c, chip].astype(F32) + from_core[chip].astype(F32)

    arrive(wave)
    next_wave = spread(2)
    for _, block, n in wave:
        forward(block, n)
    wave = next_wave

    state_sum(1, sends2, state1, sgot2, state2)
    sends3 = state_phase(2, state2, sgot3)
    state_sum(2, sends3, state2, sgot3, state3)

    each(lambda k: scatter(k).wait_recv())
    summed = (own + jnp.sum(got[...].astype(F32), axis=0)).astype(BF16)
    new_master, _, _ = adamw(state3[0], state3[1], state3[2], summed.astype(F32))
    result[c, chip, 0] = summed
    result[c, chip, 1] = new_master.astype(BF16)

    def gather(k):
        unit = result.at[c, chip]
        return copy(unit, unit, ag_send.at[k], ag_recv.at[k], far(k)[1])

    def pass_on(k):
        unit = result.at[c, (chip - k + chips) % chips]
        return copy(unit, unit, half_send.at[k], half_recv.at[k], sibling)

    each(lambda k: gather(k).start())
    pass_on(0).start()

    for go, block, n in wave:
        go.wait_recv()
        forward(block, n)

    def relay(k):
        gather(k).wait_recv()
        pass_on(k).start()

    each(relay)
    each(lambda k: scatter(k).wait_send())
    each(lambda k: gather(k).wait_send())
    for go in pending:
        go.wait_send()
    for go in forwards:
        go.wait_recv()
    each(lambda k: pass_on(k).wait_send(), 0)
    each(lambda k: pass_on(k).wait_recv(), 0)


def finish_kernel(
    err, weights, result, expand, rooted, starts_v, master, first, second,
    err_hbm, out_hbm, new_master, new_first, new_second,
    out, starts, err_sem, out_sem, starts_sem,
):
    groups = rooted.shape[0]
    to_smem = pltpu.make_async_copy(starts_v, starts, starts_sem)
    to_smem.start()
    rows = err.shape[1]
    pieces = err_sem.shape[0]
    copies = []
    for i in range(pieces):
        span = pl.ds(i * (rows // pieces), rows // pieces)
        go = pltpu.make_async_copy(err.at[0, span], err_hbm.at[0, span], err_sem.at[i])
        go.start()
        copies.append(go)

    total = jnp.concatenate(
        [
            jnp.dot(
                expand[...], result[h, :, 0].reshape(-1, 128),
                preferred_element_type=F32,
            )
            for h in range(2)
        ],
        axis=1,
    )
    new_master[...], new_first[...], new_second[...] = adamw(
        master[...], first[...], second[...], total
    )

    to_smem.wait()
    units = result.shape[1]
    window = GROUP // UNIT + 1
    batch = groups // out_sem.shape[0]

    def store(i):
        span = pl.ds(i * batch, batch)
        return pltpu.make_async_copy(out.at[span], out_hbm.at[span], out_sem.at[i])

    def fill(i, _):
        for j in range(batch):
            g = i * batch + j
            unit = jnp.minimum(starts[g, 0] // UNIT, units - window)
            near = rooted[pl.ds(g, 1), :] - (unit * UNIT).astype(F32)
            hits = onehot(iota((window * UNIT, GROUP), 0).astype(F32) == near)
            for h in range(2):
                held = result[h, pl.ds(unit, window), 1].reshape(window * UNIT, 128)
                moved = lax.dot_general(
                    hits, held, (((0,), (0,)), ((), ())), preferred_element_type=F32
                )
                for c in range(2):
                    mine = weights[g, c, h].astype(F32) + moved[c * 64 : c * 64 + 64]
                    out[g, c * 64 : c * 64 + 64, h * 128 : h * 128 + 128] = mine.astype(
                        BF16
                    )
        store(i).start()
        return 0

    steps = out_sem.shape[0]
    lax.fori_loop(0, steps, fill, 0)
    for go in copies:
        go.wait()
    lax.fori_loop(0, steps, lambda i, _: (store(i).wait(), 0)[1], 0)


def body(gradients, error_memory, block_lists, master, first_moment, second_moment):
    _, rows, width = gradients.shape
    owned = master.shape[0]
    levels, keep_n = block_lists.shape[1:]
    groups = rows // GROUP
    chunks = rows // CHUNK
    vmem = pl.BlockSpec(memory_space=pltpu.VMEM)
    anywhere = pl.BlockSpec(memory_space=pl.ANY)
    dma = pltpu.SemaphoreType.DMA

    err, weights, result, expand, rooted, starts = pl.pallas_call(
        merge_kernel,
        out_shape=(
            pltpu.VMEM((1, rows, width), F32),
            pltpu.VMEM((4, 4, 4, 2, 2, owned, 128), BF16),
            pltpu.VMEM((2, groups, 2, UNIT, 128), BF16),
            pltpu.VMEM((owned, keep_n), BF16),
            pltpu.VMEM((groups, GROUP), F32),
            pltpu.VMEM((groups, GROUP), jnp.int32),
        ),
        in_specs=[anywhere] * 6,
        out_specs=(vmem,) * 6,
        scratch_shapes=[
            pltpu.VMEM((rows, width), BF16),
            pltpu.VMEM((levels, keep_n), jnp.int32),
            pltpu.VMEM((2, 3, owned, 128), F32),
            pltpu.VMEM((3, GROUP, 128), F32),
            pltpu.VMEM((keep_n, width), F32),
            pltpu.VMEM((groups, GROUP), F32),
            pltpu.VMEM((groups, GROUP), F32),
            pltpu.VMEM((GROUP, GROUP), F32),
            pltpu.VMEM((CHUNK, width), BF16),
            pltpu.VMEM((2, groups, UNIT, 128), BF16),
            pltpu.VMEM((groups, UNIT, 128), BF16),
            pltpu.VMEM((groups, UNIT, 128), BF16),
            pltpu.VMEM((groups - 1, UNIT, 128), BF16),
            pltpu.VMEM((3, 4, 4, 4, UNIT, 128), F32),
            pltpu.VMEM((3, 4, 4, UNIT, 128), F32),
            pltpu.VMEM((3, 4, UNIT, 128), F32),
            pltpu.VMEM((3, UNIT, 128), F32),
            pltpu.VMEM((3, 3, 4, 4, UNIT, 128), F32),
            pltpu.VMEM((3, 3, 4, UNIT, 128), F32),
            pltpu.VMEM((3, 3, UNIT, 128), F32),
            dma((chunks,)), dma((chunks,)), dma, dma((2, 3)),
            dma, dma, dma, dma,
            dma((groups,)), dma((groups,)),
            dma((groups,)), dma((groups,)),
            dma((groups,)), dma((groups,)),
            dma((3, 3, 3)), dma((3, 3, 3)),
            dma((27,)), dma((27,)),
            dma((28,)), dma((28,)),
        ],
        compiler_params=pltpu.CompilerParams(
            collective_id=0, has_side_effects=True, vmem_limit_bytes=46 * MIB
        ),
        name="merge",
    )(gradients, error_memory, block_lists, master, first_moment, second_moment)

    new_errors, out, new_master, new_first, new_second = pl.pallas_call(
        finish_kernel,
        out_shape=(
            jax.ShapeDtypeStruct((1, rows, width), F32),
            jax.ShapeDtypeStruct((groups, GROUP, width), BF16),
            jax.ShapeDtypeStruct((owned, width), F32),
            jax.ShapeDtypeStruct((owned, width), F32),
            jax.ShapeDtypeStruct((owned, width), F32),
        ),
        in_specs=[vmem] * 9,
        out_specs=(anywhere, anywhere, vmem, vmem, vmem),
        scratch_shapes=[
            pltpu.VMEM((groups, GROUP, width), BF16),
            pltpu.SMEM((groups, GROUP), jnp.int32),
            dma((4,)), dma((8,)), dma,
        ],
        compiler_params=pltpu.CompilerParams(vmem_limit_bytes=32 * MIB),
        name="finish",
    )(
        err, weights.reshape(groups, 2, 2, owned, 128), result, expand, rooted, starts,
        master, first_moment, second_moment,
    )
    return new_errors, new_master, new_first, new_second, out.reshape(rows, width)


def solution(mesh):
    in_specs = (
        P("dp", None, None),
        P("dp", None, None),
        P("dp", None, None),
        P("dp", None),
        P("dp", None),
        P("dp", None),
    )
    out_specs = (P("dp", None, None), P("dp", None), P("dp", None), P("dp", None), P())
    return jax.shard_map(
        body, mesh=mesh, in_specs=in_specs, out_specs=out_specs, check_vma=False
    )
```

```python
import jax
import jax.numpy as jnp
from jax import lax
from jax.experimental import pallas as pl
from jax.experimental.pallas import tpu as pltpu
from jax.sharding import PartitionSpec as P

FIRST_BIAS = 0.9999734386011124
SECOND_BIAS = 0.09520785288629036
MESH = pl.DeviceIdType.MESH
F32 = jnp.float32
BF16 = jnp.bfloat16
MIB = 1 << 20

GROUP = 128
CHUNK = 1024
UNIT = 16
SPAN = 256

ORDERS = ("xzy", "zyx", "yxz")


def iota(shape, dim):
    return lax.broadcasted_iota(jnp.int32, shape, dim)


def onehot(hits):
    return jnp.where(hits, 1.0, 0.0).astype(BF16)


def adamw(master, first, second, summed):
    new_first = 0.9 * first + 0.1 * summed
    new_second = 0.999 * second + 0.001 * summed * summed
    first_hat = new_first / FIRST_BIAS
    second_hat = new_second / SECOND_BIAS
    new_master = master - 0.001 * (
        first_hat / (jnp.sqrt(second_hat) + 1e-08) + 0.1 * master
    )
    return new_master, new_first, new_second


def merge_kernel(
    grad_hbm, err_hbm, lists_hbm, master_hbm, first_hbm, second_hbm,
    err, weights, result, expand, rooted, starts,
    grad, lists, raw, state_rows, acc, sent, kept, column, value_b,
    packed, from_core, part, got,
    state, state1, state2, state3, sgot1, sgot2, sgot3,
    grad_sem, err_sem, list_sem, raw_sem,
    core_send, core_recv, raw_send, raw_recv,
    rs_send, rs_recv, ag_send, ag_recv, half_send, half_recv,
    s_send, s_recv, w_send, w_recv, f_send, f_recv,
):
    rows = grad.shape[0]
    groups = rows // GROUP
    chunks = rows // CHUNK
    levels, keep_n = lists.shape
    me = lax.axis_index("dp")
    c = me % 2
    y = (me // 2) % 4
    z = (me // 8) % 4
    x = me // 32
    chip = me // 2
    chips = groups
    sibling = me + 1 - 2 * c
    at = {"x": x, "z": z, "y": y}
    strides = {"x": 32, "z": 8, "y": 2}

    def far(k):
        other = (chip + k) % chips
        return other, 2 * other + c

    def along(axis, k):
        return me + ((at[axis] + k) % 4 - at[axis]) * strides[axis]

    def copy(src, dst, send, recv, peer):
        return pltpu.make_async_remote_copy(
            src_ref=src, dst_ref=dst, send_sem=send, recv_sem=recv,
            device_id=(peer,), device_id_type=MESH,
        )

    def each(act):
        def nine(i, _):
            for j in range(9):
                act(i * 9 + j + 1)
            return 0

        lax.fori_loop(0, (chips - 1) // 9, nine, 0)

    def bytes_of(ref, send, recv):
        return copy(ref, ref, send, recv, sibling)

    list_load = pltpu.make_async_copy(lists_hbm.at[0], lists, list_sem)
    list_load.start()
    for a, source in enumerate((master_hbm, first_hbm, second_hbm)):
        for h in range(2):
            go = pltpu.make_async_copy(
                source.at[:, pl.ds(h * 128, 128)], raw.at[h, a], raw_sem
            )
            go.start()

    def loads(i):
        span = pl.ds(pl.multiple_of(i * CHUNK, CHUNK), CHUNK)
        return (
            pltpu.make_async_copy(grad_hbm.at[0, span], grad.at[span], grad_sem.at[i]),
            pltpu.make_async_copy(err_hbm.at[0, span], err.at[0, span], err_sem.at[i]),
        )

    def load(i, _):
        for go in loads(i):
            go.start()
        return 0

    lax.fori_loop(0, chunks, load, 0)

    barrier = pltpu.get_barrier_semaphore()
    pl.semaphore_signal(barrier, inc=1, device_id=(sibling,), device_id_type=MESH)
    each(
        lambda k: pl.semaphore_signal(
            barrier, inc=1, device_id=(far(k)[1],), device_id_type=MESH
        )
    )

    list_load.wait()

    def member(r):
        ids = lists[r : r + 1, :]
        high = onehot(iota((groups, keep_n), 0) == ids // GROUP)
        low = onehot(iota((GROUP, keep_n), 0) == ids % GROUP)
        return lax.dot_general(
            high, low, (((1,), (1,)), ((), ())), preferred_element_type=F32
        )

    root = member(levels - 1)
    root_b = root.astype(BF16)
    before = onehot(iota((GROUP, GROUP), 0) < iota((GROUP, GROUP), 1))
    inside = jnp.dot(root_b, before, preferred_element_type=F32)
    total = jnp.dot(root_b, jnp.ones((GROUP, GROUP), BF16), preferred_element_type=F32)
    above = onehot(iota((groups, groups), 1) < iota((groups, groups), 0))
    start = jnp.dot(above, total.astype(BF16), preferred_element_type=F32)
    rank = start + inside
    starts[...] = start.astype(jnp.int32)
    rooted[...] = jnp.where(root > 0.5, rank, -1.0)

    keep = member(0)
    sent[...] = keep
    for r in range(1, levels - 1):
        keep = keep * member(r)
    kept[...] = jnp.where(keep * root > 0.5, rank, -1.0)

    chip_ranks = rooted[pl.ds(chip, 1), :]
    column[...] = jnp.transpose(jnp.broadcast_to(chip_ranks, (GROUP, GROUP)))
    half = column[pl.ds(pl.multiple_of(c * 64, 64), 64), :]
    for k in range(keep_n // GROUP):
        lanes = (iota((64, GROUP), 1) + k * GROUP).astype(F32)
        expand[:, k * GROUP : (k + 1) * GROUP] = onehot(half == lanes)

    pltpu.make_async_copy(raw, raw, raw_sem).wait()
    for h in range(2):
        new_master, _, _ = adamw(raw[h, 0], raw[h, 1], raw[h, 2], 0.0)
        weights[x, z, y, c, h] = jnp.where(half < 0.0, new_master, 0.0).astype(BF16)
    own_rows = pl.ds(pl.multiple_of(c * 64, 64), 64)
    state_rows[:, own_rows, :] = raw[c]

    pl.semaphore_wait(barrier, chips)

    raw_swap = copy(
        raw.at[1 - c], state_rows.at[:, own_rows], raw_send, raw_recv, sibling
    )
    raw_swap.start()

    parts = (
        ((0,), pl.ds(0, 48)),
        ((1,), pl.ds(0, 48)),
        ((pl.ds(0, 2),), pl.ds(48, 16)),
    )

    def region(s, taken, place):
        cols, span = parts[s]
        index = tuple(pl.ds(0, 4) if axis in taken else place[axis] for axis in "xzy")
        return weights.at[(*index, c, *cols, span)]

    def triple(s, phase, sends, recvs):
        order = ORDERS[s]
        block = region(s, order[:phase], {**at, order[phase]: pl.ds(0, 3)})
        n = s * 3 + phase
        return bytes_of(block, sends.at[n], recvs.at[n])

    def spread(phase):
        for s, order in enumerate(ORDERS):
            axis = order[phase]
            block = region(s, order[:phase], at)
            n = s * 3 + phase
            for k in (1, 2, 3):
                copy(
                    block, block, w_send.at[n], w_recv.at[n], along(axis, k)
                ).start()

    def arrive(phase, s):
        triple(s, phase, w_send, w_recv).wait_recv()

    def forward(phase, s):
        order = ORDERS[s]
        axis = order[phase]
        n = s * 3 + phase
        for k in (1, 2, 3):
            block = region(s, order[:phase], {**at, axis: (at[axis] + k) % 4})
            copy(block, block, f_send.at[n], f_recv.at[n], sibling).start()

    spread(0)
    mine = weights.at[x, z, y, c]
    own_forward = copy(mine, mine, f_send.at[9], f_recv.at[9], sibling)
    own_forward.start()

    acc[...] = jnp.zeros_like(acc)
    diagonal = iota((GROUP, GROUP), 0) == iota((GROUP, GROUP), 1)
    inner = iota((SPAN // 16, 16, GROUP), 0) * 16 + iota((SPAN // 16, 16, GROUP), 1)
    inner = inner.astype(F32).astype(BF16)
    one = jnp.ones((SPAN // 16, 16, GROUP), BF16)
    zero = jnp.zeros((SPAN // 16, 16, GROUP), BF16)

    def pack(i, _):
        for go in loads(i):
            go.wait()
        each_row = []
        for j in range(CHUNK // GROUP):
            g = i * (CHUNK // GROUP) + j
            span = pl.ds(pl.multiple_of(g * GROUP, GROUP), GROUP)
            value = grad[span, :].astype(F32) + err[0, span, :]
            stays = 1.0 - sent[pl.ds(g, 1), :]
            mask = jnp.dot(
                jnp.where(diagonal, stays, 0.0).astype(BF16),
                jnp.ones((GROUP, value.shape[1]), BF16),
                preferred_element_type=F32,
            )
            err[0, span, :] = value * mask
            value_b[j * GROUP : (j + 1) * GROUP, :] = value.astype(BF16)
            each_row.append(kept[pl.ds(g, 1), :])
        for q in range(keep_n // SPAN):
            hits = []
            for row in each_row:
                near = jnp.clip(row - q * SPAN, -1.0, SPAN)
                near = jnp.broadcast_to(near, (16, GROUP)).astype(BF16)
                hit = jnp.where(inner == near[None], one, zero)
                hits.append(hit.reshape(SPAN, GROUP))
            acc[q * SPAN : (q + 1) * SPAN, :] += jnp.dot(
                jnp.concatenate(hits, axis=1), value_b[...], preferred_element_type=F32
            )
        return 0

    lax.fori_loop(0, chunks // 4, pack, 0)

    raw_swap.wait_recv()
    split = []
    for a in range(3):
        whole = state_rows[a]
        high = whole.astype(BF16)
        rest = whole - high.astype(F32)
        middle = rest.astype(BF16)
        low = (rest - middle.astype(F32)).astype(BF16)
        split += [high, middle, low]
    split = jnp.concatenate(split, axis=1)

    def place(i, _):
        hits = onehot(chip_ranks == (iota((128, GROUP), 0) + i * 128).astype(F32))
        moved = jnp.dot(hits, split, preferred_element_type=F32)
        for a, order in enumerate(ORDERS):
            high, middle, low = (
                moved[:, (3 * a + p) * 128 : (3 * a + p + 1) * 128] for p in range(3)
            )
            exact = ((high + middle) + low).reshape(8, UNIT, 128)
            for u in range(8):
                spot = {"x": i // 2, "z": (i % 2) * 2 + u // 4, "y": u % 4}
                state[a, spot[order[0]], spot[order[1]], spot[order[2]]] = exact[u]
        return 0

    lax.fori_loop(0, keep_n // 128, place, 0)

    def state_phase(phase, source, target):
        for a, order in enumerate(ORDERS):
            axis = order[phase]
            for k in (1, 2, 3):
                go = copy(
                    source.at[a, (at[axis] + k) % 4], target.at[a, k - 1],
                    s_send.at[phase * 3 + a], s_recv.at[phase * 3 + a],
                    along(axis, k),
                )
                go.start()

    def state_bytes(phase, target, a):
        n = phase * 3 + a
        return bytes_of(target.at[a], s_send.at[n], s_recv.at[n])

    def state_sum(phase, source, target, result_ref):
        for a in range(3):
            state_bytes(phase, target, a).wait_recv()
        for a, order in enumerate(ORDERS):
            value = source[a, at[order[phase]]]
            for k in range(3):
                value = value + target[a, k]
            result_ref[a] = value

    state_phase(0, state, sgot1)

    for s in range(3):
        arrive(0, s)
    spread(1)
    for s in range(3):
        forward(0, s)

    lax.fori_loop(chunks // 4, chunks, pack, 0)

    for h in range(2):
        packed[h] = (
            acc[:, h * 128 : (h + 1) * 128].astype(BF16).reshape(packed.shape[1:])
        )
    swap = copy(packed.at[1 - c], from_core, core_send, core_recv, sibling)
    swap.start()

    state_sum(0, state, sgot1, state1)
    state_phase(1, state1, sgot2)

    swap.wait_recv()
    part[...] = (packed[c].astype(F32) + from_core[...].astype(F32)).astype(BF16)

    def scatter(k):
        other, peer = far(k)
        return copy(part.at[other], got.at[k - 1], rs_send, rs_recv, peer)

    each(lambda k: scatter(k).start())
    own = packed[c, chip].astype(F32) + from_core[chip].astype(F32)

    for s in range(3):
        arrive(1, s)
    spread(2)
    for s in range(3):
        forward(1, s)

    state_sum(1, state1, sgot2, state2)
    state_phase(2, state2, sgot3)
    state_sum(2, state2, sgot3, state3)

    scattered = bytes_of(got, rs_send, rs_recv)
    scattered.wait_recv()
    summed = (own + jnp.sum(got[...].astype(F32), axis=0)).astype(BF16)
    new_master, _, _ = adamw(state3[0], state3[1], state3[2], summed.astype(F32))
    result[c, chip, 0] = summed
    result[c, chip, 1] = new_master.astype(BF16)

    plane = chips // 4

    def gather(k):
        unit = result.at[c, chip]
        return copy(unit, unit, ag_send, ag_recv.at[x], far(k)[1])

    def pass_on(q):
        block = result.at[c, pl.ds(q * plane, plane)]
        return copy(block, block, half_send, half_recv, sibling)

    each(lambda k: gather(k).start())

    for s in range(3):
        arrive(2, s)
        forward(2, s)

    for k in (3, 2, 1):
        q = (x + k) % 4
        block = result.at[c, pl.ds(q * plane, plane)]
        bytes_of(block, ag_send, ag_recv.at[q]).wait_recv()
        pass_on(q).start()
    bytes_of(result.at[c, pl.ds(0, plane - 1)], ag_send, ag_recv.at[x]).wait_recv()
    pass_on(x).start()

    scattered.wait_send()
    bytes_of(result.at[c, pl.ds(0, chips - 1)], ag_send, ag_recv.at[x]).wait_send()
    raw_swap.wait_send()
    swap.wait_send()
    own_forward.wait()
    for a in range(3):
        state_bytes(0, sgot1, a).wait_send()
        state_bytes(1, sgot2, a).wait_send()
        state_bytes(2, sgot3, a).wait_send()
    for phase in range(3):
        for s in range(3):
            triple(s, phase, w_send, w_recv).wait_send()
            triple(s, phase, f_send, f_recv).wait()
    bytes_of(result.at[c], half_send, half_recv).wait()


def finish_kernel(
    err, weights, result, expand, rooted, starts_v, master, first, second,
    err_hbm, out_hbm, new_master, new_first, new_second,
    out, starts, err_sem, out_sem, starts_sem,
):
    groups = rooted.shape[0]
    to_smem = pltpu.make_async_copy(starts_v, starts, starts_sem)
    to_smem.start()
    rows = err.shape[1]
    pieces = err_sem.shape[0]
    copies = []
    for i in range(pieces):
        span = pl.ds(i * (rows // pieces), rows // pieces)
        go = pltpu.make_async_copy(err.at[0, span], err_hbm.at[0, span], err_sem.at[i])
        go.start()
        copies.append(go)

    total = jnp.concatenate(
        [
            jnp.dot(
                expand[...], result[h, :, 0].reshape(-1, 128),
                preferred_element_type=F32,
            )
            for h in range(2)
        ],
        axis=1,
    )
    new_master[...], new_first[...], new_second[...] = adamw(
        master[...], first[...], second[...], total
    )

    to_smem.wait()
    units = result.shape[1]
    window = GROUP // UNIT + 1
    batch = groups // out_sem.shape[0]

    def store(i):
        span = pl.ds(i * batch, batch)
        return pltpu.make_async_copy(out.at[span], out_hbm.at[span], out_sem.at[i])

    def fill(i, _):
        for j in range(batch):
            g = i * batch + j
            unit = jnp.minimum(starts[g, 0] // UNIT, units - window)
            near = rooted[pl.ds(g, 1), :] - (unit * UNIT).astype(F32)
            hits = onehot(iota((window * UNIT, GROUP), 0).astype(F32) == near)
            for h in range(2):
                held = result[h, pl.ds(unit, window), 1].reshape(window * UNIT, 128)
                moved = lax.dot_general(
                    hits, held, (((0,), (0,)), ((), ())), preferred_element_type=F32
                )
                for c in range(2):
                    mine = weights[g, c, h].astype(F32) + moved[c * 64 : c * 64 + 64]
                    out[g, c * 64 : c * 64 + 64, h * 128 : h * 128 + 128] = mine.astype(
                        BF16
                    )
        store(i).start()
        return 0

    steps = out_sem.shape[0]
    lax.fori_loop(0, steps, fill, 0)
    for go in copies:
        go.wait()
    lax.fori_loop(0, steps, lambda i, _: (store(i).wait(), 0)[1], 0)


def body(gradients, error_memory, block_lists, master, first_moment, second_moment):
    _, rows, width = gradients.shape
    owned = master.shape[0]
    levels, keep_n = block_lists.shape[1:]
    groups = rows // GROUP
    chunks = rows // CHUNK
    vmem = pl.BlockSpec(memory_space=pltpu.VMEM)
    anywhere = pl.BlockSpec(memory_space=pl.ANY)
    dma = pltpu.SemaphoreType.DMA

    err, weights, result, expand, rooted, starts = pl.pallas_call(
        merge_kernel,
        out_shape=(
            pltpu.VMEM((1, rows, width), F32),
            pltpu.VMEM((4, 4, 4, 2, 2, owned, 128), BF16),
            pltpu.VMEM((2, groups, 2, UNIT, 128), BF16),
            pltpu.VMEM((owned, keep_n), BF16),
            pltpu.VMEM((groups, GROUP), F32),
            pltpu.VMEM((groups, GROUP), jnp.int32),
        ),
        in_specs=[anywhere] * 6,
        out_specs=(vmem,) * 6,
        scratch_shapes=[
            pltpu.VMEM((rows, width), BF16),
            pltpu.VMEM((levels, keep_n), jnp.int32),
            pltpu.VMEM((2, 3, owned, 128), F32),
            pltpu.VMEM((3, GROUP, 128), F32),
            pltpu.VMEM((keep_n, width), F32),
            pltpu.VMEM((groups, GROUP), F32),
            pltpu.VMEM((groups, GROUP), F32),
            pltpu.VMEM((GROUP, GROUP), F32),
            pltpu.VMEM((CHUNK, width), BF16),
            pltpu.VMEM((2, groups, UNIT, 128), BF16),
            pltpu.VMEM((groups, UNIT, 128), BF16),
            pltpu.VMEM((groups, UNIT, 128), BF16),
            pltpu.VMEM((groups - 1, UNIT, 128), BF16),
            pltpu.VMEM((3, 4, 4, 4, UNIT, 128), F32),
            pltpu.VMEM((3, 4, 4, UNIT, 128), F32),
            pltpu.VMEM((3, 4, UNIT, 128), F32),
            pltpu.VMEM((3, UNIT, 128), F32),
            pltpu.VMEM((3, 3, 4, 4, UNIT, 128), F32),
            pltpu.VMEM((3, 3, 4, UNIT, 128), F32),
            pltpu.VMEM((3, 3, UNIT, 128), F32),
            dma((chunks,)), dma((chunks,)), dma, dma,
            dma, dma, dma, dma,
            dma, dma, dma, dma((4,)), dma, dma,
            dma((9,)), dma((9,)),
            dma((9,)), dma((9,)),
            dma((10,)), dma((10,)),
        ],
        compiler_params=pltpu.CompilerParams(
            collective_id=0, has_side_effects=True, vmem_limit_bytes=46 * MIB
        ),
        name="merge",
    )(gradients, error_memory, block_lists, master, first_moment, second_moment)

    new_errors, out, new_master, new_first, new_second = pl.pallas_call(
        finish_kernel,
        out_shape=(
            jax.ShapeDtypeStruct((1, rows, width), F32),
            jax.ShapeDtypeStruct((groups, GROUP, width), BF16),
            jax.ShapeDtypeStruct((owned, width), F32),
            jax.ShapeDtypeStruct((owned, width), F32),
            jax.ShapeDtypeStruct((owned, width), F32),
        ),
        in_specs=[vmem] * 9,
        out_specs=(anywhere, anywhere, vmem, vmem, vmem),
        scratch_shapes=[
            pltpu.VMEM((groups, GROUP, width), BF16),
            pltpu.SMEM((groups, GROUP), jnp.int32),
            dma((4,)), dma((8,)), dma,
        ],
        compiler_params=pltpu.CompilerParams(vmem_limit_bytes=32 * MIB),
        name="finish",
    )(
        err, weights.reshape(groups, 2, 2, owned, 128), result, expand, rooted, starts,
        master, first_moment, second_moment,
    )
    return new_errors, new_master, new_first, new_second, out.reshape(rows, width)


def solution(mesh):
    in_specs = (
        P("dp", None, None),
        P("dp", None, None),
        P("dp", None, None),
        P("dp", None),
        P("dp", None),
        P("dp", None),
    )
    out_specs = (P("dp", None, None), P("dp", None), P("dp", None), P("dp", None), P())
    return jax.shard_map(
        body, mesh=mesh, in_specs=in_specs, out_specs=out_specs, check_vma=False
    )
```

```python
import jax
import jax.numpy as jnp
from jax import lax
from jax.experimental import pallas as pl
from jax.experimental.pallas import tpu as pltpu
from jax.sharding import PartitionSpec as P

FIRST_BIAS = 0.9999734386011124
SECOND_BIAS = 0.09520785288629036
MESH = pl.DeviceIdType.MESH
F32 = jnp.float32
BF16 = jnp.bfloat16
MIB = 1 << 20

GROUP = 128
CHUNK = 1024
UNIT = 16
SPAN = 256

ORDERS = ("xzy", "zyx", "yxz")


def iota(shape, dim):
    return lax.broadcasted_iota(jnp.int32, shape, dim)


def onehot(hits):
    return jnp.where(hits, 1.0, 0.0).astype(BF16)


def adamw(master, first, second, summed):
    new_first = 0.9 * first + 0.1 * summed
    new_second = 0.999 * second + 0.001 * summed * summed
    first_hat = new_first / FIRST_BIAS
    second_hat = new_second / SECOND_BIAS
    new_master = master - 0.001 * (
        first_hat / (jnp.sqrt(second_hat) + 1e-08) + 0.1 * master
    )
    return new_master, new_first, new_second


def merge_kernel(
    grad_hbm, err_hbm, lists_hbm, master_hbm, first_hbm, second_hbm,
    err, weights, result, expand, rooted, starts,
    grad, lists, raw, state_rows, acc, sent, kept, column, value_b,
    packed, from_core, part, got,
    state, state1, state2, state3, sgot1, sgot2, sgot3,
    grad_sem, err_sem, list_sem, raw_sem,
    core_send, core_recv, raw_send, raw_recv,
    rs_send, rs_recv, ag_send, ag_recv, half_send, half_recv,
    s_send, s_recv, w_send, w_recv, f_send, f_recv, round_z, round_x,
):
    rows = grad.shape[0]
    groups = rows // GROUP
    chunks = rows // CHUNK
    levels, keep_n = lists.shape
    me = lax.axis_index("dp")
    c = me % 2
    y = (me // 2) % 4
    z = (me // 8) % 4
    x = me // 32
    chip = me // 2
    chips = groups
    sibling = me + 1 - 2 * c
    at = {"x": x, "z": z, "y": y}
    strides = {"x": 32, "z": 8, "y": 2}

    def far(k):
        other = (chip + k) % chips
        return other, 2 * other + c

    def along(axis, k):
        return me + ((at[axis] + k) % 4 - at[axis]) * strides[axis]

    def copy(src, dst, send, recv, peer):
        return pltpu.make_async_remote_copy(
            src_ref=src, dst_ref=dst, send_sem=send, recv_sem=recv,
            device_id=(peer,), device_id_type=MESH,
        )

    def each(act):
        def nine(i, _):
            for j in range(9):
                act(i * 9 + j + 1)
            return 0

        lax.fori_loop(0, (chips - 1) // 9, nine, 0)

    def bytes_of(ref, send, recv):
        return copy(ref, ref, send, recv, sibling)

    def greet(semaphore, peers):
        for peer in peers:
            pl.semaphore_signal(
                semaphore, inc=1, device_id=(peer,), device_id_type=MESH
            )

    line = {axis: [along(axis, k) for k in (1, 2, 3)] for axis in "xzy"}
    barrier = pltpu.get_barrier_semaphore()
    greet(barrier, [sibling, *line["y"], *line["z"], *line["x"]])

    list_load = pltpu.make_async_copy(lists_hbm.at[0], lists, list_sem)
    list_load.start()
    for a, source in enumerate((master_hbm, first_hbm, second_hbm)):
        for h in range(2):
            go = pltpu.make_async_copy(
                source.at[:, pl.ds(h * 128, 128)], raw.at[h, a], raw_sem
            )
            go.start()

    def loads(i):
        span = pl.ds(pl.multiple_of(i * CHUNK, CHUNK), CHUNK)
        return (
            pltpu.make_async_copy(grad_hbm.at[0, span], grad.at[span], grad_sem.at[i]),
            pltpu.make_async_copy(err_hbm.at[0, span], err.at[0, span], err_sem.at[i]),
        )

    def load(i, _):
        for go in loads(i):
            go.start()
        return 0

    lax.fori_loop(0, chunks, load, 0)

    list_load.wait()

    def member(r):
        ids = lists[r : r + 1, :]
        high = onehot(iota((groups, keep_n), 0) == ids // GROUP)
        low = onehot(iota((GROUP, keep_n), 0) == ids % GROUP)
        return lax.dot_general(
            high, low, (((1,), (1,)), ((), ())), preferred_element_type=F32
        )

    root = member(levels - 1)
    root_b = root.astype(BF16)
    before = onehot(iota((GROUP, GROUP), 0) < iota((GROUP, GROUP), 1))
    inside = jnp.dot(root_b, before, preferred_element_type=F32)
    total = jnp.dot(root_b, jnp.ones((GROUP, GROUP), BF16), preferred_element_type=F32)
    above = onehot(iota((groups, groups), 1) < iota((groups, groups), 0))
    start = jnp.dot(above, total.astype(BF16), preferred_element_type=F32)
    rank = start + inside
    starts[...] = start.astype(jnp.int32)
    rooted[...] = jnp.where(root > 0.5, rank, -1.0)

    keep = member(0)
    sent[...] = keep
    for r in range(1, levels - 1):
        keep = keep * member(r)
    kept[...] = jnp.where(keep * root > 0.5, rank, -1.0)

    chip_ranks = rooted[pl.ds(chip, 1), :]
    column[...] = jnp.transpose(jnp.broadcast_to(chip_ranks, (GROUP, GROUP)))
    half = column[pl.ds(pl.multiple_of(c * 64, 64), 64), :]
    for k in range(keep_n // GROUP):
        lanes = (iota((64, GROUP), 1) + k * GROUP).astype(F32)
        expand[:, k * GROUP : (k + 1) * GROUP] = onehot(half == lanes)

    pltpu.make_async_copy(raw, raw, raw_sem).wait()
    for h in range(2):
        new_master, _, _ = adamw(raw[h, 0], raw[h, 1], raw[h, 2], 0.0)
        weights[x, z, y, c, h] = jnp.where(half < 0.0, new_master, 0.0).astype(BF16)
    own_rows = pl.ds(pl.multiple_of(c * 64, 64), 64)
    state_rows[:, own_rows, :] = raw[c]

    pl.semaphore_wait(barrier, 10)
    greet(round_z, line["z"])

    raw_swap = copy(
        raw.at[1 - c], state_rows.at[:, own_rows], raw_send, raw_recv, sibling
    )
    raw_swap.start()

    parts = (
        ((0,), pl.ds(0, 48)),
        ((1,), pl.ds(0, 48)),
        ((pl.ds(0, 2),), pl.ds(48, 16)),
    )

    def region(s, taken, place):
        cols, span = parts[s]
        index = tuple(pl.ds(0, 4) if axis in taken else place[axis] for axis in "xzy")
        return weights.at[(*index, c, *cols, span)]

    def triple(s, phase, sends, recvs):
        order = ORDERS[s]
        block = region(s, order[:phase], {**at, order[phase]: pl.ds(0, 3)})
        n = s * 3 + phase
        return bytes_of(block, sends.at[n], recvs.at[n])

    def spread(phase):
        for s, order in enumerate(ORDERS):
            axis = order[phase]
            block = region(s, order[:phase], at)
            n = s * 3 + phase
            for k in (1, 2, 3):
                copy(
                    block, block, w_send.at[n], w_recv.at[n], along(axis, k)
                ).start()

    def arrive(phase, s):
        triple(s, phase, w_send, w_recv).wait_recv()

    def forward(phase, s):
        order = ORDERS[s]
        axis = order[phase]
        n = s * 3 + phase
        for k in (1, 2, 3):
            block = region(s, order[:phase], {**at, axis: (at[axis] + k) % 4})
            copy(block, block, f_send.at[n], f_recv.at[n], sibling).start()

    spread(0)
    mine = weights.at[x, z, y, c]
    own_forward = copy(mine, mine, f_send.at[9], f_recv.at[9], sibling)
    own_forward.start()

    acc[...] = jnp.zeros_like(acc)
    diagonal = iota((GROUP, GROUP), 0) == iota((GROUP, GROUP), 1)
    inner = iota((SPAN // 16, 16, GROUP), 0) * 16 + iota((SPAN // 16, 16, GROUP), 1)
    inner = inner.astype(F32).astype(BF16)
    one = jnp.ones((SPAN // 16, 16, GROUP), BF16)
    zero = jnp.zeros((SPAN // 16, 16, GROUP), BF16)

    def pack(i, _):
        for go in loads(i):
            go.wait()
        each_row = []
        for j in range(CHUNK // GROUP):
            g = i * (CHUNK // GROUP) + j
            span = pl.ds(pl.multiple_of(g * GROUP, GROUP), GROUP)
            value = grad[span, :].astype(F32) + err[0, span, :]
            value_b[j * GROUP : (j + 1) * GROUP, :] = value.astype(BF16)
            each_row.append(kept[pl.ds(g, 1), :])
        for q in range(keep_n // SPAN):
            hits = []
            for row in each_row:
                near = jnp.clip(row - q * SPAN, -1.0, SPAN)
                near = jnp.broadcast_to(near, (16, GROUP)).astype(BF16)
                hit = jnp.where(inner == near[None], one, zero)
                hits.append(hit.reshape(SPAN, GROUP))
            acc[q * SPAN : (q + 1) * SPAN, :] += jnp.dot(
                jnp.concatenate(hits, axis=1), value_b[...], preferred_element_type=F32
            )
        return 0

    def settle(i, _):
        for j in range(CHUNK // GROUP):
            g = i * (CHUNK // GROUP) + j
            span = pl.ds(pl.multiple_of(g * GROUP, GROUP), GROUP)
            stays = 1.0 - sent[pl.ds(g, 1), :]
            mask = jnp.dot(
                jnp.where(diagonal, stays, 0.0).astype(BF16),
                jnp.ones((GROUP, err.shape[2]), BF16),
                preferred_element_type=F32,
            )
            err[0, span, :] = (grad[span, :].astype(F32) + err[0, span, :]) * mask
        return 0

    lax.fori_loop(0, chunks // 4, pack, 0)

    pl.semaphore_wait(round_z, 3)
    greet(round_x, line["x"])

    raw_swap.wait_recv()
    split = []
    for a in range(3):
        whole = state_rows[a]
        high = whole.astype(BF16)
        rest = whole - high.astype(F32)
        middle = rest.astype(BF16)
        low = (rest - middle.astype(F32)).astype(BF16)
        split += [high, middle, low]
    split = jnp.concatenate(split, axis=1)

    def place(i, _):
        hits = onehot(chip_ranks == (iota((128, GROUP), 0) + i * 128).astype(F32))
        moved = jnp.dot(hits, split, preferred_element_type=F32)
        for a, order in enumerate(ORDERS):
            high, middle, low = (
                moved[:, (3 * a + p) * 128 : (3 * a + p + 1) * 128] for p in range(3)
            )
            exact = ((high + middle) + low).reshape(8, UNIT, 128)
            for u in range(8):
                spot = {"x": i // 2, "z": (i % 2) * 2 + u // 4, "y": u % 4}
                state[a, spot[order[0]], spot[order[1]], spot[order[2]]] = exact[u]
        return 0

    lax.fori_loop(0, keep_n // 128, place, 0)

    def state_phase(phase, source, target):
        for a, order in enumerate(ORDERS):
            axis = order[phase]
            for k in (1, 2, 3):
                go = copy(
                    source.at[a, (at[axis] + k) % 4], target.at[a, k - 1],
                    s_send.at[phase * 3 + a], s_recv.at[phase * 3 + a],
                    along(axis, k),
                )
                go.start()

    def state_bytes(phase, target, a):
        n = phase * 3 + a
        return bytes_of(target.at[a], s_send.at[n], s_recv.at[n])

    def state_sum(phase, source, target, result_ref):
        for a in range(3):
            state_bytes(phase, target, a).wait_recv()
        for a, order in enumerate(ORDERS):
            value = source[a, at[order[phase]]]
            for k in range(3):
                value = value + target[a, k]
            result_ref[a] = value

    state_phase(0, state, sgot1)

    lax.fori_loop(chunks // 4, chunks // 2, pack, 0)

    for s in range(3):
        arrive(0, s)
    spread(1)
    for s in range(3):
        forward(0, s)

    lax.fori_loop(chunks // 2, chunks, pack, 0)

    for h in range(2):
        packed[h] = (
            acc[:, h * 128 : (h + 1) * 128].astype(BF16).reshape(packed.shape[1:])
        )
    swap = copy(packed.at[1 - c], from_core, core_send, core_recv, sibling)
    swap.start()

    state_sum(0, state, sgot1, state1)
    state_phase(1, state1, sgot2)

    pl.semaphore_wait(round_x, 3)

    swap.wait_recv()
    part[...] = (packed[c].astype(F32) + from_core[...].astype(F32)).astype(BF16)

    def scatter(k):
        other, peer = far(k)
        return copy(part.at[other], got.at[k - 1], rs_send, rs_recv, peer)

    each(lambda k: scatter(k).start())
    own = packed[c, chip].astype(F32) + from_core[chip].astype(F32)

    for s in range(3):
        arrive(1, s)
    spread(2)
    for s in range(3):
        forward(1, s)

    state_sum(1, state1, sgot2, state2)
    state_phase(2, state2, sgot3)
    state_sum(2, state2, sgot3, state3)

    lax.fori_loop(0, chunks // 2, settle, 0)
    scattered = bytes_of(got, rs_send, rs_recv)
    scattered.wait_recv()
    summed = (own + jnp.sum(got[...].astype(F32), axis=0)).astype(BF16)
    new_master, _, _ = adamw(state3[0], state3[1], state3[2], summed.astype(F32))
    result[c, chip, 0] = summed
    result[c, chip, 1] = new_master.astype(BF16)

    plane = chips // 4

    def gather(k):
        unit = result.at[c, chip]
        return copy(unit, unit, ag_send, ag_recv.at[x], far(k)[1])

    def pass_on(q):
        block = result.at[c, pl.ds(q * plane, plane)]
        return copy(block, block, half_send, half_recv, sibling)

    each(lambda k: gather(k).start())
    lax.fori_loop(chunks // 2, chunks, settle, 0)

    for s in range(3):
        arrive(2, s)
        forward(2, s)

    for k in (3, 2, 1):
        q = (x + k) % 4
        block = result.at[c, pl.ds(q * plane, plane)]
        bytes_of(block, ag_send, ag_recv.at[q]).wait_recv()
        pass_on(q).start()
    bytes_of(result.at[c, pl.ds(0, plane - 1)], ag_send, ag_recv.at[x]).wait_recv()
    pass_on(x).start()

    scattered.wait_send()
    bytes_of(result.at[c, pl.ds(0, chips - 1)], ag_send, ag_recv.at[x]).wait_send()
    raw_swap.wait_send()
    swap.wait_send()
    own_forward.wait()
    for a in range(3):
        state_bytes(0, sgot1, a).wait_send()
        state_bytes(1, sgot2, a).wait_send()
        state_bytes(2, sgot3, a).wait_send()
    for phase in range(3):
        for s in range(3):
            triple(s, phase, w_send, w_recv).wait_send()
            triple(s, phase, f_send, f_recv).wait()
    bytes_of(result.at[c], half_send, half_recv).wait()


def finish_kernel(
    err, weights, result, expand, rooted, starts_v, master, first, second,
    err_hbm, out_hbm, new_master, new_first, new_second,
    out, starts, err_sem, out_sem, starts_sem,
):
    groups = rooted.shape[0]
    to_smem = pltpu.make_async_copy(starts_v, starts, starts_sem)
    to_smem.start()
    rows = err.shape[1]
    pieces = err_sem.shape[0]
    copies = []
    for i in range(pieces):
        span = pl.ds(i * (rows // pieces), rows // pieces)
        go = pltpu.make_async_copy(err.at[0, span], err_hbm.at[0, span], err_sem.at[i])
        go.start()
        copies.append(go)

    total = jnp.concatenate(
        [
            jnp.dot(
                expand[...], result[h, :, 0].reshape(-1, 128),
                preferred_element_type=F32,
            )
            for h in range(2)
        ],
        axis=1,
    )
    new_master[...], new_first[...], new_second[...] = adamw(
        master[...], first[...], second[...], total
    )

    to_smem.wait()
    units = result.shape[1]
    window = GROUP // UNIT + 1
    batch = groups // out_sem.shape[0]

    def store(i):
        span = pl.ds(i * batch, batch)
        return pltpu.make_async_copy(out.at[span], out_hbm.at[span], out_sem.at[i])

    def fill(i, _):
        for j in range(batch):
            g = i * batch + j
            unit = jnp.minimum(starts[g, 0] // UNIT, units - window)
            near = rooted[pl.ds(g, 1), :] - (unit * UNIT).astype(F32)
            hits = onehot(iota((window * UNIT, GROUP), 0).astype(F32) == near)
            for h in range(2):
                held = result[h, pl.ds(unit, window), 1].reshape(window * UNIT, 128)
                moved = lax.dot_general(
                    hits, held, (((0,), (0,)), ((), ())), preferred_element_type=F32
                )
                for c in range(2):
                    mine = weights[g, c, h].astype(F32) + moved[c * 64 : c * 64 + 64]
                    out[g, c * 64 : c * 64 + 64, h * 128 : h * 128 + 128] = mine.astype(
                        BF16
                    )
        store(i).start()
        return 0

    steps = out_sem.shape[0]
    lax.fori_loop(0, steps, fill, 0)
    for go in copies:
        go.wait()
    lax.fori_loop(0, steps, lambda i, _: (store(i).wait(), 0)[1], 0)


def body(gradients, error_memory, block_lists, master, first_moment, second_moment):
    _, rows, width = gradients.shape
    owned = master.shape[0]
    levels, keep_n = block_lists.shape[1:]
    groups = rows // GROUP
    chunks = rows // CHUNK
    vmem = pl.BlockSpec(memory_space=pltpu.VMEM)
    anywhere = pl.BlockSpec(memory_space=pl.ANY)
    dma = pltpu.SemaphoreType.DMA

    err, weights, result, expand, rooted, starts = pl.pallas_call(
        merge_kernel,
        out_shape=(
            pltpu.VMEM((1, rows, width), F32),
            pltpu.VMEM((4, 4, 4, 2, 2, owned, 128), BF16),
            pltpu.VMEM((2, groups, 2, UNIT, 128), BF16),
            pltpu.VMEM((owned, keep_n), BF16),
            pltpu.VMEM((groups, GROUP), F32),
            pltpu.VMEM((groups, GROUP), jnp.int32),
        ),
        in_specs=[anywhere] * 6,
        out_specs=(vmem,) * 6,
        scratch_shapes=[
            pltpu.VMEM((rows, width), BF16),
            pltpu.VMEM((levels, keep_n), jnp.int32),
            pltpu.VMEM((2, 3, owned, 128), F32),
            pltpu.VMEM((3, GROUP, 128), F32),
            pltpu.VMEM((keep_n, width), F32),
            pltpu.VMEM((groups, GROUP), F32),
            pltpu.VMEM((groups, GROUP), F32),
            pltpu.VMEM((GROUP, GROUP), F32),
            pltpu.VMEM((CHUNK, width), BF16),
            pltpu.VMEM((2, groups, UNIT, 128), BF16),
            pltpu.VMEM((groups, UNIT, 128), BF16),
            pltpu.VMEM((groups, UNIT, 128), BF16),
            pltpu.VMEM((groups - 1, UNIT, 128), BF16),
            pltpu.VMEM((3, 4, 4, 4, UNIT, 128), F32),
            pltpu.VMEM((3, 4, 4, UNIT, 128), F32),
            pltpu.VMEM((3, 4, UNIT, 128), F32),
            pltpu.VMEM((3, UNIT, 128), F32),
            pltpu.VMEM((3, 3, 4, 4, UNIT, 128), F32),
            pltpu.VMEM((3, 3, 4, UNIT, 128), F32),
            pltpu.VMEM((3, 3, UNIT, 128), F32),
            dma((chunks,)), dma((chunks,)), dma, dma,
            dma, dma, dma, dma,
            dma, dma, dma, dma((4,)), dma, dma,
            dma((9,)), dma((9,)),
            dma((9,)), dma((9,)),
            dma((10,)), dma((10,)),
            pltpu.SemaphoreType.REGULAR, pltpu.SemaphoreType.REGULAR,
        ],
        compiler_params=pltpu.CompilerParams(
            collective_id=0, has_side_effects=True, vmem_limit_bytes=46 * MIB
        ),
        name="merge",
    )(gradients, error_memory, block_lists, master, first_moment, second_moment)

    new_errors, out, new_master, new_first, new_second = pl.pallas_call(
        finish_kernel,
        out_shape=(
            jax.ShapeDtypeStruct((1, rows, width), F32),
            jax.ShapeDtypeStruct((groups, GROUP, width), BF16),
            jax.ShapeDtypeStruct((owned, width), F32),
            jax.ShapeDtypeStruct((owned, width), F32),
            jax.ShapeDtypeStruct((owned, width), F32),
        ),
        in_specs=[vmem] * 9,
        out_specs=(anywhere, anywhere, vmem, vmem, vmem),
        scratch_shapes=[
            pltpu.VMEM((groups, GROUP, width), BF16),
            pltpu.SMEM((groups, GROUP), jnp.int32),
            dma((4,)), dma((8,)), dma,
        ],
        compiler_params=pltpu.CompilerParams(vmem_limit_bytes=32 * MIB),
        name="finish",
    )(
        err, weights.reshape(groups, 2, 2, owned, 128), result, expand, rooted, starts,
        master, first_moment, second_moment,
    )
    return new_errors, new_master, new_first, new_second, out.reshape(rows, width)


def solution(mesh):
    in_specs = (
        P("dp", None, None),
        P("dp", None, None),
        P("dp", None, None),
        P("dp", None),
        P("dp", None),
        P("dp", None),
    )
    out_specs = (P("dp", None, None), P("dp", None), P("dp", None), P("dp", None), P())
    return jax.shard_map(
        body, mesh=mesh, in_specs=in_specs, out_specs=out_specs, check_vma=False
    )
```

```python
import jax
import jax.numpy as jnp
from jax import lax
from jax.experimental import pallas as pl
from jax.experimental.pallas import tpu as pltpu
from jax.sharding import PartitionSpec as P

FIRST_BIAS = 0.9999734386011124
SECOND_BIAS = 0.09520785288629036
MESH = pl.DeviceIdType.MESH
F32 = jnp.float32
BF16 = jnp.bfloat16
MIB = 1 << 20

GROUP = 128
CHUNK = 1024
UNIT = 16
SPAN = 256

ORDERS = ("xzy", "zyx", "yxz")
STATE_ORDERS = ("zyx", "xzy", "yxz")


def iota(shape, dim):
    return lax.broadcasted_iota(jnp.int32, shape, dim)


def onehot(hits):
    return jnp.where(hits, 1.0, 0.0).astype(BF16)


def adamw(master, first, second, summed):
    new_first = 0.9 * first + 0.1 * summed
    new_second = 0.999 * second + 0.001 * summed * summed
    first_hat = new_first / FIRST_BIAS
    second_hat = new_second / SECOND_BIAS
    new_master = master - 0.001 * (
        first_hat / (jnp.sqrt(second_hat) + 1e-08) + 0.1 * master
    )
    return new_master, new_first, new_second


def merge_kernel(
    grad_hbm, err_hbm, lists_hbm, master_hbm, first_hbm, second_hbm,
    err, weights, result, expand, rooted, starts,
    grad, lists, raw, state_rows, acc, sent, kept, column, value_b,
    packed, from_core, part, got,
    master0, master1, master2, master3, mgot1, mgot2, mgot3,
    moment0, moment1, moment2, moment3, vgot1, vgot2, vgot3,
    grad_sem, err_sem, list_sem, raw_sem,
    core_send, core_recv, raw_send, raw_recv,
    rs_send, rs_recv, ag_send, ag_recv, half_send, half_recv,
    s_send, s_recv, w_send, w_recv, f_send, f_recv, round_z, round_x,
):
    rows = grad.shape[0]
    groups = rows // GROUP
    chunks = rows // CHUNK
    levels, keep_n = lists.shape
    me = lax.axis_index("dp")
    c = me % 2
    y = (me // 2) % 4
    z = (me // 8) % 4
    x = me // 32
    chip = me // 2
    chips = groups
    sibling = me + 1 - 2 * c
    at = {"x": x, "z": z, "y": y}
    strides = {"x": 32, "z": 8, "y": 2}

    def far(k):
        other = (chip + k) % chips
        return other, 2 * other + c

    def along(axis, k):
        return me + ((at[axis] + k) % 4 - at[axis]) * strides[axis]

    def copy(src, dst, send, recv, peer):
        return pltpu.make_async_remote_copy(
            src_ref=src, dst_ref=dst, send_sem=send, recv_sem=recv,
            device_id=(peer,), device_id_type=MESH,
        )

    def each(act):
        def nine(i, _):
            for j in range(9):
                act(i * 9 + j + 1)
            return 0

        lax.fori_loop(0, (chips - 1) // 9, nine, 0)

    def bytes_of(ref, send, recv):
        return copy(ref, ref, send, recv, sibling)

    def three(master_ref, moments_ref):
        return master_ref, moments_ref.at[0], moments_ref.at[1]

    state = three(master0, moment0)
    state1 = three(master1, moment1)
    state2 = three(master2, moment2)
    state3 = three(master3, moment3)
    sgot1 = three(mgot1, vgot1)
    sgot2 = three(mgot2, vgot2)
    sgot3 = three(mgot3, vgot3)

    def greet(semaphore, peers):
        for peer in peers:
            pl.semaphore_signal(
                semaphore, inc=1, device_id=(peer,), device_id_type=MESH
            )

    line = {axis: [along(axis, k) for k in (1, 2, 3)] for axis in "xzy"}
    barrier = pltpu.get_barrier_semaphore()
    greet(barrier, [sibling, *line["y"], *line["z"], *line["x"]])

    list_load = pltpu.make_async_copy(lists_hbm.at[0], lists, list_sem)
    list_load.start()
    for a, source in enumerate((master_hbm, first_hbm, second_hbm)):
        for h in range(2):
            go = pltpu.make_async_copy(
                source.at[:, pl.ds(h * 128, 128)], raw.at[h, a], raw_sem
            )
            go.start()

    def loads(i):
        span = pl.ds(pl.multiple_of(i * CHUNK, CHUNK), CHUNK)
        return (
            pltpu.make_async_copy(grad_hbm.at[0, span], grad.at[span], grad_sem.at[i]),
            pltpu.make_async_copy(err_hbm.at[0, span], err.at[0, span], err_sem.at[i]),
        )

    def load(i, _):
        for go in loads(i):
            go.start()
        return 0

    lax.fori_loop(0, chunks, load, 0)

    pltpu.make_async_copy(raw, raw, raw_sem).wait()
    for h in range(2):
        new_master, _, _ = adamw(raw[h, 0], raw[h, 1], raw[h, 2], 0.0)
        weights[x, z, y, c, h] = new_master.astype(BF16)
    own_rows = pl.ds(pl.multiple_of(c * 64, 64), 64)
    state_rows[:, own_rows, :] = raw[c]

    pl.semaphore_wait(barrier, 10)
    greet(round_z, line["z"])

    raw_swap = copy(
        raw.at[1 - c], state_rows.at[:, own_rows], raw_send, raw_recv, sibling
    )
    raw_swap.start()

    parts = (
        ((0,), pl.ds(0, 48)),
        ((1,), pl.ds(0, 48)),
        ((pl.ds(0, 2),), pl.ds(48, 16)),
    )

    def region(s, taken, place):
        cols, span = parts[s]
        index = tuple(pl.ds(0, 4) if axis in taken else place[axis] for axis in "xzy")
        return weights.at[(*index, c, *cols, span)]

    def triple(s, phase, sends, recvs):
        order = ORDERS[s]
        block = region(s, order[:phase], {**at, order[phase]: pl.ds(0, 3)})
        n = s * 3 + phase
        return bytes_of(block, sends.at[n], recvs.at[n])

    def spread(phase):
        for s, order in enumerate(ORDERS):
            axis = order[phase]
            block = region(s, order[:phase], at)
            n = s * 3 + phase
            for k in (1, 2, 3):
                copy(
                    block, block, w_send.at[n], w_recv.at[n], along(axis, k)
                ).start()

    def arrive(phase, s):
        triple(s, phase, w_send, w_recv).wait_recv()

    def forward(phase, s):
        order = ORDERS[s]
        axis = order[phase]
        n = s * 3 + phase
        for k in (1, 2, 3):
            block = region(s, order[:phase], {**at, axis: (at[axis] + k) % 4})
            copy(block, block, f_send.at[n], f_recv.at[n], sibling).start()

    spread(0)
    mine = weights.at[x, z, y, c]
    own_forward = copy(mine, mine, f_send.at[9], f_recv.at[9], sibling)
    own_forward.start()

    list_load.wait()

    def member(r):
        ids = lists[r : r + 1, :]
        high = onehot(iota((groups, keep_n), 0) == ids // GROUP)
        low = onehot(iota((GROUP, keep_n), 0) == ids % GROUP)
        return lax.dot_general(
            high, low, (((1,), (1,)), ((), ())), preferred_element_type=F32
        )

    root = member(levels - 1)
    root_b = root.astype(BF16)
    before = onehot(iota((GROUP, GROUP), 0) < iota((GROUP, GROUP), 1))
    inside = jnp.dot(root_b, before, preferred_element_type=F32)
    total = jnp.dot(root_b, jnp.ones((GROUP, GROUP), BF16), preferred_element_type=F32)
    above = onehot(iota((groups, groups), 1) < iota((groups, groups), 0))
    start = jnp.dot(above, total.astype(BF16), preferred_element_type=F32)
    rank = start + inside
    starts[...] = start.astype(jnp.int32)
    rooted[...] = jnp.where(root > 0.5, rank, -1.0)

    keep = member(0)
    sent[...] = keep
    for r in range(1, levels - 1):
        keep = keep * member(r)
    kept[...] = jnp.where(keep * root > 0.5, rank, -1.0)

    chip_ranks = rooted[pl.ds(chip, 1), :]

    acc[...] = jnp.zeros_like(acc)
    diagonal = iota((GROUP, GROUP), 0) == iota((GROUP, GROUP), 1)
    inner = iota((SPAN // 16, 16, GROUP), 0) * 16 + iota((SPAN // 16, 16, GROUP), 1)
    inner = inner.astype(F32).astype(BF16)
    one = jnp.ones((SPAN // 16, 16, GROUP), BF16)
    zero = jnp.zeros((SPAN // 16, 16, GROUP), BF16)

    def pack(i, _):
        for go in loads(i):
            go.wait()
        each_row = []
        for j in range(CHUNK // GROUP):
            g = i * (CHUNK // GROUP) + j
            span = pl.ds(pl.multiple_of(g * GROUP, GROUP), GROUP)
            value = grad[span, :].astype(F32) + err[0, span, :]
            value_b[j * GROUP : (j + 1) * GROUP, :] = value.astype(BF16)
            each_row.append(kept[pl.ds(g, 1), :])
        for q in range(keep_n // SPAN):
            hits = []
            for row in each_row:
                near = jnp.clip(row - q * SPAN, -1.0, SPAN)
                near = jnp.broadcast_to(near, (16, GROUP)).astype(BF16)
                hit = jnp.where(inner == near[None], one, zero)
                hits.append(hit.reshape(SPAN, GROUP))
            acc[q * SPAN : (q + 1) * SPAN, :] += jnp.dot(
                jnp.concatenate(hits, axis=1), value_b[...], preferred_element_type=F32
            )
        return 0

    def settle(i, _):
        for j in range(CHUNK // GROUP):
            g = i * (CHUNK // GROUP) + j
            span = pl.ds(pl.multiple_of(g * GROUP, GROUP), GROUP)
            stays = 1.0 - sent[pl.ds(g, 1), :]
            mask = jnp.dot(
                jnp.where(diagonal, stays, 0.0).astype(BF16),
                jnp.ones((GROUP, err.shape[2]), BF16),
                preferred_element_type=F32,
            )
            err[0, span, :] = (grad[span, :].astype(F32) + err[0, span, :]) * mask
        return 0

    lax.fori_loop(0, chunks // 4, pack, 0)

    pl.semaphore_wait(round_z, 3)
    greet(round_x, line["x"])

    raw_swap.wait_recv()
    whole = state_rows[0]
    high = whole.astype(BF16)
    rest = whole - high.astype(F32)
    middle = rest.astype(BF16)
    low = (rest - middle.astype(F32)).astype(BF16)
    moments = [state_rows[a].astype(BF16) for a in (1, 2)]
    split = jnp.concatenate([high, middle, low, *moments], axis=1)

    def place(i, _):
        hits = onehot(chip_ranks == (iota((128, GROUP), 0) + i * 128).astype(F32))
        moved = jnp.dot(hits, split, preferred_element_type=F32)
        high, middle, low, *pair = (
            moved[:, p * 128 : (p + 1) * 128] for p in range(5)
        )
        values = ((high + middle) + low, *(value.astype(BF16) for value in pair))
        for a, order in enumerate(STATE_ORDERS):
            value = values[a].reshape(8, UNIT, 128)
            for u in range(8):
                spot = {"x": i // 2, "z": (i % 2) * 2 + u // 4, "y": u % 4}
                index = tuple(spot[axis] for axis in order)
                if a == 0:
                    master0[index] = value[u]
                else:
                    moment0[(a - 1, *index)] = value[u]
        return 0

    lax.fori_loop(0, keep_n // 128, place, 0)

    def state_phase(phase, source, target):
        for a, order in enumerate(STATE_ORDERS):
            axis = order[phase]
            n = phase * 3 + a
            for k in (1, 2, 3):
                copy(
                    source[a].at[(at[axis] + k) % 4], target[a].at[k - 1],
                    s_send.at[n], s_recv.at[n], along(axis, k),
                ).start()

    def state_bytes(phase, target, a):
        n = phase * 3 + a
        return bytes_of(target[a], s_send.at[n], s_recv.at[n])

    def state_sum(phase, source, target, total):
        for a in range(3):
            state_bytes(phase, target, a).wait_recv()
        for a, order in enumerate(STATE_ORDERS):
            value = source[a][at[order[phase]]].astype(F32)
            for k in range(3):
                value = value + target[a][k].astype(F32)
            total[a][...] = value.astype(total[a].dtype)

    state_phase(0, state, sgot1)

    lax.fori_loop(chunks // 4, chunks // 2, pack, 0)

    for s in range(3):
        arrive(0, s)
    spread(1)
    for s in range(3):
        forward(0, s)

    lax.fori_loop(chunks // 2, chunks, pack, 0)

    for h in range(2):
        packed[h] = (
            acc[:, h * 128 : (h + 1) * 128].astype(BF16).reshape(packed.shape[1:])
        )
    swap = copy(packed.at[1 - c], from_core, core_send, core_recv, sibling)
    swap.start()

    state_sum(0, state, sgot1, state1)
    state_phase(1, state1, sgot2)

    pl.semaphore_wait(round_x, 3)

    swap.wait_recv()
    part[...] = (packed[c].astype(F32) + from_core[...].astype(F32)).astype(BF16)

    def scatter(k):
        other, peer = far(k)
        return copy(part.at[other], got.at[k - 1], rs_send, rs_recv, peer)

    each(lambda k: scatter(k).start())
    own = packed[c, chip].astype(F32) + from_core[chip].astype(F32)

    for s in range(3):
        arrive(1, s)
    spread(2)
    for s in range(3):
        forward(1, s)

    state_sum(1, state1, sgot2, state2)
    state_phase(2, state2, sgot3)
    state_sum(2, state2, sgot3, state3)

    column[...] = jnp.transpose(jnp.broadcast_to(chip_ranks, (GROUP, GROUP)))
    half = column[own_rows, :]
    for k in range(keep_n // GROUP):
        lanes = (iota((64, GROUP), 1) + k * GROUP).astype(F32)
        expand[:, k * GROUP : (k + 1) * GROUP] = onehot(half == lanes)

    lax.fori_loop(0, chunks // 2, settle, 0)
    scattered = bytes_of(got, rs_send, rs_recv)
    scattered.wait_recv()
    summed = (own + jnp.sum(got[...].astype(F32), axis=0)).astype(BF16)
    new_master, _, _ = adamw(*(ref[...].astype(F32) for ref in state3), summed.astype(F32))
    result[c, chip, 0] = summed
    result[c, chip, 1] = new_master.astype(BF16)

    plane = chips // 4

    def gather(k):
        unit = result.at[c, chip]
        return copy(unit, unit, ag_send, ag_recv.at[x], far(k)[1])

    def pass_on(q):
        block = result.at[c, pl.ds(q * plane, plane)]
        return copy(block, block, half_send, half_recv, sibling)

    each(lambda k: gather(k).start())
    lax.fori_loop(chunks // 2, chunks, settle, 0)

    for k in (3, 2, 1):
        q = (x + k) % 4
        block = result.at[c, pl.ds(q * plane, plane)]
        bytes_of(block, ag_send, ag_recv.at[q]).wait_recv()
        pass_on(q).start()
    bytes_of(result.at[c, pl.ds(0, plane - 1)], ag_send, ag_recv.at[x]).wait_recv()
    pass_on(x).start()

    for s in range(3):
        arrive(2, s)
        forward(2, s)

    scattered.wait_send()
    bytes_of(result.at[c, pl.ds(0, chips - 1)], ag_send, ag_recv.at[x]).wait_send()
    raw_swap.wait_send()
    swap.wait_send()
    own_forward.wait()
    for a in range(3):
        state_bytes(0, sgot1, a).wait_send()
        state_bytes(1, sgot2, a).wait_send()
        state_bytes(2, sgot3, a).wait_send()
    for phase in range(3):
        for s in range(3):
            triple(s, phase, w_send, w_recv).wait_send()
            triple(s, phase, f_send, f_recv).wait()
    bytes_of(result.at[c], half_send, half_recv).wait()


def finish_kernel(
    err, weights, result, expand, rooted, starts_v, master, first, second,
    err_hbm, out_hbm, new_master, new_first, new_second,
    out, starts, err_sem, out_sem, starts_sem,
):
    groups = rooted.shape[0]
    to_smem = pltpu.make_async_copy(starts_v, starts, starts_sem)
    to_smem.start()
    rows = err.shape[1]
    pieces = err_sem.shape[0]
    copies = []
    for i in range(pieces):
        span = pl.ds(i * (rows // pieces), rows // pieces)
        go = pltpu.make_async_copy(err.at[0, span], err_hbm.at[0, span], err_sem.at[i])
        go.start()
        copies.append(go)

    total = jnp.concatenate(
        [
            jnp.dot(
                expand[...], result[h, :, 0].reshape(-1, 128),
                preferred_element_type=F32,
            )
            for h in range(2)
        ],
        axis=1,
    )
    new_master[...], new_first[...], new_second[...] = adamw(
        master[...], first[...], second[...], total
    )

    to_smem.wait()
    units = result.shape[1]
    window = GROUP // UNIT + 1
    batch = groups // out_sem.shape[0]

    def store(i):
        span = pl.ds(i * batch, batch)
        return pltpu.make_async_copy(out.at[span], out_hbm.at[span], out_sem.at[i])

    def fill(i, _):
        for j in range(batch):
            g = i * batch + j
            unit = jnp.minimum(starts[g, 0] // UNIT, units - window)
            near = rooted[pl.ds(g, 1), :] - (unit * UNIT).astype(F32)
            hits = onehot(iota((window * UNIT, GROUP), 0).astype(F32) == near)
            held = [
                result[h, pl.ds(unit, window), 1].reshape(window * UNIT, 128)
                for h in range(2)
            ]
            held = jnp.concatenate([*held, jnp.ones_like(held[0])], axis=1)
            moved = lax.dot_general(
                hits, held, (((0,), (0,)), ((), ())), preferred_element_type=F32
            )
            for c in range(2):
                span = slice(c * 64, c * 64 + 64)
                reached = moved[span, 256:] > 0.5
                for h in range(2):
                    lanes = slice(h * 128, h * 128 + 128)
                    before = weights[g, c, h].astype(F32)
                    out[g, span, lanes] = jnp.where(
                        reached, moved[span, lanes], before
                    ).astype(BF16)
        store(i).start()
        return 0

    steps = out_sem.shape[0]
    lax.fori_loop(0, steps, fill, 0)
    for go in copies:
        go.wait()
    lax.fori_loop(0, steps, lambda i, _: (store(i).wait(), 0)[1], 0)


def body(gradients, error_memory, block_lists, master, first_moment, second_moment):
    _, rows, width = gradients.shape
    owned = master.shape[0]
    levels, keep_n = block_lists.shape[1:]
    groups = rows // GROUP
    chunks = rows // CHUNK
    vmem = pl.BlockSpec(memory_space=pltpu.VMEM)
    anywhere = pl.BlockSpec(memory_space=pl.ANY)
    dma = pltpu.SemaphoreType.DMA

    err, weights, result, expand, rooted, starts = pl.pallas_call(
        merge_kernel,
        out_shape=(
            pltpu.VMEM((1, rows, width), F32),
            pltpu.VMEM((4, 4, 4, 2, 2, owned, 128), BF16),
            pltpu.VMEM((2, groups, 2, UNIT, 128), BF16),
            pltpu.VMEM((owned, keep_n), BF16),
            pltpu.VMEM((groups, GROUP), F32),
            pltpu.VMEM((groups, GROUP), jnp.int32),
        ),
        in_specs=[anywhere] * 6,
        out_specs=(vmem,) * 6,
        scratch_shapes=[
            pltpu.VMEM((rows, width), BF16),
            pltpu.VMEM((levels, keep_n), jnp.int32),
            pltpu.VMEM((2, 3, owned, 128), F32),
            pltpu.VMEM((3, GROUP, 128), F32),
            pltpu.VMEM((keep_n, width), F32),
            pltpu.VMEM((groups, GROUP), F32),
            pltpu.VMEM((groups, GROUP), F32),
            pltpu.VMEM((GROUP, GROUP), F32),
            pltpu.VMEM((CHUNK, width), BF16),
            pltpu.VMEM((2, groups, UNIT, 128), BF16),
            pltpu.VMEM((groups, UNIT, 128), BF16),
            pltpu.VMEM((groups, UNIT, 128), BF16),
            pltpu.VMEM((groups - 1, UNIT, 128), BF16),
            *(
                pltpu.VMEM((*lead, *shape, UNIT, 128), kind)
                for lead, kind in (((), F32), ((2,), BF16))
                for shape in (
                    (4, 4, 4), (4, 4), (4,), (), (3, 4, 4), (3, 4), (3,)
                )
            ),
            dma((chunks,)), dma((chunks,)), dma, dma,
            dma, dma, dma, dma,
            dma, dma, dma, dma((4,)), dma, dma,
            dma((9,)), dma((9,)),
            dma((9,)), dma((9,)),
            dma((10,)), dma((10,)),
            pltpu.SemaphoreType.REGULAR, pltpu.SemaphoreType.REGULAR,
        ],
        compiler_params=pltpu.CompilerParams(
            collective_id=0, has_side_effects=True, vmem_limit_bytes=46 * MIB
        ),
        name="merge",
    )(gradients, error_memory, block_lists, master, first_moment, second_moment)

    new_errors, out, new_master, new_first, new_second = pl.pallas_call(
        finish_kernel,
        out_shape=(
            jax.ShapeDtypeStruct((1, rows, width), F32),
            jax.ShapeDtypeStruct((groups, GROUP, width), BF16),
            jax.ShapeDtypeStruct((owned, width), F32),
            jax.ShapeDtypeStruct((owned, width), F32),
            jax.ShapeDtypeStruct((owned, width), F32),
        ),
        in_specs=[vmem] * 9,
        out_specs=(anywhere, anywhere, vmem, vmem, vmem),
        scratch_shapes=[
            pltpu.VMEM((groups, GROUP, width), BF16),
            pltpu.SMEM((groups, GROUP), jnp.int32),
            dma((4,)), dma((8,)), dma,
        ],
        compiler_params=pltpu.CompilerParams(vmem_limit_bytes=32 * MIB),
        name="finish",
    )(
        err, weights.reshape(groups, 2, 2, owned, 128), result, expand, rooted, starts,
        master, first_moment, second_moment,
    )
    return new_errors, new_master, new_first, new_second, out.reshape(rows, width)


def solution(mesh):
    in_specs = (
        P("dp", None, None),
        P("dp", None, None),
        P("dp", None, None),
        P("dp", None),
        P("dp", None),
        P("dp", None),
    )
    out_specs = (P("dp", None, None), P("dp", None), P("dp", None), P("dp", None), P())
    return jax.shard_map(
        body, mesh=mesh, in_specs=in_specs, out_specs=out_specs, check_vma=False
    )
```

```python
import jax
import jax.numpy as jnp
from jax import lax
from jax.experimental import pallas as pl
from jax.experimental.pallas import tpu as pltpu
from jax.sharding import PartitionSpec as P

FIRST_BIAS = 0.9999734386011124
SECOND_BIAS = 0.09520785288629036
MESH = pl.DeviceIdType.MESH
F32 = jnp.float32
BF16 = jnp.bfloat16
MIB = 1 << 20

GROUP = 128
CHUNK = 1024
UNIT = 16
SPAN = 256

ORDERS = ("xzy", "zyx", "yxz")
STATE_ORDERS = ("zyx", "xzy", "yxz")


def iota(shape, dim):
    return lax.broadcasted_iota(jnp.int32, shape, dim)


def onehot(hits):
    return jnp.where(hits, 1.0, 0.0).astype(BF16)


def adamw(master, first, second, summed):
    new_first = 0.9 * first + 0.1 * summed
    new_second = 0.999 * second + 0.001 * summed * summed
    first_hat = new_first / FIRST_BIAS
    second_hat = new_second / SECOND_BIAS
    new_master = master - 0.001 * (
        first_hat / (jnp.sqrt(second_hat) + 1e-08) + 0.1 * master
    )
    return new_master, new_first, new_second


def merge_kernel(
    grad_hbm, err_hbm, lists_hbm, master_hbm, first_hbm, second_hbm,
    err, weights, result, expand, rooted, starts,
    grad, lists, raw, raw_b, acc, sent, kept, column, value_b,
    packed, from_core, part, got,
    master0, master1, master2, master3, mgot2, mgot3,
    moment0, moment1, moment2, moment3, vgot2, vgot3,
    grad_sem, err_sem, list_sem, raw_sem,
    core_send, core_recv, raw_send, raw_recv, rawb_send, rawb_recv,
    rs_send, rs_recv, ag_send, ag_recv, half_send, half_recv,
    s_send, s_recv, w_send, w_recv, f_send, f_recv, round_z, round_x,
):
    rows = grad.shape[0]
    groups = rows // GROUP
    chunks = rows // CHUNK
    levels, keep_n = lists.shape
    me = lax.axis_index("dp")
    c = me % 2
    y = (me // 2) % 4
    z = (me // 8) % 4
    x = me // 32
    chip = me // 2
    chips = groups
    sibling = me + 1 - 2 * c
    at = {"x": x, "z": z, "y": y}
    strides = {"x": 32, "z": 8, "y": 2}

    def far(k):
        other = (chip + k) % chips
        return other, 2 * other + c

    def along(axis, k):
        return me + ((at[axis] + k) % 4 - at[axis]) * strides[axis]

    def copy(src, dst, send, recv, peer):
        return pltpu.make_async_remote_copy(
            src_ref=src, dst_ref=dst, send_sem=send, recv_sem=recv,
            device_id=(peer,), device_id_type=MESH,
        )

    def each(act):
        def nine(i, _):
            for j in range(9):
                act(i * 9 + j + 1)
            return 0

        lax.fori_loop(0, (chips - 1) // 9, nine, 0)

    def bytes_of(ref, send, recv):
        return copy(ref, ref, send, recv, sibling)

    def three(master_ref, moments_ref):
        return master_ref, moments_ref.at[0], moments_ref.at[1]

    state = three(master0, moment0)
    state1 = three(master1, moment1)
    state2 = three(master2, moment2)
    state3 = three(master3, moment3)
    sgot2 = three(mgot2, vgot2)
    sgot3 = three(mgot3, vgot3)

    def greet(semaphore, peers):
        for peer in peers:
            pl.semaphore_signal(
                semaphore, inc=1, device_id=(peer,), device_id_type=MESH
            )

    line = {axis: [along(axis, k) for k in (1, 2, 3)] for axis in "xzy"}
    barrier = pltpu.get_barrier_semaphore()
    greet(barrier, [sibling, *line["y"], *line["z"], *line["x"]])

    list_load = pltpu.make_async_copy(lists_hbm.at[0], lists, list_sem)
    list_load.start()
    for a, source in enumerate((master_hbm, first_hbm, second_hbm)):
        for h in range(2):
            go = pltpu.make_async_copy(
                source.at[:, pl.ds(h * 128, 128)], raw.at[h, a], raw_sem
            )
            go.start()

    def loads(i):
        span = pl.ds(pl.multiple_of(i * CHUNK, CHUNK), CHUNK)
        return (
            pltpu.make_async_copy(grad_hbm.at[0, span], grad.at[span], grad_sem.at[i]),
            pltpu.make_async_copy(err_hbm.at[0, span], err.at[0, span], err_sem.at[i]),
        )

    def load(i, _):
        for go in loads(i):
            go.start()
        return 0

    lax.fori_loop(0, chunks, load, 0)

    pltpu.make_async_copy(raw, raw, raw_sem).wait()
    for h in range(2):
        new_master, _, _ = adamw(raw[h, 0], raw[h, 1], raw[h, 2], 0.0)
        weights[x, z, y, c, h] = new_master.astype(BF16)
    own_rows = pl.ds(pl.multiple_of(c * 64, 64), 64)
    raw_b[...] = raw[:, 1:].astype(BF16)
    mine_at = [at[order[0]] for order in STATE_ORDERS]
    master0[mine_at[0], own_rows, :] = raw[c, 0]
    for a in (1, 2):
        moment0[a - 1, mine_at[a], own_rows, :] = raw_b[c, a - 1]

    pl.semaphore_wait(barrier, 10)
    greet(round_z, line["z"])

    raw_swaps = [
        copy(
            raw.at[1 - c, 0], state[0].at[mine_at[0], own_rows],
            raw_send, raw_recv, sibling,
        )
    ]
    for a in (1, 2):
        raw_swaps.append(
            copy(
                raw_b.at[1 - c, a - 1], state[a].at[mine_at[a], own_rows],
                rawb_send.at[a - 1], rawb_recv.at[a - 1], sibling,
            )
        )
    for go in raw_swaps:
        go.start()

    parts = (
        ((0,), pl.ds(0, 48)),
        ((1,), pl.ds(0, 48)),
        ((pl.ds(0, 2),), pl.ds(48, 16)),
    )

    def region(s, taken, place):
        cols, span = parts[s]
        index = tuple(pl.ds(0, 4) if axis in taken else place[axis] for axis in "xzy")
        return weights.at[(*index, c, *cols, span)]

    def triple(s, phase, sends, recvs):
        order = ORDERS[s]
        block = region(s, order[:phase], {**at, order[phase]: pl.ds(0, 3)})
        n = s * 3 + phase
        return bytes_of(block, sends.at[n], recvs.at[n])

    def spread(phase):
        for s, order in enumerate(ORDERS):
            axis = order[phase]
            block = region(s, order[:phase], at)
            n = s * 3 + phase
            for k in (1, 2, 3):
                copy(
                    block, block, w_send.at[n], w_recv.at[n], along(axis, k)
                ).start()

    def arrive(phase, s):
        triple(s, phase, w_send, w_recv).wait_recv()

    def forward(phase, s):
        order = ORDERS[s]
        axis = order[phase]
        n = s * 3 + phase
        for k in (1, 2, 3):
            block = region(s, order[:phase], {**at, axis: (at[axis] + k) % 4})
            copy(block, block, f_send.at[n], f_recv.at[n], sibling).start()

    spread(0)
    mine = weights.at[x, z, y, c]
    own_forward = copy(mine, mine, f_send.at[9], f_recv.at[9], sibling)
    own_forward.start()

    list_load.wait()

    def member(r):
        ids = lists[r : r + 1, :]
        high = onehot(iota((groups, keep_n), 0) == ids // GROUP)
        low = onehot(iota((GROUP, keep_n), 0) == ids % GROUP)
        return lax.dot_general(
            high, low, (((1,), (1,)), ((), ())), preferred_element_type=F32
        )

    root = member(levels - 1)
    root_b = root.astype(BF16)
    before = onehot(iota((GROUP, GROUP), 0) < iota((GROUP, GROUP), 1))
    inside = jnp.dot(root_b, before, preferred_element_type=F32)
    total = jnp.dot(root_b, jnp.ones((GROUP, GROUP), BF16), preferred_element_type=F32)
    above = onehot(iota((groups, groups), 1) < iota((groups, groups), 0))
    start = jnp.dot(above, total.astype(BF16), preferred_element_type=F32)
    rank = start + inside
    starts[...] = start.astype(jnp.int32)
    rooted[...] = jnp.where(root > 0.5, rank, -1.0)

    for go in raw_swaps:
        go.wait_recv()
    for a, order in enumerate(STATE_ORDERS):
        block = state[a].at[mine_at[a]]
        for k in (1, 2, 3):
            copy(
                block, block, s_send.at[a], s_recv.at[a], along(order[0], k)
            ).start()

    keep = member(0)
    sent[...] = keep
    for r in range(1, levels - 1):
        keep = keep * member(r)
    kept[...] = jnp.where(keep * root > 0.5, rank, -1.0)

    chip_ranks = rooted[pl.ds(chip, 1), :]

    acc[...] = jnp.zeros_like(acc)
    diagonal = iota((GROUP, GROUP), 0) == iota((GROUP, GROUP), 1)
    inner = iota((SPAN // 16, 16, GROUP), 0) * 16 + iota((SPAN // 16, 16, GROUP), 1)
    inner = inner.astype(F32).astype(BF16)
    one = jnp.ones((SPAN // 16, 16, GROUP), BF16)
    zero = jnp.zeros((SPAN // 16, 16, GROUP), BF16)

    def pack(i, _):
        for go in loads(i):
            go.wait()
        each_row = []
        for j in range(CHUNK // GROUP):
            g = i * (CHUNK // GROUP) + j
            span = pl.ds(pl.multiple_of(g * GROUP, GROUP), GROUP)
            value = grad[span, :].astype(F32) + err[0, span, :]
            value_b[j * GROUP : (j + 1) * GROUP, :] = value.astype(BF16)
            each_row.append(kept[pl.ds(g, 1), :])
        for q in range(keep_n // SPAN):
            hits = []
            for row in each_row:
                near = jnp.clip(row - q * SPAN, -1.0, SPAN)
                near = jnp.broadcast_to(near, (16, GROUP)).astype(BF16)
                hit = jnp.where(inner == near[None], one, zero)
                hits.append(hit.reshape(SPAN, GROUP))
            acc[q * SPAN : (q + 1) * SPAN, :] += jnp.dot(
                jnp.concatenate(hits, axis=1), value_b[...], preferred_element_type=F32
            )
        return 0

    def settle(i, _):
        for j in range(CHUNK // GROUP):
            g = i * (CHUNK // GROUP) + j
            span = pl.ds(pl.multiple_of(g * GROUP, GROUP), GROUP)
            stays = 1.0 - sent[pl.ds(g, 1), :]
            mask = jnp.dot(
                jnp.where(diagonal, stays, 0.0).astype(BF16),
                jnp.ones((GROUP, err.shape[2]), BF16),
                preferred_element_type=F32,
            )
            err[0, span, :] = (grad[span, :].astype(F32) + err[0, span, :]) * mask
        return 0

    lax.fori_loop(0, chunks // 4, pack, 0)

    pl.semaphore_wait(round_z, 3)
    greet(round_x, line["x"])

    def place(a):
        order = STATE_ORDERS[a]
        bytes_of(state[a].at[pl.ds(0, 3)], s_send.at[a], s_recv.at[a]).wait_recv()
        units = {"x": 16, "z": 4, "y": 1}
        spot = iota((16 * UNIT, GROUP), 0)
        target = (
            (spot // 64) * (units[order[1]] * UNIT)
            + (spot // 16) % 4 * (units[order[2]] * UNIT)
            + spot % 16
            + at[order[0]] * (units[order[0]] * UNIT)
        ).astype(F32)
        hits = []
        for k in range(4):
            source = chip + (k - at[order[0]]) * units[order[0]]
            hits.append(onehot(rooted[pl.ds(source, 1), :] == target))
        hits = jnp.concatenate(hits, axis=1)
        whole = state[a][...].reshape(4 * GROUP, 128)
        if a:
            split = whole
        else:
            high = whole.astype(BF16)
            rest = whole - high.astype(F32)
            middle = rest.astype(BF16)
            low = (rest - middle.astype(F32)).astype(BF16)
            split = jnp.concatenate([high, middle, low], axis=1)
        moved = jnp.dot(hits, split, preferred_element_type=F32)
        if not a:
            moved = (moved[:, :128] + moved[:, 128:256]) + moved[:, 256:]
        state1[a][...] = moved.astype(state1[a].dtype).reshape(state1[a].shape)

    def state_phase(phase, source, target):
        for a, order in enumerate(STATE_ORDERS):
            axis = order[phase]
            n = phase * 3 + a
            for k in (1, 2, 3):
                copy(
                    source[a].at[(at[axis] + k) % 4], target[a].at[k - 1],
                    s_send.at[n], s_recv.at[n], along(axis, k),
                ).start()

    def state_bytes(phase, target, a):
        n = phase * 3 + a
        return bytes_of(target[a], s_send.at[n], s_recv.at[n])

    def state_sum(phase, source, target, total):
        for a in range(3):
            state_bytes(phase, target, a).wait_recv()
        for a, order in enumerate(STATE_ORDERS):
            value = source[a][at[order[phase]]].astype(F32)
            for k in range(3):
                value = value + target[a][k].astype(F32)
            total[a][...] = value.astype(total[a].dtype)

    lax.fori_loop(chunks // 4, chunks // 2, pack, 0)

    for s in range(3):
        arrive(0, s)
    spread(1)
    for s in range(3):
        forward(0, s)

    for a in range(3):
        place(a)
    state_phase(1, state1, sgot2)

    lax.fori_loop(chunks // 2, chunks, pack, 0)

    for h in range(2):
        packed[h] = (
            acc[:, h * 128 : (h + 1) * 128].astype(BF16).reshape(packed.shape[1:])
        )
    swap = copy(packed.at[1 - c], from_core, core_send, core_recv, sibling)
    swap.start()

    pl.semaphore_wait(round_x, 3)

    swap.wait_recv()
    part[...] = (packed[c].astype(F32) + from_core[...].astype(F32)).astype(BF16)

    def scatter(k):
        other, peer = far(k)
        return copy(part.at[other], got.at[k - 1], rs_send, rs_recv, peer)

    each(lambda k: scatter(k).start())
    own = packed[c, chip].astype(F32) + from_core[chip].astype(F32)

    for s in range(3):
        arrive(1, s)
    spread(2)
    for s in range(3):
        forward(1, s)

    state_sum(1, state1, sgot2, state2)
    state_phase(2, state2, sgot3)

    column[...] = jnp.transpose(jnp.broadcast_to(chip_ranks, (GROUP, GROUP)))
    half = column[own_rows, :]
    for k in range(keep_n // GROUP):
        lanes = (iota((64, GROUP), 1) + k * GROUP).astype(F32)
        expand[:, k * GROUP : (k + 1) * GROUP] = onehot(half == lanes)

    lax.fori_loop(0, chunks // 2, settle, 0)
    state_sum(2, state2, sgot3, state3)
    scattered = bytes_of(got, rs_send, rs_recv)
    scattered.wait_recv()
    summed = (own + jnp.sum(got[...].astype(F32), axis=0)).astype(BF16)
    new_master, _, _ = adamw(*(ref[...].astype(F32) for ref in state3), summed.astype(F32))
    result[c, chip, 0] = summed
    result[c, chip, 1] = new_master.astype(BF16)

    plane = chips // 4

    def gather(k):
        unit = result.at[c, chip]
        return copy(unit, unit, ag_send, ag_recv.at[x], far(k)[1])

    def pass_on(q):
        block = result.at[c, pl.ds(q * plane, plane)]
        return copy(block, block, half_send, half_recv, sibling)

    each(lambda k: gather(k).start())
    lax.fori_loop(chunks // 2, chunks, settle, 0)

    for k in (3, 2, 1):
        q = (x + k) % 4
        block = result.at[c, pl.ds(q * plane, plane)]
        bytes_of(block, ag_send, ag_recv.at[q]).wait_recv()
        pass_on(q).start()
    bytes_of(result.at[c, pl.ds(0, plane - 1)], ag_send, ag_recv.at[x]).wait_recv()
    pass_on(x).start()

    for s in range(3):
        arrive(2, s)
        forward(2, s)

    scattered.wait_send()
    bytes_of(result.at[c, pl.ds(0, chips - 1)], ag_send, ag_recv.at[x]).wait_send()
    for go in raw_swaps:
        go.wait_send()
    swap.wait_send()
    own_forward.wait()
    for a in range(3):
        bytes_of(state[a].at[pl.ds(0, 3)], s_send.at[a], s_recv.at[a]).wait_send()
        state_bytes(1, sgot2, a).wait_send()
        state_bytes(2, sgot3, a).wait_send()
    for phase in range(3):
        for s in range(3):
            triple(s, phase, w_send, w_recv).wait_send()
            triple(s, phase, f_send, f_recv).wait()
    bytes_of(result.at[c], half_send, half_recv).wait()


def finish_kernel(
    err, weights, result, expand, rooted, starts_v, master, first, second,
    err_hbm, out_hbm, new_master, new_first, new_second,
    out, starts, err_sem, out_sem, starts_sem,
):
    groups = rooted.shape[0]
    to_smem = pltpu.make_async_copy(starts_v, starts, starts_sem)
    to_smem.start()
    rows = err.shape[1]
    pieces = err_sem.shape[0]
    copies = []
    for i in range(pieces):
        span = pl.ds(i * (rows // pieces), rows // pieces)
        go = pltpu.make_async_copy(err.at[0, span], err_hbm.at[0, span], err_sem.at[i])
        go.start()
        copies.append(go)

    total = jnp.concatenate(
        [
            jnp.dot(
                expand[...], result[h, :, 0].reshape(-1, 128),
                preferred_element_type=F32,
            )
            for h in range(2)
        ],
        axis=1,
    )
    new_master[...], new_first[...], new_second[...] = adamw(
        master[...], first[...], second[...], total
    )

    to_smem.wait()
    units = result.shape[1]
    window = GROUP // UNIT + 1
    batch = groups // out_sem.shape[0]

    def store(i):
        span = pl.ds(i * batch, batch)
        return pltpu.make_async_copy(out.at[span], out_hbm.at[span], out_sem.at[i])

    def fill(i, _):
        for j in range(batch):
            g = i * batch + j
            unit = jnp.minimum(starts[g, 0] // UNIT, units - window)
            near = rooted[pl.ds(g, 1), :] - (unit * UNIT).astype(F32)
            hits = onehot(iota((window * UNIT, GROUP), 0).astype(F32) == near)
            held = [
                result[h, pl.ds(unit, window), 1].reshape(window * UNIT, 128)
                for h in range(2)
            ]
            held = jnp.concatenate([*held, jnp.ones_like(held[0])], axis=1)
            moved = lax.dot_general(
                hits, held, (((0,), (0,)), ((), ())), preferred_element_type=F32
            )
            for c in range(2):
                span = slice(c * 64, c * 64 + 64)
                reached = moved[span, 256:] > 0.5
                for h in range(2):
                    lanes = slice(h * 128, h * 128 + 128)
                    before = weights[g, c, h].astype(F32)
                    out[g, span, lanes] = jnp.where(
                        reached, moved[span, lanes], before
                    ).astype(BF16)
        store(i).start()
        return 0

    steps = out_sem.shape[0]
    lax.fori_loop(0, steps, fill, 0)
    for go in copies:
        go.wait()
    lax.fori_loop(0, steps, lambda i, _: (store(i).wait(), 0)[1], 0)


def body(gradients, error_memory, block_lists, master, first_moment, second_moment):
    _, rows, width = gradients.shape
    owned = master.shape[0]
    levels, keep_n = block_lists.shape[1:]
    groups = rows // GROUP
    chunks = rows // CHUNK
    vmem = pl.BlockSpec(memory_space=pltpu.VMEM)
    anywhere = pl.BlockSpec(memory_space=pl.ANY)
    dma = pltpu.SemaphoreType.DMA

    err, weights, result, expand, rooted, starts = pl.pallas_call(
        merge_kernel,
        out_shape=(
            pltpu.VMEM((1, rows, width), F32),
            pltpu.VMEM((4, 4, 4, 2, 2, owned, 128), BF16),
            pltpu.VMEM((2, groups, 2, UNIT, 128), BF16),
            pltpu.VMEM((owned, keep_n), BF16),
            pltpu.VMEM((groups, GROUP), F32),
            pltpu.VMEM((groups, GROUP), jnp.int32),
        ),
        in_specs=[anywhere] * 6,
        out_specs=(vmem,) * 6,
        scratch_shapes=[
            pltpu.VMEM((rows, width), BF16),
            pltpu.VMEM((levels, keep_n), jnp.int32),
            pltpu.VMEM((2, 3, owned, 128), F32),
            pltpu.VMEM((2, 2, owned, 128), BF16),
            pltpu.VMEM((keep_n, width), F32),
            pltpu.VMEM((groups, GROUP), F32),
            pltpu.VMEM((groups, GROUP), F32),
            pltpu.VMEM((GROUP, GROUP), F32),
            pltpu.VMEM((CHUNK, width), BF16),
            pltpu.VMEM((2, groups, UNIT, 128), BF16),
            pltpu.VMEM((groups, UNIT, 128), BF16),
            pltpu.VMEM((groups, UNIT, 128), BF16),
            pltpu.VMEM((groups - 1, UNIT, 128), BF16),
            *(
                pltpu.VMEM((*lead, *shape, 128), kind)
                for lead, kind in (((), F32), ((2,), BF16))
                for shape in (
                    (4, GROUP), (4, 4, UNIT), (4, UNIT), (UNIT,),
                    (3, 4, UNIT), (3, UNIT),
                )
            ),
            dma((chunks,)), dma((chunks,)), dma, dma,
            dma, dma, dma, dma, dma((2,)), dma((2,)),
            dma, dma, dma, dma((4,)), dma, dma,
            dma((9,)), dma((9,)),
            dma((9,)), dma((9,)),
            dma((10,)), dma((10,)),
            pltpu.SemaphoreType.REGULAR, pltpu.SemaphoreType.REGULAR,
        ],
        compiler_params=pltpu.CompilerParams(
            collective_id=0, has_side_effects=True, vmem_limit_bytes=46 * MIB
        ),
        name="merge",
    )(gradients, error_memory, block_lists, master, first_moment, second_moment)

    new_errors, out, new_master, new_first, new_second = pl.pallas_call(
        finish_kernel,
        out_shape=(
            jax.ShapeDtypeStruct((1, rows, width), F32),
            jax.ShapeDtypeStruct((groups, GROUP, width), BF16),
            jax.ShapeDtypeStruct((owned, width), F32),
            jax.ShapeDtypeStruct((owned, width), F32),
            jax.ShapeDtypeStruct((owned, width), F32),
        ),
        in_specs=[vmem] * 9,
        out_specs=(anywhere, anywhere, vmem, vmem, vmem),
        scratch_shapes=[
            pltpu.VMEM((groups, GROUP, width), BF16),
            pltpu.SMEM((groups, GROUP), jnp.int32),
            dma((4,)), dma((8,)), dma,
        ],
        compiler_params=pltpu.CompilerParams(vmem_limit_bytes=32 * MIB),
        name="finish",
    )(
        err, weights.reshape(groups, 2, 2, owned, 128), result, expand, rooted, starts,
        master, first_moment, second_moment,
    )
    return new_errors, new_master, new_first, new_second, out.reshape(rows, width)


def solution(mesh):
    in_specs = (
        P("dp", None, None),
        P("dp", None, None),
        P("dp", None, None),
        P("dp", None),
        P("dp", None),
        P("dp", None),
    )
    out_specs = (P("dp", None, None), P("dp", None), P("dp", None), P("dp", None), P())
    return jax.shard_map(
        body, mesh=mesh, in_specs=in_specs, out_specs=out_specs, check_vma=False
    )
```

```python
import jax
import jax.numpy as jnp
from jax import lax
from jax.experimental import pallas as pl
from jax.experimental.pallas import tpu as pltpu
from jax.sharding import PartitionSpec as P

FIRST_BIAS = 0.9999734386011124
SECOND_BIAS = 0.09520785288629036
MESH = pl.DeviceIdType.MESH
F32 = jnp.float32
BF16 = jnp.bfloat16
MIB = 1 << 20

GROUP = 128
CHUNK = 1024
UNIT = 16
SPAN = 256

ORDERS = ("xzy", "zyx", "yxz")
STATE_ORDERS = ("zyx", "xzy", "yxz")


def iota(shape, dim):
    return lax.broadcasted_iota(jnp.int32, shape, dim)


def onehot(hits):
    return jnp.where(hits, 1.0, 0.0).astype(BF16)


def adamw(master, first, second, summed):
    new_first = 0.9 * first + 0.1 * summed
    new_second = 0.999 * second + 0.001 * summed * summed
    first_hat = new_first / FIRST_BIAS
    second_hat = new_second / SECOND_BIAS
    new_master = master - 0.001 * (
        first_hat / (jnp.sqrt(second_hat) + 1e-08) + 0.1 * master
    )
    return new_master, new_first, new_second


def merge_kernel(
    grad_hbm, err_hbm, lists_hbm, master_hbm, first_hbm, second_hbm,
    err, weights, result, expand, rooted, starts,
    grad, lists, raw, raw_b, acc, sent, kept, column, value_b,
    packed, from_core, part, got,
    master0, master1, master2, master3, mgot2, mgot3,
    moment0, moment1, moment2, moment3, vgot2, vgot3,
    grad_sem, err_sem, list_sem, raw_sem,
    core_send, core_recv, raw_send, raw_recv, rawb_send, rawb_recv,
    rs_send, rs_recv, ag_send, ag_recv, half_send, half_recv,
    s_send, s_recv, w_send, w_recv, f_send, f_recv, round_z, round_x,
):
    rows = grad.shape[0]
    groups = rows // GROUP
    chunks = rows // CHUNK
    levels, keep_n = lists.shape
    me = lax.axis_index("dp")
    c = me % 2
    y = (me // 2) % 4
    z = (me // 8) % 4
    x = me // 32
    chip = me // 2
    chips = groups
    sibling = me + 1 - 2 * c
    at = {"x": x, "z": z, "y": y}
    strides = {"x": 32, "z": 8, "y": 2}

    def far(k):
        other = (chip + k) % chips
        return other, 2 * other + c

    def along(axis, k):
        return me + ((at[axis] + k) % 4 - at[axis]) * strides[axis]

    def copy(src, dst, send, recv, peer):
        return pltpu.make_async_remote_copy(
            src_ref=src, dst_ref=dst, send_sem=send, recv_sem=recv,
            device_id=(peer,), device_id_type=MESH,
        )

    def each(act):
        def nine(i, _):
            for j in range(9):
                act(i * 9 + j + 1)
            return 0

        lax.fori_loop(0, (chips - 1) // 9, nine, 0)

    def bytes_of(ref, send, recv):
        return copy(ref, ref, send, recv, sibling)

    def three(master_ref, moments_ref):
        return master_ref, moments_ref.at[0], moments_ref.at[1]

    state = three(master0, moment0)
    state1 = three(master1, moment1)
    state2 = three(master2, moment2)
    state3 = three(master3, moment3)
    sgot2 = three(mgot2, vgot2)
    sgot3 = three(mgot3, vgot3)

    def greet(semaphore, peers):
        for peer in peers:
            pl.semaphore_signal(
                semaphore, inc=1, device_id=(peer,), device_id_type=MESH
            )

    line = {axis: [along(axis, k) for k in (1, 2, 3)] for axis in "xzy"}
    barrier = pltpu.get_barrier_semaphore()
    greet(barrier, [sibling, *line["y"], *line["z"], *line["x"]])

    list_load = pltpu.make_async_copy(lists_hbm.at[0], lists, list_sem)
    list_load.start()
    for a, source in enumerate((master_hbm, first_hbm, second_hbm)):
        for h in range(2):
            go = pltpu.make_async_copy(
                source.at[:, pl.ds(h * 128, 128)], raw.at[h, a], raw_sem
            )
            go.start()

    def loads(i):
        span = pl.ds(pl.multiple_of(i * CHUNK, CHUNK), CHUNK)
        return (
            pltpu.make_async_copy(grad_hbm.at[0, span], grad.at[span], grad_sem.at[i]),
            pltpu.make_async_copy(err_hbm.at[0, span], err.at[0, span], err_sem.at[i]),
        )

    def load(i, _):
        for go in loads(i):
            go.start()
        return 0

    lax.fori_loop(0, chunks, load, 0)

    pltpu.make_async_copy(raw, raw, raw_sem).wait()
    for h in range(2):
        new_master, _, _ = adamw(raw[h, 0], raw[h, 1], raw[h, 2], 0.0)
        weights[x, z, y, c, h] = new_master.astype(BF16)
    own_rows = pl.ds(pl.multiple_of(c * 64, 64), 64)
    raw_b[...] = raw[:, 1:].astype(BF16)
    mine_at = [at[order[0]] for order in STATE_ORDERS]
    master0[mine_at[0], own_rows, :] = raw[c, 0]
    for a in (1, 2):
        moment0[a - 1, mine_at[a], own_rows, :] = raw_b[c, a - 1]

    pl.semaphore_wait(barrier, 10)
    greet(round_z, line["z"])

    raw_swaps = [
        copy(
            raw.at[1 - c, 0], state[0].at[mine_at[0], own_rows],
            raw_send, raw_recv, sibling,
        )
    ]
    for a in (1, 2):
        raw_swaps.append(
            copy(
                raw_b.at[1 - c, a - 1], state[a].at[mine_at[a], own_rows],
                rawb_send.at[a - 1], rawb_recv.at[a - 1], sibling,
            )
        )
    for go in raw_swaps:
        go.start()

    parts = (
        ((0,), pl.ds(0, 48)),
        ((1,), pl.ds(0, 48)),
        ((pl.ds(0, 2),), pl.ds(48, 16)),
    )
    pieces = (
        (((0,), pl.ds(0, 16)), ((0,), pl.ds(16, 32))),
        (((1,), pl.ds(0, 16)), ((1,), pl.ds(16, 32))),
        (((0,), pl.ds(48, 16)), ((1,), pl.ds(48, 16))),
    )

    def region(s, stage, place):
        cols, span = parts[s] if stage < 2 else pieces[s][stage - 2]
        taken = ORDERS[s][: min(stage, 2)]
        index = tuple(pl.ds(0, 4) if axis in taken else place[axis] for axis in "xzy")
        return weights.at[(*index, c, *cols, span)]

    def triple(s, stage, sends, recvs):
        axis = ORDERS[s][min(stage, 2)]
        n = s * 4 + stage
        block = region(s, stage, {**at, axis: pl.ds(0, 3)})
        return bytes_of(block, sends.at[n], recvs.at[n])

    def spread(stage):
        for s, order in enumerate(ORDERS):
            block = region(s, stage, at)
            n = s * 4 + stage
            for k in (1, 2, 3):
                copy(
                    block, block, w_send.at[n], w_recv.at[n],
                    along(order[min(stage, 2)], k),
                ).start()

    def arrive(stage, s):
        triple(s, stage, w_send, w_recv).wait_recv()

    def forward(stage, s):
        axis = ORDERS[s][min(stage, 2)]
        n = s * 4 + stage
        for k in (1, 2, 3):
            block = region(s, stage, {**at, axis: (at[axis] + k) % 4})
            copy(block, block, f_send.at[n], f_recv.at[n], sibling).start()

    spread(0)
    mine = weights.at[x, z, y, c]
    own_forward = copy(mine, mine, f_send.at[12], f_recv.at[12], sibling)
    own_forward.start()

    list_load.wait()

    def member(r):
        ids = lists[r : r + 1, :]
        high = onehot(iota((groups, keep_n), 0) == ids // GROUP)
        low = onehot(iota((GROUP, keep_n), 0) == ids % GROUP)
        return lax.dot_general(
            high, low, (((1,), (1,)), ((), ())), preferred_element_type=F32
        )

    root = member(levels - 1)
    root_b = root.astype(BF16)
    before = onehot(iota((GROUP, GROUP), 0) < iota((GROUP, GROUP), 1))
    inside = jnp.dot(root_b, before, preferred_element_type=F32)
    total = jnp.dot(root_b, jnp.ones((GROUP, GROUP), BF16), preferred_element_type=F32)
    above = onehot(iota((groups, groups), 1) < iota((groups, groups), 0))
    start = jnp.dot(above, total.astype(BF16), preferred_element_type=F32)
    rank = start + inside
    starts[...] = start.astype(jnp.int32)
    rooted[...] = jnp.where(root > 0.5, rank, -1.0)

    for go in raw_swaps:
        go.wait_recv()
    for a, order in enumerate(STATE_ORDERS):
        block = state[a].at[mine_at[a]]
        for k in (1, 2, 3):
            copy(
                block, block, s_send.at[a], s_recv.at[a], along(order[0], k)
            ).start()

    keep = member(0)
    sent[...] = keep
    for r in range(1, levels - 1):
        keep = keep * member(r)
    kept[...] = jnp.where(keep * root > 0.5, rank, -1.0)

    chip_ranks = rooted[pl.ds(chip, 1), :]

    acc[...] = jnp.zeros_like(acc)
    diagonal = iota((GROUP, GROUP), 0) == iota((GROUP, GROUP), 1)
    inner = iota((SPAN // 16, 16, GROUP), 0) * 16 + iota((SPAN // 16, 16, GROUP), 1)
    inner = inner.astype(F32).astype(BF16)
    one = jnp.ones((SPAN // 16, 16, GROUP), BF16)
    zero = jnp.zeros((SPAN // 16, 16, GROUP), BF16)

    def pack(i, _):
        for go in loads(i):
            go.wait()
        each_row = []
        for j in range(CHUNK // GROUP):
            g = i * (CHUNK // GROUP) + j
            span = pl.ds(pl.multiple_of(g * GROUP, GROUP), GROUP)
            value = grad[span, :].astype(F32) + err[0, span, :]
            value_b[j * GROUP : (j + 1) * GROUP, :] = value.astype(BF16)
            each_row.append(kept[pl.ds(g, 1), :])
        for q in range(keep_n // SPAN):
            hits = []
            for row in each_row:
                near = jnp.clip(row - q * SPAN, -1.0, SPAN)
                near = jnp.broadcast_to(near, (16, GROUP)).astype(BF16)
                hit = jnp.where(inner == near[None], one, zero)
                hits.append(hit.reshape(SPAN, GROUP))
            acc[q * SPAN : (q + 1) * SPAN, :] += jnp.dot(
                jnp.concatenate(hits, axis=1), value_b[...], preferred_element_type=F32
            )
        return 0

    def settle(i, _):
        for j in range(CHUNK // GROUP):
            g = i * (CHUNK // GROUP) + j
            span = pl.ds(pl.multiple_of(g * GROUP, GROUP), GROUP)
            stays = 1.0 - sent[pl.ds(g, 1), :]
            mask = jnp.dot(
                jnp.where(diagonal, stays, 0.0).astype(BF16),
                jnp.ones((GROUP, err.shape[2]), BF16),
                preferred_element_type=F32,
            )
            err[0, span, :] = (grad[span, :].astype(F32) + err[0, span, :]) * mask
        return 0

    lax.fori_loop(0, chunks // 4, pack, 0)

    pl.semaphore_wait(round_z, 3)
    greet(round_x, line["x"])

    def place(a):
        order = STATE_ORDERS[a]
        bytes_of(state[a].at[pl.ds(0, 3)], s_send.at[a], s_recv.at[a]).wait_recv()
        units = {"x": 16, "z": 4, "y": 1}
        spot = iota((16 * UNIT, GROUP), 0)
        target = (
            (spot // 64) * (units[order[1]] * UNIT)
            + (spot // 16) % 4 * (units[order[2]] * UNIT)
            + spot % 16
            + at[order[0]] * (units[order[0]] * UNIT)
        ).astype(F32)
        hits = []
        for k in range(4):
            source = chip + (k - at[order[0]]) * units[order[0]]
            hits.append(onehot(rooted[pl.ds(source, 1), :] == target))
        hits = jnp.concatenate(hits, axis=1)
        whole = state[a][...].reshape(4 * GROUP, 128)
        if a:
            split = whole
        else:
            high = whole.astype(BF16)
            rest = whole - high.astype(F32)
            middle = rest.astype(BF16)
            low = (rest - middle.astype(F32)).astype(BF16)
            split = jnp.concatenate([high, middle, low], axis=1)
        moved = jnp.dot(hits, split, preferred_element_type=F32)
        if not a:
            moved = (moved[:, :128] + moved[:, 128:256]) + moved[:, 256:]
        state1[a][...] = moved.astype(state1[a].dtype).reshape(state1[a].shape)

    def state_phase(phase, source, target):
        for a, order in enumerate(STATE_ORDERS):
            axis = order[phase]
            n = phase * 3 + a
            for k in (1, 2, 3):
                copy(
                    source[a].at[(at[axis] + k) % 4], target[a].at[k - 1],
                    s_send.at[n], s_recv.at[n], along(axis, k),
                ).start()

    def state_bytes(phase, target, a):
        n = phase * 3 + a
        return bytes_of(target[a], s_send.at[n], s_recv.at[n])

    def state_sum(phase, source, target, total):
        for a in range(3):
            state_bytes(phase, target, a).wait_recv()
        for a, order in enumerate(STATE_ORDERS):
            value = source[a][at[order[phase]]].astype(F32)
            for k in range(3):
                value = value + target[a][k].astype(F32)
            total[a][...] = value.astype(total[a].dtype)

    lax.fori_loop(chunks // 4, chunks // 2, pack, 0)

    for s in range(3):
        arrive(0, s)
    spread(1)
    for s in range(3):
        forward(0, s)

    for a in range(3):
        place(a)
    state_phase(1, state1, sgot2)

    lax.fori_loop(chunks // 2, chunks, pack, 0)

    for h in range(2):
        packed[h] = (
            acc[:, h * 128 : (h + 1) * 128].astype(BF16).reshape(packed.shape[1:])
        )
    swap = copy(packed.at[1 - c], from_core, core_send, core_recv, sibling)
    swap.start()

    pl.semaphore_wait(round_x, 3)

    swap.wait_recv()
    part[...] = (packed[c].astype(F32) + from_core[...].astype(F32)).astype(BF16)

    def scatter(k):
        other, peer = far(k)
        return copy(part.at[other], got.at[k - 1], rs_send, rs_recv, peer)

    each(lambda k: scatter(k).start())
    own = packed[c, chip].astype(F32) + from_core[chip].astype(F32)

    state_sum(1, state1, sgot2, state2)
    state_phase(2, state2, sgot3)

    for s in range(3):
        arrive(1, s)
    spread(2)
    for s in range(3):
        forward(1, s)

    column[...] = jnp.transpose(jnp.broadcast_to(chip_ranks, (GROUP, GROUP)))
    half = column[own_rows, :]
    for k in range(keep_n // GROUP):
        lanes = (iota((64, GROUP), 1) + k * GROUP).astype(F32)
        expand[:, k * GROUP : (k + 1) * GROUP] = onehot(half == lanes)

    lax.fori_loop(0, chunks // 2, settle, 0)
    state_sum(2, state2, sgot3, state3)
    scattered = bytes_of(got, rs_send, rs_recv)
    scattered.wait_recv()
    summed = (own + jnp.sum(got[...].astype(F32), axis=0)).astype(BF16)
    new_master, _, _ = adamw(*(ref[...].astype(F32) for ref in state3), summed.astype(F32))
    result[c, chip, 0] = summed
    result[c, chip, 1] = new_master.astype(BF16)

    plane = chips // 4

    def gather(k):
        unit = result.at[c, chip]
        return copy(unit, unit, ag_send, ag_recv.at[x], far(k)[1])

    def pass_on(q):
        block = result.at[c, pl.ds(q * plane, plane)]
        return copy(block, block, half_send, half_recv, sibling)

    each(lambda k: gather(k).start())
    spread(3)
    for s in range(3):
        arrive(2, s)
        forward(2, s)
    lax.fori_loop(chunks // 2, chunks, settle, 0)

    for k in (3, 2, 1):
        q = (x + k) % 4
        block = result.at[c, pl.ds(q * plane, plane)]
        bytes_of(block, ag_send, ag_recv.at[q]).wait_recv()
        pass_on(q).start()
    bytes_of(result.at[c, pl.ds(0, plane - 1)], ag_send, ag_recv.at[x]).wait_recv()
    pass_on(x).start()

    for s in range(3):
        arrive(3, s)
        forward(3, s)

    scattered.wait_send()
    bytes_of(result.at[c, pl.ds(0, chips - 1)], ag_send, ag_recv.at[x]).wait_send()
    for go in raw_swaps:
        go.wait_send()
    swap.wait_send()
    own_forward.wait()
    for a in range(3):
        bytes_of(state[a].at[pl.ds(0, 3)], s_send.at[a], s_recv.at[a]).wait_send()
        state_bytes(1, sgot2, a).wait_send()
        state_bytes(2, sgot3, a).wait_send()
    for stage in range(4):
        for s in range(3):
            triple(s, stage, w_send, w_recv).wait_send()
            triple(s, stage, f_send, f_recv).wait()
    bytes_of(result.at[c], half_send, half_recv).wait()


def finish_kernel(
    err, weights, result, expand, rooted, starts_v, master, first, second,
    err_hbm, out_hbm, new_master, new_first, new_second,
    out, starts, err_sem, out_sem, starts_sem,
):
    groups = rooted.shape[0]
    to_smem = pltpu.make_async_copy(starts_v, starts, starts_sem)
    to_smem.start()
    rows = err.shape[1]
    pieces = err_sem.shape[0]
    copies = []
    for i in range(pieces):
        span = pl.ds(i * (rows // pieces), rows // pieces)
        go = pltpu.make_async_copy(err.at[0, span], err_hbm.at[0, span], err_sem.at[i])
        go.start()
        copies.append(go)

    total = jnp.concatenate(
        [
            jnp.dot(
                expand[...], result[h, :, 0].reshape(-1, 128),
                preferred_element_type=F32,
            )
            for h in range(2)
        ],
        axis=1,
    )
    new_master[...], new_first[...], new_second[...] = adamw(
        master[...], first[...], second[...], total
    )

    to_smem.wait()
    units = result.shape[1]
    window = GROUP // UNIT + 1
    batch = groups // out_sem.shape[0]

    def store(i):
        span = pl.ds(i * batch, batch)
        return pltpu.make_async_copy(out.at[span], out_hbm.at[span], out_sem.at[i])

    def fill(i, _):
        for j in range(batch):
            g = i * batch + j
            unit = jnp.minimum(starts[g, 0] // UNIT, units - window)
            near = rooted[pl.ds(g, 1), :] - (unit * UNIT).astype(F32)
            hits = onehot(iota((window * UNIT, GROUP), 0).astype(F32) == near)
            held = [
                result[h, pl.ds(unit, window), 1].reshape(window * UNIT, 128)
                for h in range(2)
            ]
            held = jnp.concatenate([*held, jnp.ones_like(held[0])], axis=1)
            moved = lax.dot_general(
                hits, held, (((0,), (0,)), ((), ())), preferred_element_type=F32
            )
            for c in range(2):
                span = slice(c * 64, c * 64 + 64)
                reached = moved[span, 256:] > 0.5
                for h in range(2):
                    lanes = slice(h * 128, h * 128 + 128)
                    before = weights[g, c, h].astype(F32)
                    out[g, span, lanes] = jnp.where(
                        reached, moved[span, lanes], before
                    ).astype(BF16)
        store(i).start()
        return 0

    steps = out_sem.shape[0]
    lax.fori_loop(0, steps, fill, 0)
    for go in copies:
        go.wait()
    lax.fori_loop(0, steps, lambda i, _: (store(i).wait(), 0)[1], 0)


def body(gradients, error_memory, block_lists, master, first_moment, second_moment):
    _, rows, width = gradients.shape
    owned = master.shape[0]
    levels, keep_n = block_lists.shape[1:]
    groups = rows // GROUP
    chunks = rows // CHUNK
    vmem = pl.BlockSpec(memory_space=pltpu.VMEM)
    anywhere = pl.BlockSpec(memory_space=pl.ANY)
    dma = pltpu.SemaphoreType.DMA

    err, weights, result, expand, rooted, starts = pl.pallas_call(
        merge_kernel,
        out_shape=(
            pltpu.VMEM((1, rows, width), F32),
            pltpu.VMEM((4, 4, 4, 2, 2, owned, 128), BF16),
            pltpu.VMEM((2, groups, 2, UNIT, 128), BF16),
            pltpu.VMEM((owned, keep_n), BF16),
            pltpu.VMEM((groups, GROUP), F32),
            pltpu.VMEM((groups, GROUP), jnp.int32),
        ),
        in_specs=[anywhere] * 6,
        out_specs=(vmem,) * 6,
        scratch_shapes=[
            pltpu.VMEM((rows, width), BF16),
            pltpu.VMEM((levels, keep_n), jnp.int32),
            pltpu.VMEM((2, 3, owned, 128), F32),
            pltpu.VMEM((2, 2, owned, 128), BF16),
            pltpu.VMEM((keep_n, width), F32),
            pltpu.VMEM((groups, GROUP), F32),
            pltpu.VMEM((groups, GROUP), F32),
            pltpu.VMEM((GROUP, GROUP), F32),
            pltpu.VMEM((CHUNK, width), BF16),
            pltpu.VMEM((2, groups, UNIT, 128), BF16),
            pltpu.VMEM((groups, UNIT, 128), BF16),
            pltpu.VMEM((groups, UNIT, 128), BF16),
            pltpu.VMEM((groups - 1, UNIT, 128), BF16),
            *(
                pltpu.VMEM((*lead, *shape, 128), kind)
                for lead, kind in (((), F32), ((2,), BF16))
                for shape in (
                    (4, GROUP), (4, 4, UNIT), (4, UNIT), (UNIT,),
                    (3, 4, UNIT), (3, UNIT),
                )
            ),
            dma((chunks,)), dma((chunks,)), dma, dma,
            dma, dma, dma, dma, dma((2,)), dma((2,)),
            dma, dma, dma, dma((4,)), dma, dma,
            dma((9,)), dma((9,)),
            dma((12,)), dma((12,)),
            dma((13,)), dma((13,)),
            pltpu.SemaphoreType.REGULAR, pltpu.SemaphoreType.REGULAR,
        ],
        compiler_params=pltpu.CompilerParams(
            collective_id=0, has_side_effects=True, vmem_limit_bytes=46 * MIB
        ),
        name="merge",
    )(gradients, error_memory, block_lists, master, first_moment, second_moment)

    new_errors, out, new_master, new_first, new_second = pl.pallas_call(
        finish_kernel,
        out_shape=(
            jax.ShapeDtypeStruct((1, rows, width), F32),
            jax.ShapeDtypeStruct((groups, GROUP, width), BF16),
            jax.ShapeDtypeStruct((owned, width), F32),
            jax.ShapeDtypeStruct((owned, width), F32),
            jax.ShapeDtypeStruct((owned, width), F32),
        ),
        in_specs=[vmem] * 9,
        out_specs=(anywhere, anywhere, vmem, vmem, vmem),
        scratch_shapes=[
            pltpu.VMEM((groups, GROUP, width), BF16),
            pltpu.SMEM((groups, GROUP), jnp.int32),
            dma((4,)), dma((8,)), dma,
        ],
        compiler_params=pltpu.CompilerParams(vmem_limit_bytes=32 * MIB),
        name="finish",
    )(
        err, weights.reshape(groups, 2, 2, owned, 128), result, expand, rooted, starts,
        master, first_moment, second_moment,
    )
    return new_errors, new_master, new_first, new_second, out.reshape(rows, width)


def solution(mesh):
    in_specs = (
        P("dp", None, None),
        P("dp", None, None),
        P("dp", None, None),
        P("dp", None),
        P("dp", None),
        P("dp", None),
    )
    out_specs = (P("dp", None, None), P("dp", None), P("dp", None), P("dp", None), P())
    return jax.shard_map(
        body, mesh=mesh, in_specs=in_specs, out_specs=out_specs, check_vma=False
    )
```

```python
import jax
import jax.numpy as jnp
from jax import lax
from jax.experimental import pallas as pl
from jax.experimental.pallas import tpu as pltpu
from jax.sharding import PartitionSpec as P

FIRST_BIAS = 0.9999734386011124
SECOND_BIAS = 0.09520785288629036
MESH = pl.DeviceIdType.MESH
F32 = jnp.float32
BF16 = jnp.bfloat16
MIB = 1 << 20

GROUP = 128
CHUNK = 1024
UNIT = 16
SPAN = 256

ORDERS = ("xzy", "zyx", "yxz")
STATE_ORDERS = ("zyx", "xzy", "yxz")


def iota(shape, dim):
    return lax.broadcasted_iota(jnp.int32, shape, dim)


def onehot(hits):
    return jnp.where(hits, 1.0, 0.0).astype(BF16)


def adamw(master, first, second, summed):
    new_first = 0.9 * first + 0.1 * summed
    new_second = 0.999 * second + 0.001 * summed * summed
    first_hat = new_first / FIRST_BIAS
    second_hat = new_second / SECOND_BIAS
    new_master = master - 0.001 * (
        first_hat / (jnp.sqrt(second_hat) + 1e-08) + 0.1 * master
    )
    return new_master, new_first, new_second


def merge_kernel(
    grad_hbm, err_hbm, lists_hbm, master_hbm, first_hbm, second_hbm,
    err, weights, result, expand, rooted, starts,
    grad, lists, raw, raw_b, acc, sent, kept, column, value_b,
    packed, from_core, part, got,
    master0, master1, master2, master3, mgot2, mgot3,
    moment0, moment1, moment2, moment3, vgot2, vgot3,
    grad_sem, err_sem, list_sem, raw_sem,
    core_send, core_recv, raw_send, raw_recv, rawb_send, rawb_recv,
    rs_send, rs_recv, ag_send, ag_recv, half_send, half_recv,
    s_send, s_recv, w_send, w_recv, f_send, f_recv, round_z, round_x,
):
    rows = grad.shape[0]
    groups = rows // GROUP
    chunks = rows // CHUNK
    levels, keep_n = lists.shape
    me = lax.axis_index("dp")
    c = me % 2
    y = (me // 2) % 4
    z = (me // 8) % 4
    x = me // 32
    chip = me // 2
    chips = groups
    sibling = me + 1 - 2 * c
    at = {"x": x, "z": z, "y": y}
    strides = {"x": 32, "z": 8, "y": 2}

    def far(k):
        other = (chip + k) % chips
        return other, 2 * other + c

    def along(axis, k):
        return me + ((at[axis] + k) % 4 - at[axis]) * strides[axis]

    def copy(src, dst, send, recv, peer):
        return pltpu.make_async_remote_copy(
            src_ref=src, dst_ref=dst, send_sem=send, recv_sem=recv,
            device_id=(peer,), device_id_type=MESH,
        )

    def each(act):
        def nine(i, _):
            for j in range(9):
                act(i * 9 + j + 1)
            return 0

        lax.fori_loop(0, (chips - 1) // 9, nine, 0)

    def bytes_of(ref, send, recv):
        return copy(ref, ref, send, recv, sibling)

    def three(master_ref, moments_ref):
        return master_ref, moments_ref.at[0], moments_ref.at[1]

    state = three(master0, moment0)
    state1 = three(master1, moment1)
    state2 = three(master2, moment2)
    state3 = three(master3, moment3)
    sgot2 = three(mgot2, vgot2)
    sgot3 = three(mgot3, vgot3)

    def greet(semaphore, peers):
        for peer in peers:
            pl.semaphore_signal(
                semaphore, inc=1, device_id=(peer,), device_id_type=MESH
            )

    line = {axis: [along(axis, k) for k in (1, 2, 3)] for axis in "xzy"}
    barrier = pltpu.get_barrier_semaphore()
    greet(barrier, [sibling, *line["y"], *line["z"], *line["x"]])

    list_load = pltpu.make_async_copy(lists_hbm.at[0], lists, list_sem)
    list_load.start()
    for a, source in enumerate((master_hbm, first_hbm, second_hbm)):
        for h in range(2):
            go = pltpu.make_async_copy(
                source.at[:, pl.ds(h * 128, 128)], raw.at[h, a], raw_sem
            )
            go.start()

    def loads(i):
        span = pl.ds(pl.multiple_of(i * CHUNK, CHUNK), CHUNK)
        return (
            pltpu.make_async_copy(grad_hbm.at[0, span], grad.at[span], grad_sem.at[i]),
            pltpu.make_async_copy(err_hbm.at[0, span], err.at[0, span], err_sem.at[i]),
        )

    def load(i, _):
        for go in loads(i):
            go.start()
        return 0

    lax.fori_loop(0, chunks, load, 0)

    own_rows = pl.ds(pl.multiple_of(c * 64, 64), 64)
    pltpu.make_async_copy(raw, raw, raw_sem).wait()
    raw_b[...] = raw[:, 1:].astype(BF16)
    mine_at = [at[order[0]] for order in STATE_ORDERS]
    master0[mine_at[0], own_rows, :] = raw[c, 0]
    for a in (1, 2):
        moment0[a - 1, mine_at[a], own_rows, :] = raw_b[c, a - 1]

    pl.semaphore_wait(barrier, 10)
    greet(round_z, line["z"])

    raw_swaps = [
        copy(
            raw.at[1 - c, 0], state[0].at[mine_at[0], own_rows],
            raw_send, raw_recv, sibling,
        )
    ]
    for a in (1, 2):
        raw_swaps.append(
            copy(
                raw_b.at[1 - c, a - 1], state[a].at[mine_at[a], own_rows],
                rawb_send.at[a - 1], rawb_recv.at[a - 1], sibling,
            )
        )
    for go in raw_swaps:
        go.start()

    parts = (
        ((0,), pl.ds(0, 48)),
        ((1,), pl.ds(0, 48)),
        ((pl.ds(0, 2),), pl.ds(48, 16)),
    )
    pieces = (
        (((0,), pl.ds(0, 16)), ((0,), pl.ds(16, 16)), ((0,), pl.ds(32, 16))),
        (((1,), pl.ds(0, 16)), ((1,), pl.ds(16, 16)), ((1,), pl.ds(32, 16))),
        (((0,), pl.ds(48, 16)), ((1,), pl.ds(48, 16))),
    )

    def streams(stage):
        return range(2 if stage == 4 else 3)

    def region(s, stage, place):
        cols, span = parts[s] if stage < 2 else pieces[s][stage - 2]
        taken = ORDERS[s][: min(stage, 2)]
        index = tuple(pl.ds(0, 4) if axis in taken else place[axis] for axis in "xzy")
        return weights.at[(*index, c, *cols, span)]

    def triple(s, stage, sends, recvs):
        axis = ORDERS[s][min(stage, 2)]
        n = s * 5 + stage
        block = region(s, stage, {**at, axis: pl.ds(0, 3)})
        return bytes_of(block, sends.at[n], recvs.at[n])

    def spread(stage):
        for s in streams(stage):
            order = ORDERS[s]
            block = region(s, stage, at)
            n = s * 5 + stage
            for k in (1, 2, 3):
                copy(
                    block, block, w_send.at[n], w_recv.at[n],
                    along(order[min(stage, 2)], k),
                ).start()

    def arrive(stage):
        for s in streams(stage):
            triple(s, stage, w_send, w_recv).wait_recv()

    def forward(stage):
        for s in streams(stage):
            axis = ORDERS[s][min(stage, 2)]
            n = s * 5 + stage
            for k in (1, 2, 3):
                block = region(s, stage, {**at, axis: (at[axis] + k) % 4})
                copy(block, block, f_send.at[n], f_recv.at[n], sibling).start()

    list_load.wait()

    def member(r):
        ids = lists[r : r + 1, :]
        high = onehot(iota((groups, keep_n), 0) == ids // GROUP)
        low = onehot(iota((GROUP, keep_n), 0) == ids % GROUP)
        return lax.dot_general(
            high, low, (((1,), (1,)), ((), ())), preferred_element_type=F32
        )

    root = member(levels - 1)
    root_b = root.astype(BF16)
    before = onehot(iota((GROUP, GROUP), 0) < iota((GROUP, GROUP), 1))
    inside = jnp.dot(root_b, before, preferred_element_type=F32)
    total = jnp.dot(root_b, jnp.ones((GROUP, GROUP), BF16), preferred_element_type=F32)
    above = onehot(iota((groups, groups), 1) < iota((groups, groups), 0))
    start = jnp.dot(above, total.astype(BF16), preferred_element_type=F32)
    rank = start + inside
    starts[...] = start.astype(jnp.int32)
    rooted[...] = jnp.where(root > 0.5, rank, -1.0)

    chip_ranks = rooted[pl.ds(chip, 1), :]
    column[...] = jnp.transpose(jnp.broadcast_to(chip_ranks, (GROUP, GROUP)))
    half = column[own_rows, :]
    for h in range(2):
        new_master, _, _ = adamw(raw[h, 0], raw[h, 1], raw[h, 2], 0.0)
        weights[x, z, y, c, h] = jnp.where(half < 0.0, new_master, 0.0).astype(BF16)
    spread(0)
    mine = weights.at[x, z, y, c]
    own_forward = copy(mine, mine, f_send.at[15], f_recv.at[15], sibling)
    own_forward.start()

    for go in raw_swaps:
        go.wait_recv()
    for a, order in enumerate(STATE_ORDERS):
        block = state[a].at[mine_at[a]]
        for k in (1, 2, 3):
            copy(
                block, block, s_send.at[a], s_recv.at[a], along(order[0], k)
            ).start()

    keep = member(0)
    sent[...] = keep
    for r in range(1, levels - 1):
        keep = keep * member(r)
    kept[...] = jnp.where(keep * root > 0.5, rank, -1.0)

    acc[...] = jnp.zeros_like(acc)
    diagonal = iota((GROUP, GROUP), 0) == iota((GROUP, GROUP), 1)
    inner = iota((SPAN // 16, 16, GROUP), 0) * 16 + iota((SPAN // 16, 16, GROUP), 1)
    inner = inner.astype(F32).astype(BF16)
    one = jnp.ones((SPAN // 16, 16, GROUP), BF16)
    zero = jnp.zeros((SPAN // 16, 16, GROUP), BF16)

    def pack(i, _):
        for go in loads(i):
            go.wait()
        each_row = []
        for j in range(CHUNK // GROUP):
            g = i * (CHUNK // GROUP) + j
            span = pl.ds(pl.multiple_of(g * GROUP, GROUP), GROUP)
            value = grad[span, :].astype(F32) + err[0, span, :]
            value_b[j * GROUP : (j + 1) * GROUP, :] = value.astype(BF16)
            each_row.append(kept[pl.ds(g, 1), :])
        for q in range(keep_n // SPAN):
            hits = []
            for row in each_row:
                near = jnp.clip(row - q * SPAN, -1.0, SPAN)
                near = jnp.broadcast_to(near, (16, GROUP)).astype(BF16)
                hit = jnp.where(inner == near[None], one, zero)
                hits.append(hit.reshape(SPAN, GROUP))
            acc[q * SPAN : (q + 1) * SPAN, :] += jnp.dot(
                jnp.concatenate(hits, axis=1), value_b[...], preferred_element_type=F32
            )
        return 0

    def settle(i, _):
        for j in range(CHUNK // GROUP):
            g = i * (CHUNK // GROUP) + j
            span = pl.ds(pl.multiple_of(g * GROUP, GROUP), GROUP)
            stays = 1.0 - sent[pl.ds(g, 1), :]
            mask = jnp.dot(
                jnp.where(diagonal, stays, 0.0).astype(BF16),
                jnp.ones((GROUP, err.shape[2]), BF16),
                preferred_element_type=F32,
            )
            err[0, span, :] = (grad[span, :].astype(F32) + err[0, span, :]) * mask
        return 0

    lax.fori_loop(0, chunks // 4, pack, 0)

    pl.semaphore_wait(round_z, 3)
    greet(round_x, line["x"])

    def place(a):
        order = STATE_ORDERS[a]
        bytes_of(state[a].at[pl.ds(0, 3)], s_send.at[a], s_recv.at[a]).wait_recv()
        units = {"x": 16, "z": 4, "y": 1}
        spot = iota((16 * UNIT, GROUP), 0)
        target = (
            (spot // 64) * (units[order[1]] * UNIT)
            + (spot // 16) % 4 * (units[order[2]] * UNIT)
            + spot % 16
            + at[order[0]] * (units[order[0]] * UNIT)
        ).astype(F32)
        hits = []
        for k in range(4):
            source = chip + (k - at[order[0]]) * units[order[0]]
            hits.append(onehot(rooted[pl.ds(source, 1), :] == target))
        hits = jnp.concatenate(hits, axis=1)
        whole = state[a][...].reshape(4 * GROUP, 128)
        if a:
            split = whole
        else:
            high = whole.astype(BF16)
            rest = whole - high.astype(F32)
            middle = rest.astype(BF16)
            low = (rest - middle.astype(F32)).astype(BF16)
            split = jnp.concatenate([high, middle, low], axis=1)
        moved = jnp.dot(hits, split, preferred_element_type=F32)
        if not a:
            moved = (moved[:, :128] + moved[:, 128:256]) + moved[:, 256:]
        state1[a][...] = moved.astype(state1[a].dtype).reshape(state1[a].shape)

    def state_phase(phase, source, target):
        for a, order in enumerate(STATE_ORDERS):
            axis = order[phase]
            n = phase * 3 + a
            for k in (1, 2, 3):
                copy(
                    source[a].at[(at[axis] + k) % 4], target[a].at[k - 1],
                    s_send.at[n], s_recv.at[n], along(axis, k),
                ).start()

    def state_bytes(phase, target, a):
        n = phase * 3 + a
        return bytes_of(target[a], s_send.at[n], s_recv.at[n])

    def state_sum(phase, source, target, total):
        for a in range(3):
            state_bytes(phase, target, a).wait_recv()
        for a, order in enumerate(STATE_ORDERS):
            value = source[a][at[order[phase]]].astype(F32)
            for k in range(3):
                value = value + target[a][k].astype(F32)
            total[a][...] = value.astype(total[a].dtype)

    lax.fori_loop(chunks // 4, chunks // 2, pack, 0)

    arrive(0)
    spread(1)
    forward(0)

    lax.fori_loop(chunks // 2, chunks, pack, 0)

    half_chips = chips // 2
    swaps = []
    for p in range(2):
        ranks = slice(p * keep_n // 2, (p + 1) * keep_n // 2)
        span = pl.ds(p * half_chips, half_chips)
        for h in range(2):
            packed[h, span] = (
                acc[ranks, h * 128 : (h + 1) * 128]
                .astype(BF16)
                .reshape(half_chips, UNIT, 128)
            )
        swap = copy(
            packed.at[1 - c, span], from_core.at[span],
            core_send.at[p], core_recv.at[p], sibling,
        )
        swap.start()
        swaps.append(swap)

    for a in range(3):
        place(a)
    state_phase(1, state1, sgot2)
    pl.semaphore_wait(round_x, 3)


    def scatter(k):
        other, peer = far(k)
        return copy(part.at[other], got.at[k - 1], rs_send, rs_recv, peer)

    for p in range(2):
        swaps[p].wait_recv()
        span = pl.ds(p * half_chips, half_chips)
        part[span] = (packed[c, span].astype(F32) + from_core[span].astype(F32)).astype(
            BF16
        )

    each(lambda k: scatter(k).start())
    own = packed[c, chip].astype(F32) + from_core[chip].astype(F32)

    state_sum(1, state1, sgot2, state2)
    state_phase(2, state2, sgot3)

    arrive(1)
    spread(2)
    spread(3)
    forward(1)

    for k in range(keep_n // GROUP):
        lanes = (iota((64, GROUP), 1) + k * GROUP).astype(F32)
        expand[:, k * GROUP : (k + 1) * GROUP] = onehot(half == lanes)

    state_sum(2, state2, sgot3, state3)
    scattered = bytes_of(got, rs_send, rs_recv)
    scattered.wait_recv()
    summed = (own + jnp.sum(got[...].astype(F32), axis=0)).astype(BF16)
    new_master, _, _ = adamw(*(ref[...].astype(F32) for ref in state3), summed.astype(F32))
    result[c, chip, 0] = summed
    result[c, chip, 1] = new_master.astype(BF16)

    plane = chips // 4

    def gather(k):
        unit = result.at[c, chip]
        return copy(unit, unit, ag_send, ag_recv.at[x], far(k)[1])

    def pass_on(q):
        block = result.at[c, pl.ds(q * plane, plane)]
        return copy(block, block, half_send, half_recv, sibling)

    each(lambda k: gather(k).start())
    spread(4)
    for stage in (2, 3):
        arrive(stage)
        forward(stage)
    lax.fori_loop(0, chunks, settle, 0)

    for k in (3, 2, 1):
        q = (x + k) % 4
        block = result.at[c, pl.ds(q * plane, plane)]
        bytes_of(block, ag_send, ag_recv.at[q]).wait_recv()
        pass_on(q).start()
    bytes_of(result.at[c, pl.ds(0, plane - 1)], ag_send, ag_recv.at[x]).wait_recv()
    pass_on(x).start()

    arrive(4)
    forward(4)

    scattered.wait_send()
    bytes_of(result.at[c, pl.ds(0, chips - 1)], ag_send, ag_recv.at[x]).wait_send()
    for go in raw_swaps:
        go.wait_send()
    for go in swaps:
        go.wait_send()
    own_forward.wait()
    for a in range(3):
        bytes_of(state[a].at[pl.ds(0, 3)], s_send.at[a], s_recv.at[a]).wait_send()
        state_bytes(1, sgot2, a).wait_send()
        state_bytes(2, sgot3, a).wait_send()
    for stage in range(5):
        for s in streams(stage):
            triple(s, stage, w_send, w_recv).wait_send()
            triple(s, stage, f_send, f_recv).wait()
    bytes_of(result.at[c], half_send, half_recv).wait()


def finish_kernel(
    err, weights, result, expand, rooted, starts_v, master, first, second,
    err_hbm, out_hbm, new_master, new_first, new_second,
    out, starts, err_sem, out_sem, starts_sem,
):
    groups = rooted.shape[0]
    to_smem = pltpu.make_async_copy(starts_v, starts, starts_sem)
    to_smem.start()
    rows = err.shape[1]
    pieces = err_sem.shape[0]
    copies = []
    for i in range(pieces):
        span = pl.ds(i * (rows // pieces), rows // pieces)
        go = pltpu.make_async_copy(err.at[0, span], err_hbm.at[0, span], err_sem.at[i])
        go.start()
        copies.append(go)

    to_smem.wait()
    units = result.shape[1]
    window = GROUP // UNIT + 1
    batch = groups // out_sem.shape[0]

    def store(i):
        span = pl.ds(i * batch, batch)
        return pltpu.make_async_copy(out.at[span], out_hbm.at[span], out_sem.at[i])

    def fill(i, _):
        for j in range(batch):
            g = i * batch + j
            unit = jnp.minimum(starts[g, 0] // UNIT, units - window)
            near = rooted[pl.ds(g, 1), :] - (unit * UNIT).astype(F32)
            hits = onehot(iota((window * UNIT, GROUP), 0).astype(F32) == near)
            held = jnp.concatenate(
                [
                    result[h, pl.ds(unit, window), 1].reshape(window * UNIT, 128)
                    for h in range(2)
                ],
                axis=1,
            )
            moved = lax.dot_general(
                hits, held, (((0,), (0,)), ((), ())), preferred_element_type=F32
            ).astype(BF16)
            for c in range(2):
                span = slice(c * 64, c * 64 + 64)
                for h in range(2):
                    lanes = slice(h * 128, h * 128 + 128)
                    out[g, span, lanes] = weights[g, c, h] + moved[span, lanes]
        store(i).start()
        return 0

    steps = out_sem.shape[0]
    lax.fori_loop(0, steps, fill, 0)
    total = jnp.concatenate(
        [
            jnp.dot(
                expand[...], result[h, :, 0].reshape(-1, 128),
                preferred_element_type=F32,
            )
            for h in range(2)
        ],
        axis=1,
    )
    new_master[...], new_first[...], new_second[...] = adamw(
        master[...], first[...], second[...], total
    )

    for go in copies:
        go.wait()
    lax.fori_loop(0, steps, lambda i, _: (store(i).wait(), 0)[1], 0)


def body(gradients, error_memory, block_lists, master, first_moment, second_moment):
    _, rows, width = gradients.shape
    owned = master.shape[0]
    levels, keep_n = block_lists.shape[1:]
    groups = rows // GROUP
    chunks = rows // CHUNK
    vmem = pl.BlockSpec(memory_space=pltpu.VMEM)
    anywhere = pl.BlockSpec(memory_space=pl.ANY)
    dma = pltpu.SemaphoreType.DMA

    err, weights, result, expand, rooted, starts = pl.pallas_call(
        merge_kernel,
        out_shape=(
            pltpu.VMEM((1, rows, width), F32),
            pltpu.VMEM((4, 4, 4, 2, 2, owned, 128), BF16),
            pltpu.VMEM((2, groups, 2, UNIT, 128), BF16),
            pltpu.VMEM((owned, keep_n), BF16),
            pltpu.VMEM((groups, GROUP), F32),
            pltpu.VMEM((groups, GROUP), jnp.int32),
        ),
        in_specs=[anywhere] * 6,
        out_specs=(vmem,) * 6,
        scratch_shapes=[
            pltpu.VMEM((rows, width), BF16),
            pltpu.VMEM((levels, keep_n), jnp.int32),
            pltpu.VMEM((2, 3, owned, 128), F32),
            pltpu.VMEM((2, 2, owned, 128), BF16),
            pltpu.VMEM((keep_n, width), F32),
            pltpu.VMEM((groups, GROUP), F32),
            pltpu.VMEM((groups, GROUP), F32),
            pltpu.VMEM((GROUP, GROUP), F32),
            pltpu.VMEM((CHUNK, width), BF16),
            pltpu.VMEM((2, groups, UNIT, 128), BF16),
            pltpu.VMEM((groups, UNIT, 128), BF16),
            pltpu.VMEM((groups, UNIT, 128), BF16),
            pltpu.VMEM((groups - 1, UNIT, 128), BF16),
            *(
                pltpu.VMEM((*lead, *shape, 128), kind)
                for lead, kind in (((), F32), ((2,), BF16))
                for shape in (
                    (4, GROUP), (4, 4, UNIT), (4, UNIT), (UNIT,),
                    (3, 4, UNIT), (3, UNIT),
                )
            ),
            dma((chunks,)), dma((chunks,)), dma, dma,
            dma((2,)), dma((2,)), dma, dma, dma((2,)), dma((2,)),
            dma, dma, dma, dma((4,)), dma, dma,
            dma((9,)), dma((9,)),
            dma((15,)), dma((15,)),
            dma((16,)), dma((16,)),
            pltpu.SemaphoreType.REGULAR, pltpu.SemaphoreType.REGULAR,
        ],
        compiler_params=pltpu.CompilerParams(
            collective_id=0, has_side_effects=True, vmem_limit_bytes=46 * MIB
        ),
        name="merge",
    )(gradients, error_memory, block_lists, master, first_moment, second_moment)

    new_errors, out, new_master, new_first, new_second = pl.pallas_call(
        finish_kernel,
        out_shape=(
            jax.ShapeDtypeStruct((1, rows, width), F32),
            jax.ShapeDtypeStruct((groups, GROUP, width), BF16),
            jax.ShapeDtypeStruct((owned, width), F32),
            jax.ShapeDtypeStruct((owned, width), F32),
            jax.ShapeDtypeStruct((owned, width), F32),
        ),
        in_specs=[vmem] * 9,
        out_specs=(anywhere, anywhere, vmem, vmem, vmem),
        scratch_shapes=[
            pltpu.VMEM((groups, GROUP, width), BF16),
            pltpu.SMEM((groups, GROUP), jnp.int32),
            dma((4,)), dma((8,)), dma,
        ],
        compiler_params=pltpu.CompilerParams(vmem_limit_bytes=32 * MIB),
        name="finish",
    )(
        err, weights.reshape(groups, 2, 2, owned, 128), result, expand, rooted, starts,
        master, first_moment, second_moment,
    )
    return new_errors, new_master, new_first, new_second, out.reshape(rows, width)


def solution(mesh):
    in_specs = (
        P("dp", None, None),
        P("dp", None, None),
        P("dp", None, None),
        P("dp", None),
        P("dp", None),
        P("dp", None),
    )
    out_specs = (P("dp", None, None), P("dp", None), P("dp", None), P("dp", None), P())
    return jax.shard_map(
        body, mesh=mesh, in_specs=in_specs, out_specs=out_specs, check_vma=False
    )
```

```python
import jax
import jax.numpy as jnp
from jax import lax
from jax.experimental import pallas as pl
from jax.experimental.pallas import tpu as pltpu
from jax.sharding import PartitionSpec as P

FIRST_BIAS = 0.9999734386011124
SECOND_BIAS = 0.09520785288629036
MESH = pl.DeviceIdType.MESH
F32 = jnp.float32
BF16 = jnp.bfloat16
MIB = 1 << 20

GROUP = 128
CHUNK = 1024
UNIT = 16
SPAN = 256

ORDERS = ("xzy", "zyx", "yxz")
STATE_ORDERS = ("zyx", "xzy", "yxz")


def iota(shape, dim):
    return lax.broadcasted_iota(jnp.int32, shape, dim)


def onehot(hits):
    return jnp.where(hits, 1.0, 0.0).astype(BF16)


def adamw(master, first, second, summed):
    new_first = 0.9 * first + 0.1 * summed
    new_second = 0.999 * second + 0.001 * summed * summed
    first_hat = new_first / FIRST_BIAS
    second_hat = new_second / SECOND_BIAS
    new_master = master - 0.001 * (
        first_hat / (jnp.sqrt(second_hat) + 1e-08) + 0.1 * master
    )
    return new_master, new_first, new_second


def merge_kernel(
    grad_hbm, err_hbm, lists_hbm, master_hbm, first_hbm, second_hbm,
    err, weights, result, expand, rooted, starts,
    grad, lists, raw, raw_b, acc, sent, kept, column, value_b,
    packed, from_core, part, got,
    master0, master1, master2, master3, mgot2, mgot3,
    moment0, moment1, moment2, moment3, vgot2, vgot3,
    grad_sem, err_sem, list_sem, raw_sem,
    core_send, core_recv, raw_send, raw_recv, rawb_send, rawb_recv,
    rs_send, rs_recv, ag_send, ag_recv, half_send, half_recv,
    s_send, s_recv, w_send, w_recv, f_send, f_recv, round_z, round_x,
):
    rows = grad.shape[0]
    groups = rows // GROUP
    chunks = rows // CHUNK
    levels, keep_n = lists.shape
    me = lax.axis_index("dp")
    c = me % 2
    y = (me // 2) % 4
    z = (me // 8) % 4
    x = me // 32
    chip = me // 2
    chips = groups
    sibling = me + 1 - 2 * c
    at = {"x": x, "z": z, "y": y}
    strides = {"x": 32, "z": 8, "y": 2}

    def far(k):
        other = (chip + k) % chips
        return other, 2 * other + c

    def along(axis, k):
        return me + ((at[axis] + k) % 4 - at[axis]) * strides[axis]

    def copy(src, dst, send, recv, peer):
        return pltpu.make_async_remote_copy(
            src_ref=src, dst_ref=dst, send_sem=send, recv_sem=recv,
            device_id=(peer,), device_id_type=MESH,
        )

    def each(act):
        def some(i, _):
            for j in range(21):
                act(i * 21 + j + 1)
            return 0

        lax.fori_loop(0, (chips - 1) // 21, some, 0)

    def bytes_of(ref, send, recv):
        return copy(ref, ref, send, recv, sibling)

    def three(master_ref, moments_ref):
        return master_ref, moments_ref.at[0], moments_ref.at[1]

    state = three(master0, moment0)
    state1 = three(master1, moment1)
    state2 = three(master2, moment2)
    state3 = three(master3, moment3)
    sgot2 = three(mgot2, vgot2)
    sgot3 = three(mgot3, vgot3)

    def greet(semaphore, peers):
        for peer in peers:
            pl.semaphore_signal(
                semaphore, inc=1, device_id=(peer,), device_id_type=MESH
            )

    line = {axis: [along(axis, k) for k in (1, 2, 3)] for axis in "xzy"}
    barrier = pltpu.get_barrier_semaphore()
    greet(barrier, [sibling, *line["y"], *line["z"], *line["x"]])

    list_load = pltpu.make_async_copy(lists_hbm.at[0], lists, list_sem)
    list_load.start()
    for a, source in enumerate((master_hbm, first_hbm, second_hbm)):
        for h in range(2):
            go = pltpu.make_async_copy(
                source.at[:, pl.ds(h * 128, 128)], raw.at[h, a], raw_sem
            )
            go.start()

    def loads(i):
        span = pl.ds(pl.multiple_of(i * CHUNK, CHUNK), CHUNK)
        return (
            pltpu.make_async_copy(grad_hbm.at[0, span], grad.at[span], grad_sem.at[i]),
            pltpu.make_async_copy(err_hbm.at[0, span], err.at[0, span], err_sem.at[i]),
        )

    def load(i, _):
        for go in loads(i):
            go.start()
        return 0

    lax.fori_loop(0, chunks, load, 0)

    own_rows = pl.ds(pl.multiple_of(c * 64, 64), 64)
    pltpu.make_async_copy(raw, raw, raw_sem).wait()
    raw_b[...] = raw[:, 1:].astype(BF16)
    mine_at = [at[order[0]] for order in STATE_ORDERS]
    master0[mine_at[0], own_rows, :] = raw[c, 0]
    for a in (1, 2):
        moment0[a - 1, mine_at[a], own_rows, :] = raw_b[c, a - 1]

    pl.semaphore_wait(barrier, 10)
    greet(round_z, line["z"])

    raw_swaps = [
        copy(
            raw.at[1 - c, 0], state[0].at[mine_at[0], own_rows],
            raw_send, raw_recv, sibling,
        )
    ]
    for a in (1, 2):
        raw_swaps.append(
            copy(
                raw_b.at[1 - c, a - 1], state[a].at[mine_at[a], own_rows],
                rawb_send.at[a - 1], rawb_recv.at[a - 1], sibling,
            )
        )
    for go in raw_swaps:
        go.start()

    parts = (
        ((0,), pl.ds(0, 48)),
        ((1,), pl.ds(0, 48)),
        ((pl.ds(0, 2),), pl.ds(48, 16)),
    )
    pieces = (
        (((0,), pl.ds(0, 16)), ((0,), pl.ds(16, 16)), ((0,), pl.ds(32, 16))),
        (((1,), pl.ds(0, 16)), ((1,), pl.ds(16, 16)), ((1,), pl.ds(32, 16))),
        (((0,), pl.ds(48, 16)), ((1,), pl.ds(48, 16))),
    )

    def streams(stage):
        return range(2 if stage == 4 else 3)

    def region(s, stage, place):
        cols, span = parts[s] if stage < 2 else pieces[s][stage - 2]
        taken = ORDERS[s][: min(stage, 2)]
        index = tuple(pl.ds(0, 4) if axis in taken else place[axis] for axis in "xzy")
        return weights.at[(*index, c, *cols, span)]

    def triple(s, stage, sends, recvs):
        axis = ORDERS[s][min(stage, 2)]
        n = s * 5 + stage
        block = region(s, stage, {**at, axis: pl.ds(0, 3)})
        return bytes_of(block, sends.at[n], recvs.at[n])

    def spread(stage):
        for s in streams(stage):
            order = ORDERS[s]
            block = region(s, stage, at)
            n = s * 5 + stage
            for k in (1, 2, 3):
                copy(
                    block, block, w_send.at[n], w_recv.at[n],
                    along(order[min(stage, 2)], k),
                ).start()

    def arrive(stage):
        for s in streams(stage):
            triple(s, stage, w_send, w_recv).wait_recv()

    def forward(stage):
        for s in streams(stage):
            axis = ORDERS[s][min(stage, 2)]
            n = s * 5 + stage
            for k in (1, 2, 3):
                block = region(s, stage, {**at, axis: (at[axis] + k) % 4})
                copy(block, block, f_send.at[n], f_recv.at[n], sibling).start()

    list_load.wait()

    ids = lists[...]
    high_ids = (ids >> 7).astype(F32)
    low_ids = (ids & 127).astype(F32)

    inner = iota((SPAN // 16, 16, GROUP), 0) * 16 + iota((SPAN // 16, 16, GROUP), 1)
    inner = inner.astype(F32).astype(BF16)
    one = jnp.ones((SPAN // 16, 16, GROUP), BF16)
    zero = jnp.zeros((SPAN // 16, 16, GROUP), BF16)

    def ladder(row, count):
        tiles = count // 16
        near = jnp.broadcast_to(row, (16, GROUP)).astype(BF16)
        hit = jnp.where(inner[:tiles] == near[None], one[:tiles], zero[:tiles])
        return hit.reshape(count, GROUP)

    def member(r):
        spans = [slice(j, j + GROUP) for j in range(0, keep_n, GROUP)]
        high = [ladder(high_ids[r : r + 1, span], groups) for span in spans]
        low = [ladder(low_ids[r : r + 1, span], GROUP) for span in spans]
        return lax.dot_general(
            jnp.concatenate(high, axis=1), jnp.concatenate(low, axis=1),
            (((1,), (1,)), ((), ())), preferred_element_type=F32,
        )

    root = member(levels - 1)
    root_b = root.astype(BF16)
    before = onehot(iota((GROUP, GROUP), 0) < iota((GROUP, GROUP), 1))
    inside = jnp.dot(root_b, before, preferred_element_type=F32)
    total = jnp.dot(root_b, jnp.ones((GROUP, GROUP), BF16), preferred_element_type=F32)
    above = onehot(iota((groups, groups), 1) < iota((groups, groups), 0))
    start = jnp.dot(above, total.astype(BF16), preferred_element_type=F32)
    rank = start + inside
    starts[...] = start.astype(jnp.int32)
    rooted[...] = jnp.where(root > 0.5, rank, -1.0)

    chip_ranks = rooted[pl.ds(chip, 1), :]
    column[...] = jnp.transpose(jnp.broadcast_to(chip_ranks, (GROUP, GROUP)))
    half = column[own_rows, :]
    for h in range(2):
        new_master, _, _ = adamw(raw[h, 0], raw[h, 1], raw[h, 2], 0.0)
        weights[x, z, y, c, h] = jnp.where(half < 0.0, new_master, 0.0).astype(BF16)
    spread(0)
    mine = weights.at[x, z, y, c]
    own_forward = copy(mine, mine, f_send.at[15], f_recv.at[15], sibling)
    own_forward.start()

    for go in raw_swaps:
        go.wait_recv()
    for a, order in enumerate(STATE_ORDERS):
        block = state[a].at[mine_at[a]]
        for k in (1, 2, 3):
            copy(
                block, block, s_send.at[a], s_recv.at[a], along(order[0], k)
            ).start()

    keep = member(0)
    sent[...] = keep
    for r in range(1, levels - 1):
        keep = keep * member(r)
    kept[...] = jnp.where(keep * root > 0.5, rank, -1.0)

    acc[...] = jnp.zeros_like(acc)
    diagonal = iota((GROUP, GROUP), 0) == iota((GROUP, GROUP), 1)

    def pack(i, _):
        for go in loads(i):
            go.wait()
        each_row = []
        for j in range(CHUNK // GROUP):
            g = i * (CHUNK // GROUP) + j
            span = pl.ds(pl.multiple_of(g * GROUP, GROUP), GROUP)
            value = grad[span, :].astype(F32) + err[0, span, :]
            value_b[j * GROUP : (j + 1) * GROUP, :] = value.astype(BF16)
            each_row.append(kept[pl.ds(g, 1), :])
        for q in range(keep_n // SPAN):
            hits = []
            for row in each_row:
                hits.append(ladder(jnp.clip(row - q * SPAN, -1.0, SPAN), SPAN))
            acc[q * SPAN : (q + 1) * SPAN, :] += jnp.dot(
                jnp.concatenate(hits, axis=1), value_b[...], preferred_element_type=F32
            )
        return 0

    def settle(i, _):
        for j in range(CHUNK // GROUP):
            g = i * (CHUNK // GROUP) + j
            span = pl.ds(pl.multiple_of(g * GROUP, GROUP), GROUP)
            stays = 1.0 - sent[pl.ds(g, 1), :]
            mask = jnp.dot(
                jnp.where(diagonal, stays, 0.0).astype(BF16),
                jnp.ones((GROUP, err.shape[2]), BF16),
                preferred_element_type=F32,
            )
            err[0, span, :] = (grad[span, :].astype(F32) + err[0, span, :]) * mask
        return 0

    lax.fori_loop(0, chunks // 4, pack, 0)

    pl.semaphore_wait(round_z, 3)
    greet(round_x, line["x"])

    def place(a):
        order = STATE_ORDERS[a]
        bytes_of(state[a].at[pl.ds(0, 3)], s_send.at[a], s_recv.at[a]).wait_recv()
        units = {"x": 16, "z": 4, "y": 1}
        spot = iota((16 * UNIT, GROUP), 0)
        target = (
            (spot // 64) * (units[order[1]] * UNIT)
            + (spot // 16) % 4 * (units[order[2]] * UNIT)
            + spot % 16
            + at[order[0]] * (units[order[0]] * UNIT)
        ).astype(F32)
        hits = []
        for k in range(4):
            source = chip + (k - at[order[0]]) * units[order[0]]
            hits.append(onehot(rooted[pl.ds(source, 1), :] == target))
        hits = jnp.concatenate(hits, axis=1)
        whole = state[a][...].reshape(4 * GROUP, 128)
        if a:
            split = whole
        else:
            high = whole.astype(BF16)
            rest = whole - high.astype(F32)
            middle = rest.astype(BF16)
            low = (rest - middle.astype(F32)).astype(BF16)
            split = jnp.concatenate([high, middle, low], axis=1)
        moved = jnp.dot(hits, split, preferred_element_type=F32)
        if not a:
            moved = (moved[:, :128] + moved[:, 128:256]) + moved[:, 256:]
        state1[a][...] = moved.astype(state1[a].dtype).reshape(state1[a].shape)

    def state_phase(phase, source, target):
        for a, order in enumerate(STATE_ORDERS):
            axis = order[phase]
            n = phase * 3 + a
            for k in (1, 2, 3):
                copy(
                    source[a].at[(at[axis] + k) % 4], target[a].at[k - 1],
                    s_send.at[n], s_recv.at[n], along(axis, k),
                ).start()

    def state_bytes(phase, target, a):
        n = phase * 3 + a
        return bytes_of(target[a], s_send.at[n], s_recv.at[n])

    def state_sum(phase, source, target, total):
        for a in range(3):
            state_bytes(phase, target, a).wait_recv()
        for a, order in enumerate(STATE_ORDERS):
            value = source[a][at[order[phase]]].astype(F32)
            for k in range(3):
                value = value + target[a][k].astype(F32)
            total[a][...] = value.astype(total[a].dtype)

    lax.fori_loop(chunks // 4, chunks // 2, pack, 0)

    arrive(0)
    spread(1)
    forward(0)

    lax.fori_loop(chunks // 2, chunks, pack, 0)

    half_chips = chips // 2
    swaps = []
    for p in range(2):
        ranks = slice(p * keep_n // 2, (p + 1) * keep_n // 2)
        span = pl.ds(p * half_chips, half_chips)
        for h in range(2):
            packed[h, span] = (
                acc[ranks, h * 128 : (h + 1) * 128]
                .astype(BF16)
                .reshape(half_chips, UNIT, 128)
            )
        swap = copy(
            packed.at[1 - c, span], from_core.at[span],
            core_send.at[p], core_recv.at[p], sibling,
        )
        swap.start()
        swaps.append(swap)

    for a in range(3):
        place(a)
    state_phase(1, state1, sgot2)
    pl.semaphore_wait(round_x, 3)


    def scatter(k):
        other, peer = far(k)
        return copy(part.at[other], got.at[k - 1], rs_send, rs_recv, peer)

    for p in range(2):
        swaps[p].wait_recv()
        span = pl.ds(p * half_chips, half_chips)
        part[span] = (packed[c, span].astype(F32) + from_core[span].astype(F32)).astype(
            BF16
        )

    each(lambda k: scatter(k).start())
    own = packed[c, chip].astype(F32) + from_core[chip].astype(F32)

    state_sum(1, state1, sgot2, state2)
    state_phase(2, state2, sgot3)

    arrive(1)
    spread(2)
    spread(3)
    forward(1)

    for k in range(keep_n // GROUP):
        lanes = (iota((64, GROUP), 1) + k * GROUP).astype(F32)
        expand[:, k * GROUP : (k + 1) * GROUP] = onehot(half == lanes)

    state_sum(2, state2, sgot3, state3)
    scattered = bytes_of(got, rs_send, rs_recv)
    scattered.wait_recv()
    summed = (own + jnp.sum(got[...].astype(F32), axis=0)).astype(BF16)
    new_master, _, _ = adamw(*(ref[...].astype(F32) for ref in state3), summed.astype(F32))
    result[c, chip, 0] = summed
    result[c, chip, 1] = new_master.astype(BF16)

    plane = chips // 4

    def gather(k):
        unit = result.at[c, chip]
        return copy(unit, unit, ag_send, ag_recv.at[x], far(k)[1])

    def pass_on(q):
        block = result.at[c, pl.ds(q * plane, plane)]
        return copy(block, block, half_send, half_recv, sibling)

    each(lambda k: gather(k).start())
    spread(4)
    for stage in (2, 3):
        arrive(stage)
        forward(stage)
    lax.fori_loop(0, chunks, settle, 0)

    for k in (3, 2, 1):
        q = (x + k) % 4
        block = result.at[c, pl.ds(q * plane, plane)]
        bytes_of(block, ag_send, ag_recv.at[q]).wait_recv()
        pass_on(q).start()
    bytes_of(result.at[c, pl.ds(0, plane - 1)], ag_send, ag_recv.at[x]).wait_recv()
    pass_on(x).start()

    arrive(4)
    forward(4)

    scattered.wait_send()
    bytes_of(result.at[c, pl.ds(0, chips - 1)], ag_send, ag_recv.at[x]).wait_send()
    for go in raw_swaps:
        go.wait_send()
    for go in swaps:
        go.wait_send()
    own_forward.wait()
    for a in range(3):
        bytes_of(state[a].at[pl.ds(0, 3)], s_send.at[a], s_recv.at[a]).wait_send()
        state_bytes(1, sgot2, a).wait_send()
        state_bytes(2, sgot3, a).wait_send()
    for stage in range(5):
        for s in streams(stage):
            triple(s, stage, w_send, w_recv).wait_send()
            triple(s, stage, f_send, f_recv).wait()
    bytes_of(result.at[c], half_send, half_recv).wait()


def finish_kernel(
    err, weights, result, expand, rooted, starts_v, master, first, second,
    err_hbm, out_hbm, new_master, new_first, new_second,
    out, starts, err_sem, out_sem, starts_sem,
):
    groups = rooted.shape[0]
    to_smem = pltpu.make_async_copy(starts_v, starts, starts_sem)
    to_smem.start()
    rows = err.shape[1]
    pieces = err_sem.shape[0]
    copies = []
    for i in range(pieces):
        span = pl.ds(i * (rows // pieces), rows // pieces)
        go = pltpu.make_async_copy(err.at[0, span], err_hbm.at[0, span], err_sem.at[i])
        go.start()
        copies.append(go)

    to_smem.wait()
    units = result.shape[1]
    window = GROUP // UNIT + 1
    batch = groups // out_sem.shape[0]

    def store(i):
        span = pl.ds(i * batch, batch)
        return pltpu.make_async_copy(out.at[span], out_hbm.at[span], out_sem.at[i])

    def fill(i, _):
        for j in range(batch):
            g = i * batch + j
            unit = jnp.minimum(starts[g, 0] // UNIT, units - window)
            near = rooted[pl.ds(g, 1), :] - (unit * UNIT).astype(F32)
            hits = onehot(iota((window * UNIT, GROUP), 0).astype(F32) == near)
            held = jnp.concatenate(
                [
                    result[h, pl.ds(unit, window), 1].reshape(window * UNIT, 128)
                    for h in range(2)
                ],
                axis=1,
            )
            moved = lax.dot_general(
                hits, held, (((0,), (0,)), ((), ())), preferred_element_type=F32
            ).astype(BF16)
            for c in range(2):
                span = slice(c * 64, c * 64 + 64)
                for h in range(2):
                    lanes = slice(h * 128, h * 128 + 128)
                    out[g, span, lanes] = weights[g, c, h] + moved[span, lanes]
        store(i).start()
        return 0

    steps = out_sem.shape[0]
    lax.fori_loop(0, steps, fill, 0)
    total = jnp.concatenate(
        [
            jnp.dot(
                expand[...], result[h, :, 0].reshape(-1, 128),
                preferred_element_type=F32,
            )
            for h in range(2)
        ],
        axis=1,
    )
    new_master[...], new_first[...], new_second[...] = adamw(
        master[...], first[...], second[...], total
    )

    for go in copies:
        go.wait()
    lax.fori_loop(0, steps, lambda i, _: (store(i).wait(), 0)[1], 0)


def body(gradients, error_memory, block_lists, master, first_moment, second_moment):
    _, rows, width = gradients.shape
    owned = master.shape[0]
    levels, keep_n = block_lists.shape[1:]
    groups = rows // GROUP
    chunks = rows // CHUNK
    vmem = pl.BlockSpec(memory_space=pltpu.VMEM)
    anywhere = pl.BlockSpec(memory_space=pl.ANY)
    dma = pltpu.SemaphoreType.DMA

    err, weights, result, expand, rooted, starts = pl.pallas_call(
        merge_kernel,
        out_shape=(
            pltpu.VMEM((1, rows, width), F32),
            pltpu.VMEM((4, 4, 4, 2, 2, owned, 128), BF16),
            pltpu.VMEM((2, groups, 2, UNIT, 128), BF16),
            pltpu.VMEM((owned, keep_n), BF16),
            pltpu.VMEM((groups, GROUP), F32),
            pltpu.VMEM((groups, GROUP), jnp.int32),
        ),
        in_specs=[anywhere] * 6,
        out_specs=(vmem,) * 6,
        scratch_shapes=[
            pltpu.VMEM((rows, width), BF16),
            pltpu.VMEM((levels, keep_n), jnp.int32),
            pltpu.VMEM((2, 3, owned, 128), F32),
            pltpu.VMEM((2, 2, owned, 128), BF16),
            pltpu.VMEM((keep_n, width), F32),
            pltpu.VMEM((groups, GROUP), F32),
            pltpu.VMEM((groups, GROUP), F32),
            pltpu.VMEM((GROUP, GROUP), F32),
            pltpu.VMEM((CHUNK, width), BF16),
            pltpu.VMEM((2, groups, UNIT, 128), BF16),
            pltpu.VMEM((groups, UNIT, 128), BF16),
            pltpu.VMEM((groups, UNIT, 128), BF16),
            pltpu.VMEM((groups - 1, UNIT, 128), BF16),
            *(
                pltpu.VMEM((*lead, *shape, 128), kind)
                for lead, kind in (((), F32), ((2,), BF16))
                for shape in (
                    (4, GROUP), (4, 4, UNIT), (4, UNIT), (UNIT,),
                    (3, 4, UNIT), (3, UNIT),
                )
            ),
            dma((chunks,)), dma((chunks,)), dma, dma,
            dma((2,)), dma((2,)), dma, dma, dma((2,)), dma((2,)),
            dma, dma, dma, dma((4,)), dma, dma,
            dma((9,)), dma((9,)),
            dma((15,)), dma((15,)),
            dma((16,)), dma((16,)),
            pltpu.SemaphoreType.REGULAR, pltpu.SemaphoreType.REGULAR,
        ],
        compiler_params=pltpu.CompilerParams(
            collective_id=0, has_side_effects=True, vmem_limit_bytes=46 * MIB
        ),
        name="merge",
    )(gradients, error_memory, block_lists, master, first_moment, second_moment)

    new_errors, out, new_master, new_first, new_second = pl.pallas_call(
        finish_kernel,
        out_shape=(
            jax.ShapeDtypeStruct((1, rows, width), F32),
            jax.ShapeDtypeStruct((groups, GROUP, width), BF16),
            jax.ShapeDtypeStruct((owned, width), F32),
            jax.ShapeDtypeStruct((owned, width), F32),
            jax.ShapeDtypeStruct((owned, width), F32),
        ),
        in_specs=[vmem] * 9,
        out_specs=(anywhere, anywhere, vmem, vmem, vmem),
        scratch_shapes=[
            pltpu.VMEM((groups, GROUP, width), BF16),
            pltpu.SMEM((groups, GROUP), jnp.int32),
            dma((4,)), dma((8,)), dma,
        ],
        compiler_params=pltpu.CompilerParams(vmem_limit_bytes=32 * MIB),
        name="finish",
    )(
        err, weights.reshape(groups, 2, 2, owned, 128), result, expand, rooted, starts,
        master, first_moment, second_moment,
    )
    return new_errors, new_master, new_first, new_second, out.reshape(rows, width)


def solution(mesh):
    in_specs = (
        P("dp", None, None),
        P("dp", None, None),
        P("dp", None, None),
        P("dp", None),
        P("dp", None),
        P("dp", None),
    )
    out_specs = (P("dp", None, None), P("dp", None), P("dp", None), P("dp", None), P())
    return jax.shard_map(
        body, mesh=mesh, in_specs=in_specs, out_specs=out_specs, check_vma=False
    )
```

```python
import jax
import jax.numpy as jnp
from jax import lax
from jax.experimental import pallas as pl
from jax.experimental.pallas import tpu as pltpu
from jax.sharding import PartitionSpec as P

FIRST_BIAS = 0.9999734386011124
SECOND_BIAS = 0.09520785288629036
MESH = pl.DeviceIdType.MESH
F32 = jnp.float32
BF16 = jnp.bfloat16
MIB = 1 << 20

GROUP = 128
CHUNK = 2048
UNIT = 16
SPAN = 256

ORDERS = ("xzy", "zyx", "yxz")
STATE_ORDERS = ("zyx", "xzy", "yxz")


def iota(shape, dim):
    return lax.broadcasted_iota(jnp.int32, shape, dim)


def onehot(hits):
    return jnp.where(hits, 1.0, 0.0).astype(BF16)


def adamw(master, first, second, summed):
    new_first = 0.9 * first + 0.1 * summed
    new_second = 0.999 * second + 0.001 * summed * summed
    first_hat = new_first / FIRST_BIAS
    second_hat = new_second / SECOND_BIAS
    new_master = master - 0.001 * (
        first_hat / (jnp.sqrt(second_hat) + 1e-08) + 0.1 * master
    )
    return new_master, new_first, new_second


def merge_kernel(
    grad_hbm, err_hbm, lists_hbm, master_hbm, first_hbm, second_hbm,
    err, weights, result, expand, rooted, starts,
    grad, lists, raw, raw_b, acc, sent, kept, column, value_b,
    packed, from_core, part, got,
    master0, master1, master2, master3, mgot2, mgot3,
    moment0, moment1, moment2, moment3, vgot2, vgot3,
    grad_sem, err_sem, list_sem, raw_sem,
    core_send, core_recv, raw_send, raw_recv, rawb_send, rawb_recv,
    rs_send, rs_recv, ag_send, ag_recv, half_send, half_recv,
    s_send, s_recv, w_send, w_recv, f_send, f_recv, round_z, round_x,
):
    rows = grad.shape[0]
    groups = rows // GROUP
    chunks = rows // CHUNK
    levels, keep_n = lists.shape
    me = lax.axis_index("dp")
    c = me % 2
    y = (me // 2) % 4
    z = (me // 8) % 4
    x = me // 32
    chip = me // 2
    chips = groups
    sibling = me + 1 - 2 * c
    at = {"x": x, "z": z, "y": y}
    strides = {"x": 32, "z": 8, "y": 2}

    def far(k):
        other = (chip + k) % chips
        return other, 2 * other + c

    def along(axis, k):
        return me + ((at[axis] + k) % 4 - at[axis]) * strides[axis]

    def copy(src, dst, send, recv, peer):
        return pltpu.make_async_remote_copy(
            src_ref=src, dst_ref=dst, send_sem=send, recv_sem=recv,
            device_id=(peer,), device_id_type=MESH,
        )

    def each(act):
        def some(i, _):
            for j in range(21):
                act(i * 21 + j + 1)
            return 0

        lax.fori_loop(0, (chips - 1) // 21, some, 0)

    def bytes_of(ref, send, recv):
        return copy(ref, ref, send, recv, sibling)

    def three(master_ref, moments_ref):
        return master_ref, moments_ref.at[0], moments_ref.at[1]

    state = three(master0, moment0)
    state1 = three(master1, moment1)
    state2 = three(master2, moment2)
    state3 = three(master3, moment3)
    sgot2 = three(mgot2, vgot2)
    sgot3 = three(mgot3, vgot3)

    def greet(semaphore, peers):
        for peer in peers:
            pl.semaphore_signal(
                semaphore, inc=1, device_id=(peer,), device_id_type=MESH
            )

    line = {axis: [along(axis, k) for k in (1, 2, 3)] for axis in "xzy"}
    barrier = pltpu.get_barrier_semaphore()
    greet(barrier, [sibling, *line["y"], *line["z"], *line["x"]])

    list_load = pltpu.make_async_copy(lists_hbm.at[0], lists, list_sem)
    list_load.start()
    for a, source in enumerate((master_hbm, first_hbm, second_hbm)):
        for h in range(2):
            go = pltpu.make_async_copy(
                source.at[:, pl.ds(h * 128, 128)], raw.at[h, a], raw_sem
            )
            go.start()

    def loads(i):
        span = pl.ds(pl.multiple_of(i * CHUNK, CHUNK), CHUNK)
        return (
            pltpu.make_async_copy(grad_hbm.at[0, span], grad.at[span], grad_sem.at[i]),
            pltpu.make_async_copy(err_hbm.at[0, span], err.at[0, span], err_sem.at[i]),
        )

    def load(i, _):
        for go in loads(i):
            go.start()
        return 0

    lax.fori_loop(0, chunks, load, 0)

    parts = (
        ((0,), pl.ds(0, 48)),
        ((1,), pl.ds(0, 48)),
        ((pl.ds(0, 2),), pl.ds(48, 16)),
    )
    pieces = (
        (((0,), pl.ds(0, 16)), ((0,), pl.ds(16, 16)), ((0,), pl.ds(32, 16))),
        (((1,), pl.ds(0, 16)), ((1,), pl.ds(16, 16)), ((1,), pl.ds(32, 16))),
        (((0,), pl.ds(48, 16)), ((1,), pl.ds(48, 16))),
    )

    def streams(stage):
        return range(2 if stage == 4 else 3)

    def region(s, stage, place):
        cols, span = parts[s] if stage < 2 else pieces[s][stage - 2]
        taken = ORDERS[s][: min(stage, 2)]
        index = tuple(pl.ds(0, 4) if axis in taken else place[axis] for axis in "xzy")
        return weights.at[(*index, c, *cols, span)]

    def stage_bytes(stage, sends, recvs):
        three_of = (
            weights.at[0, 0, pl.ds(0, 3), c],
            weights.at[0, pl.ds(0, 3), :, c],
            weights.at[pl.ds(0, 3), :, :, c, 0, pl.ds(0, 48)],
            weights.at[pl.ds(0, 3), :, :, c, 0, pl.ds(0, 48)],
            weights.at[pl.ds(0, 3), :, :, c, 0, pl.ds(0, 32)],
        )
        return bytes_of(three_of[stage], sends.at[stage], recvs.at[stage])

    def spread(stage):
        for s in streams(stage):
            order = ORDERS[s]
            block = region(s, stage, at)
            for k in (1, 2, 3):
                copy(
                    block, block, w_send.at[stage], w_recv.at[stage],
                    along(order[min(stage, 2)], k),
                ).start()

    def arrive(stage):
        stage_bytes(stage, w_send, w_recv).wait_recv()

    def forward(stage):
        for s in streams(stage):
            axis = ORDERS[s][min(stage, 2)]
            for k in (1, 2, 3):
                block = region(s, stage, {**at, axis: (at[axis] + k) % 4})
                copy(block, block, f_send, f_recv, sibling).start()

    list_load.wait()

    ids = lists[...]
    high_ids = (ids >> 7).astype(F32)
    low_ids = (ids & 127).astype(F32)

    inner = iota((SPAN // 16, 16, GROUP), 0) * 16 + iota((SPAN // 16, 16, GROUP), 1)
    inner = inner.astype(F32).astype(BF16)
    one = jnp.ones((SPAN // 16, 16, GROUP), BF16)
    zero = jnp.zeros((SPAN // 16, 16, GROUP), BF16)

    def ladder(row, count):
        tiles = count // 16
        near = jnp.broadcast_to(row, (16, GROUP)).astype(BF16)
        hit = jnp.where(inner[:tiles] == near[None], one[:tiles], zero[:tiles])
        return hit.reshape(count, GROUP)

    def member(r):
        spans = [slice(j, j + GROUP) for j in range(0, keep_n, GROUP)]
        high = [ladder(high_ids[r : r + 1, span], groups) for span in spans]
        low = [ladder(low_ids[r : r + 1, span], GROUP) for span in spans]
        return lax.dot_general(
            jnp.concatenate(high, axis=1), jnp.concatenate(low, axis=1),
            (((1,), (1,)), ((), ())), preferred_element_type=F32,
        )

    root = member(levels - 1)
    root_b = root.astype(BF16)
    before = onehot(iota((GROUP, GROUP), 0) < iota((GROUP, GROUP), 1))
    inside = jnp.dot(root_b, before, preferred_element_type=F32)
    total = jnp.dot(root_b, jnp.ones((GROUP, GROUP), BF16), preferred_element_type=F32)
    above = onehot(iota((groups, groups), 1) < iota((groups, groups), 0))
    start = jnp.dot(above, total.astype(BF16), preferred_element_type=F32)
    rank = start + inside
    starts[...] = start.astype(jnp.int32)
    rooted[...] = jnp.where(root > 0.5, rank, -1.0)

    keep = member(0)
    sent[...] = keep
    for r in range(1, levels - 1):
        keep = keep * member(r)
    kept[...] = jnp.where(keep * root > 0.5, rank, -1.0)

    chip_ranks = rooted[pl.ds(chip, 1), :]
    column[...] = jnp.transpose(jnp.broadcast_to(chip_ranks, (GROUP, GROUP)))
    own_rows = pl.ds(pl.multiple_of(c * 64, 64), 64)
    half = column[own_rows, :]
    pltpu.make_async_copy(raw, raw, raw_sem).wait()
    raw_b[...] = raw[:, 1:].astype(BF16)
    mine_at = [at[order[0]] for order in STATE_ORDERS]
    master0[mine_at[0], own_rows, :] = raw[c, 0]
    for a in (1, 2):
        moment0[a - 1, mine_at[a], own_rows, :] = raw_b[c, a - 1]

    for h in range(2):
        new_master, _, _ = adamw(raw[h, 0], raw[h, 1], raw[h, 2], 0.0)
        weights[x, z, y, c, h] = jnp.where(half < 0.0, new_master, 0.0).astype(BF16)
    acc[...] = jnp.zeros_like(acc)
    diagonal = iota((GROUP, GROUP), 0) == iota((GROUP, GROUP), 1)

    def pack(i):
        for go in loads(i):
            go.wait()
        each_row = []
        for j in range(CHUNK // GROUP):
            g = i * (CHUNK // GROUP) + j
            span = pl.ds(pl.multiple_of(g * GROUP, GROUP), GROUP)
            value = grad[span, :].astype(F32) + err[0, span, :]
            value_b[j * GROUP : (j + 1) * GROUP, :] = value.astype(BF16)
            each_row.append(kept[pl.ds(g, 1), :])
        for q in range(keep_n // SPAN):
            hits = []
            for row in each_row:
                hits.append(ladder(jnp.clip(row - q * SPAN, -1.0, SPAN), SPAN))
            acc[q * SPAN : (q + 1) * SPAN, :] += jnp.dot(
                jnp.concatenate(hits, axis=1), value_b[...], preferred_element_type=F32
            )

    def settle(i, _):
        for j in range(CHUNK // GROUP):
            g = i * (CHUNK // GROUP) + j
            span = pl.ds(pl.multiple_of(g * GROUP, GROUP), GROUP)
            stays = 1.0 - sent[pl.ds(g, 1), :]
            mask = jnp.dot(
                jnp.where(diagonal, stays, 0.0).astype(BF16),
                jnp.ones((GROUP, err.shape[2]), BF16),
                preferred_element_type=F32,
            )
            err[0, span, :] = (grad[span, :].astype(F32) + err[0, span, :]) * mask
        return 0

    pack(0)
    pl.semaphore_wait(barrier, 10)
    greet(round_z, line["z"])

    raw_swaps = [
        copy(
            raw.at[1 - c, 0], state[0].at[mine_at[0], own_rows],
            raw_send, raw_recv, sibling,
        )
    ]
    for a in (1, 2):
        raw_swaps.append(
            copy(
                raw_b.at[1 - c, a - 1], state[a].at[mine_at[a], own_rows],
                rawb_send.at[a - 1], rawb_recv.at[a - 1], sibling,
            )
        )
    for go in raw_swaps:
        go.start()

    spread(0)
    mine = weights.at[x, z, y, c]
    copy(mine, mine, f_send, f_recv, sibling).start()

    pack(1)

    for go in raw_swaps:
        go.wait_recv()
    for a, order in enumerate(STATE_ORDERS):
        block = state[a].at[mine_at[a]]
        for k in (1, 2, 3):
            copy(
                block, block, s_send.at[a], s_recv.at[a], along(order[0], k)
            ).start()

    pl.semaphore_wait(round_z, 3)
    greet(round_x, line["x"])
    pack(2)

    arrive(0)
    spread(1)
    forward(0)
    pack(3)

    def place(a):
        order = STATE_ORDERS[a]
        bytes_of(state[a].at[pl.ds(0, 3)], s_send.at[a], s_recv.at[a]).wait_recv()
        units = {"x": 16, "z": 4, "y": 1}
        spot = iota((16 * UNIT, GROUP), 0)
        target = (
            (spot // 64) * (units[order[1]] * UNIT)
            + (spot // 16) % 4 * (units[order[2]] * UNIT)
            + spot % 16
            + at[order[0]] * (units[order[0]] * UNIT)
        ).astype(F32)
        hits = []
        for k in range(4):
            source = chip + (k - at[order[0]]) * units[order[0]]
            hits.append(onehot(rooted[pl.ds(source, 1), :] == target))
        hits = jnp.concatenate(hits, axis=1)
        whole = state[a][...].reshape(4 * GROUP, 128)
        if a:
            split = whole
        else:
            high = whole.astype(BF16)
            rest = whole - high.astype(F32)
            middle = rest.astype(BF16)
            low = (rest - middle.astype(F32)).astype(BF16)
            split = jnp.concatenate([high, middle, low], axis=1)
        moved = jnp.dot(hits, split, preferred_element_type=F32)
        if not a:
            moved = (moved[:, :128] + moved[:, 128:256]) + moved[:, 256:]
        state1[a][...] = moved.astype(state1[a].dtype).reshape(state1[a].shape)

    def state_phase(phase, source, target):
        for a, order in enumerate(STATE_ORDERS):
            axis = order[phase]
            n = phase * 3 + a
            for k in (1, 2, 3):
                copy(
                    source[a].at[(at[axis] + k) % 4], target[a].at[k - 1],
                    s_send.at[n], s_recv.at[n], along(axis, k),
                ).start()

    def state_bytes(phase, target, a):
        n = phase * 3 + a
        return bytes_of(target[a], s_send.at[n], s_recv.at[n])

    def state_sum(phase, source, target, total):
        for a in range(3):
            state_bytes(phase, target, a).wait_recv()
        for a, order in enumerate(STATE_ORDERS):
            value = source[a][at[order[phase]]].astype(F32)
            for k in range(3):
                value = value + target[a][k].astype(F32)
            total[a][...] = value.astype(total[a].dtype)

    half_chips = chips // 2
    swaps = []
    for p in range(2):
        ranks = slice(p * keep_n // 2, (p + 1) * keep_n // 2)
        span = pl.ds(p * half_chips, half_chips)
        for h in range(2):
            packed[h, span] = (
                acc[ranks, h * 128 : (h + 1) * 128]
                .astype(BF16)
                .reshape(half_chips, UNIT, 128)
            )
        swap = copy(
            packed.at[1 - c, span], from_core.at[span],
            core_send.at[p], core_recv.at[p], sibling,
        )
        swap.start()
        swaps.append(swap)

    for a in range(3):
        place(a)
    state_phase(1, state1, sgot2)
    pl.semaphore_wait(round_x, 3)


    def scatter(k):
        other, peer = far(k)
        return copy(part.at[other], got.at[k - 1], rs_send, rs_recv, peer)

    for p in range(2):
        swaps[p].wait_recv()
        span = pl.ds(p * half_chips, half_chips)
        part[span] = (packed[c, span].astype(F32) + from_core[span].astype(F32)).astype(
            BF16
        )

    each(lambda k: scatter(k).start())
    own = packed[c, chip].astype(F32) + from_core[chip].astype(F32)

    state_sum(1, state1, sgot2, state2)
    state_phase(2, state2, sgot3)

    arrive(1)
    spread(2)
    spread(3)
    forward(1)

    for k in range(keep_n // GROUP):
        lanes = (iota((64, GROUP), 1) + k * GROUP).astype(F32)
        expand[:, k * GROUP : (k + 1) * GROUP] = onehot(half == lanes)

    state_sum(2, state2, sgot3, state3)
    scattered = bytes_of(got, rs_send, rs_recv)
    scattered.wait_recv()
    summed = (own + jnp.sum(got[...].astype(F32), axis=0)).astype(BF16)
    new_master, _, _ = adamw(*(ref[...].astype(F32) for ref in state3), summed.astype(F32))
    result[c, chip, 0] = summed
    result[c, chip, 1] = new_master.astype(BF16)

    plane = chips // 4

    def gather(k):
        unit = result.at[c, chip]
        return copy(unit, unit, ag_send, ag_recv.at[x], far(k)[1])

    def pass_on(q):
        block = result.at[c, pl.ds(q * plane, plane)]
        return copy(block, block, half_send, half_recv, sibling)

    each(lambda k: gather(k).start())
    spread(4)
    for stage in (2, 3):
        arrive(stage)
        forward(stage)
    lax.fori_loop(0, chunks, settle, 0)

    for k in (3, 2, 1):
        q = (x + k) % 4
        block = result.at[c, pl.ds(q * plane, plane)]
        bytes_of(block, ag_send, ag_recv.at[q]).wait_recv()
        pass_on(q).start()
    bytes_of(result.at[c, pl.ds(0, plane - 1)], ag_send, ag_recv.at[x]).wait_recv()
    pass_on(x).start()

    arrive(4)
    forward(4)

    scattered.wait_send()
    bytes_of(result.at[c, pl.ds(0, chips - 1)], ag_send, ag_recv.at[x]).wait_send()
    for go in raw_swaps:
        go.wait_send()
    for go in swaps:
        go.wait_send()
    for a in range(3):
        bytes_of(state[a].at[pl.ds(0, 3)], s_send.at[a], s_recv.at[a]).wait_send()
        state_bytes(1, sgot2, a).wait_send()
        state_bytes(2, sgot3, a).wait_send()
    for stage in range(5):
        stage_bytes(stage, w_send, w_recv).wait_send()
    bytes_of(weights.at[:, :, :, c], f_send, f_recv).wait()
    bytes_of(result.at[c], half_send, half_recv).wait()


def finish_kernel(
    err, weights, result, expand, rooted, starts_v, master, first, second,
    err_hbm, out_hbm, new_master, new_first, new_second,
    out, starts, err_sem, out_sem, starts_sem,
):
    groups = rooted.shape[0]
    to_smem = pltpu.make_async_copy(starts_v, starts, starts_sem)
    to_smem.start()
    rows = err.shape[1]
    pieces = err_sem.shape[0]
    copies = []
    for i in range(pieces):
        span = pl.ds(i * (rows // pieces), rows // pieces)
        go = pltpu.make_async_copy(err.at[0, span], err_hbm.at[0, span], err_sem.at[i])
        go.start()
        copies.append(go)

    to_smem.wait()
    units = result.shape[1]
    window = GROUP // UNIT + 1
    batch = groups // out_sem.shape[0]

    def store(i):
        span = pl.ds(i * batch, batch)
        return pltpu.make_async_copy(out.at[span], out_hbm.at[span], out_sem.at[i])

    def fill(i, _):
        for j in range(batch):
            g = i * batch + j
            unit = jnp.minimum(starts[g, 0] // UNIT, units - window)
            near = rooted[pl.ds(g, 1), :] - (unit * UNIT).astype(F32)
            hits = onehot(iota((window * UNIT, GROUP), 0).astype(F32) == near)
            held = jnp.concatenate(
                [
                    result[h, pl.ds(unit, window), 1].reshape(window * UNIT, 128)
                    for h in range(2)
                ],
                axis=1,
            )
            moved = lax.dot_general(
                hits, held, (((0,), (0,)), ((), ())), preferred_element_type=F32
            ).astype(BF16)
            for c in range(2):
                span = slice(c * 64, c * 64 + 64)
                for h in range(2):
                    lanes = slice(h * 128, h * 128 + 128)
                    out[g, span, lanes] = weights[g, c, h] + moved[span, lanes]
        store(i).start()
        return 0

    steps = out_sem.shape[0]
    lax.fori_loop(0, steps, fill, 0)
    total = jnp.concatenate(
        [
            jnp.dot(
                expand[...], result[h, :, 0].reshape(-1, 128),
                preferred_element_type=F32,
            )
            for h in range(2)
        ],
        axis=1,
    )
    new_master[...], new_first[...], new_second[...] = adamw(
        master[...], first[...], second[...], total
    )

    for go in copies:
        go.wait()
    lax.fori_loop(0, steps, lambda i, _: (store(i).wait(), 0)[1], 0)


def body(gradients, error_memory, block_lists, master, first_moment, second_moment):
    _, rows, width = gradients.shape
    owned = master.shape[0]
    levels, keep_n = block_lists.shape[1:]
    groups = rows // GROUP
    chunks = rows // CHUNK
    vmem = pl.BlockSpec(memory_space=pltpu.VMEM)
    anywhere = pl.BlockSpec(memory_space=pl.ANY)
    dma = pltpu.SemaphoreType.DMA

    err, weights, result, expand, rooted, starts = pl.pallas_call(
        merge_kernel,
        out_shape=(
            pltpu.VMEM((1, rows, width), F32),
            pltpu.VMEM((4, 4, 4, 2, 2, owned, 128), BF16),
            pltpu.VMEM((2, groups, 2, UNIT, 128), BF16),
            pltpu.VMEM((owned, keep_n), BF16),
            pltpu.VMEM((groups, GROUP), F32),
            pltpu.VMEM((groups, GROUP), jnp.int32),
        ),
        in_specs=[anywhere] * 6,
        out_specs=(vmem,) * 6,
        scratch_shapes=[
            pltpu.VMEM((rows, width), BF16),
            pltpu.VMEM((levels, keep_n), jnp.int32),
            pltpu.VMEM((2, 3, owned, 128), F32),
            pltpu.VMEM((2, 2, owned, 128), BF16),
            pltpu.VMEM((keep_n, width), F32),
            pltpu.VMEM((groups, GROUP), F32),
            pltpu.VMEM((groups, GROUP), F32),
            pltpu.VMEM((GROUP, GROUP), F32),
            pltpu.VMEM((CHUNK, width), BF16),
            pltpu.VMEM((2, groups, UNIT, 128), BF16),
            pltpu.VMEM((groups, UNIT, 128), BF16),
            pltpu.VMEM((groups, UNIT, 128), BF16),
            pltpu.VMEM((groups - 1, UNIT, 128), BF16),
            *(
                pltpu.VMEM((*lead, *shape, 128), kind)
                for lead, kind in (((), F32), ((2,), BF16))
                for shape in (
                    (4, GROUP), (4, 4, UNIT), (4, UNIT), (UNIT,),
                    (3, 4, UNIT), (3, UNIT),
                )
            ),
            dma((chunks,)), dma((chunks,)), dma, dma,
            dma((2,)), dma((2,)), dma, dma, dma((2,)), dma((2,)),
            dma, dma, dma, dma((4,)), dma, dma,
            dma((9,)), dma((9,)),
            dma((5,)), dma((5,)), dma, dma,
            pltpu.SemaphoreType.REGULAR, pltpu.SemaphoreType.REGULAR,
        ],
        compiler_params=pltpu.CompilerParams(
            collective_id=0, has_side_effects=True, vmem_limit_bytes=46 * MIB
        ),
        name="merge",
    )(gradients, error_memory, block_lists, master, first_moment, second_moment)

    new_errors, out, new_master, new_first, new_second = pl.pallas_call(
        finish_kernel,
        out_shape=(
            jax.ShapeDtypeStruct((1, rows, width), F32),
            jax.ShapeDtypeStruct((groups, GROUP, width), BF16),
            jax.ShapeDtypeStruct((owned, width), F32),
            jax.ShapeDtypeStruct((owned, width), F32),
            jax.ShapeDtypeStruct((owned, width), F32),
        ),
        in_specs=[vmem] * 9,
        out_specs=(anywhere, anywhere, vmem, vmem, vmem),
        scratch_shapes=[
            pltpu.VMEM((groups, GROUP, width), BF16),
            pltpu.SMEM((groups, GROUP), jnp.int32),
            dma((4,)), dma((8,)), dma,
        ],
        compiler_params=pltpu.CompilerParams(vmem_limit_bytes=32 * MIB),
        name="finish",
    )(
        err, weights.reshape(groups, 2, 2, owned, 128), result, expand, rooted, starts,
        master, first_moment, second_moment,
    )
    return new_errors, new_master, new_first, new_second, out.reshape(rows, width)


def solution(mesh):
    in_specs = (
        P("dp", None, None),
        P("dp", None, None),
        P("dp", None, None),
        P("dp", None),
        P("dp", None),
        P("dp", None),
    )
    out_specs = (P("dp", None, None), P("dp", None), P("dp", None), P("dp", None), P())
    return jax.shard_map(
        body, mesh=mesh, in_specs=in_specs, out_specs=out_specs, check_vma=False
    )
```

```python
import jax
import jax.numpy as jnp
from jax import lax
from jax.experimental import pallas as pl
from jax.experimental.pallas import tpu as pltpu
from jax.sharding import PartitionSpec as P

FIRST_BIAS = 0.9999734386011124
SECOND_BIAS = 0.09520785288629036
MESH = pl.DeviceIdType.MESH
F32 = jnp.float32
BF16 = jnp.bfloat16
MIB = 1 << 20

GROUP = 128
CHUNK = 2048
UNIT = 16
SPAN = 256

ORDERS = ("xzy", "zyx", "yxz")
STATE_ORDERS = ("zyx", "xzy", "yxz")


def iota(shape, dim):
    return lax.broadcasted_iota(jnp.int32, shape, dim)


def onehot(hits):
    return jnp.where(hits, 1.0, 0.0).astype(BF16)


def adamw(master, first, second, summed):
    new_first = 0.9 * first + 0.1 * summed
    new_second = 0.999 * second + 0.001 * summed * summed
    first_hat = new_first / FIRST_BIAS
    second_hat = new_second / SECOND_BIAS
    new_master = master - 0.001 * (
        first_hat / (jnp.sqrt(second_hat) + 1e-08) + 0.1 * master
    )
    return new_master, new_first, new_second


def merge_kernel(
    grad_hbm, err_hbm, lists_hbm, master_hbm, first_hbm, second_hbm,
    err, weights, result, expand, rooted, starts,
    grad, lists, raw, raw_b, acc, sent, kept, column, value_b,
    packed, from_core, part, got,
    master0, master1, master2, master3, mgot2, mgot3,
    moment0, moment1, moment2, moment3, vgot2, vgot3,
    grad_sem, err_sem, list_sem, raw_sem,
    core_send, core_recv, raw_send, raw_recv, rawb_send, rawb_recv,
    rs_send, rs_recv, ag_send, ag_recv, half_send, half_recv,
    s_send, s_recv, w_send, w_recv, f_send, f_recv, round_z, round_x,
):
    rows = grad.shape[0]
    groups = rows // GROUP
    chunks = rows // CHUNK
    levels, keep_n = lists.shape
    me = lax.axis_index("dp")
    c = me % 2
    y = (me // 2) % 4
    z = (me // 8) % 4
    x = me // 32
    chip = me // 2
    chips = groups
    sibling = me + 1 - 2 * c
    at = {"x": x, "z": z, "y": y}
    strides = {"x": 32, "z": 8, "y": 2}

    def far(k):
        other = (chip + k) % chips
        return other, 2 * other + c

    def along(axis, k):
        return me + ((at[axis] + k) % 4 - at[axis]) * strides[axis]

    def copy(src, dst, send, recv, peer):
        return pltpu.make_async_remote_copy(
            src_ref=src, dst_ref=dst, send_sem=send, recv_sem=recv,
            device_id=(peer,), device_id_type=MESH,
        )

    def each(act):
        def some(i, _):
            for j in range(21):
                act(i * 21 + j + 1)
            return 0

        lax.fori_loop(0, (chips - 1) // 21, some, 0)

    def bytes_of(ref, send, recv):
        return copy(ref, ref, send, recv, sibling)

    def three(master_ref, moments_ref):
        return master_ref, moments_ref.at[0], moments_ref.at[1]

    state = three(master0, moment0)
    state1 = three(master1, moment1)
    state2 = three(master2, moment2)
    state3 = three(master3, moment3)
    sgot2 = three(mgot2, vgot2)
    sgot3 = three(mgot3, vgot3)

    def greet(semaphore, peers):
        for peer in peers:
            pl.semaphore_signal(
                semaphore, inc=1, device_id=(peer,), device_id_type=MESH
            )

    line = {axis: [along(axis, k) for k in (1, 2, 3)] for axis in "xzy"}
    barrier = pltpu.get_barrier_semaphore()
    greet(barrier, [sibling, *line["y"], *line["z"], *line["x"]])

    list_load = pltpu.make_async_copy(lists_hbm.at[0], lists, list_sem)
    list_load.start()
    for a, source in enumerate((master_hbm, first_hbm, second_hbm)):
        for h in range(2):
            go = pltpu.make_async_copy(
                source.at[:, pl.ds(h * 128, 128)], raw.at[h, a], raw_sem
            )
            go.start()

    def loads(i):
        span = pl.ds(pl.multiple_of(i * CHUNK, CHUNK), CHUNK)
        return (
            pltpu.make_async_copy(grad_hbm.at[0, span], grad.at[span], grad_sem.at[i]),
            pltpu.make_async_copy(err_hbm.at[0, span], err.at[0, span], err_sem.at[i]),
        )

    def load(i, _):
        for go in loads(i):
            go.start()
        return 0

    lax.fori_loop(0, chunks, load, 0)

    parts = (
        ((0,), pl.ds(0, 48)),
        ((1,), pl.ds(0, 48)),
        ((pl.ds(0, 2),), pl.ds(48, 16)),
    )

    def region(s, stage, place, half=None):
        cols, span = parts[s]
        taken = ORDERS[s][: min(stage, 2)]
        index = [pl.ds(0, 4) if axis in taken else place[axis] for axis in "xzy"]
        if half is not None:
            index["xzy".index(taken[0])] = pl.ds(2 * half, 2)
        return weights.at[(*index, c, *cols, span)]

    def stage_bytes(stage, sends, recvs):
        same = (
            weights.at[0, 0, pl.ds(0, 3), c],
            weights.at[0, pl.ds(0, 3), :, c],
            weights.at[pl.ds(0, 2), :, :, c],
            weights.at[0, :, :, c],
        )
        return bytes_of(same[stage], sends.at[stage], recvs.at[stage])

    def spread(stage):
        for s, order in enumerate(ORDERS):
            axis = order[min(stage, 2)]
            for k in (1, 2, 3) if stage < 2 else (1, 3):
                if stage < 3:
                    block = region(s, stage, at)
                else:
                    origin = {**at, axis: (at[axis] + 4 - k) % 4}
                    block = region(s, stage, origin, k // 2)
                copy(
                    block, block, w_send.at[stage], w_recv.at[stage], along(axis, k)
                ).start()

    def arrive(stage):
        stage_bytes(stage, w_send, w_recv).wait_recv()

    def forward(stage):
        for s, order in enumerate(ORDERS):
            axis = order[min(stage, 2)]
            for k in ((1, 2, 3), (1, 2, 3), (1, 3), (2,))[stage]:
                block = region(s, stage, {**at, axis: (at[axis] + k) % 4})
                copy(block, block, f_send, f_recv, sibling).start()

    list_load.wait()

    ids = lists[...]
    high_ids = (ids >> 7).astype(F32)
    low_ids = (ids & 127).astype(F32)

    inner = iota((SPAN // 16, 16, GROUP), 0) * 16 + iota((SPAN // 16, 16, GROUP), 1)
    inner = inner.astype(F32).astype(BF16)
    one = jnp.ones((SPAN // 16, 16, GROUP), BF16)
    zero = jnp.zeros((SPAN // 16, 16, GROUP), BF16)

    def ladder(row, count):
        tiles = count // 16
        near = jnp.broadcast_to(row, (16, GROUP)).astype(BF16)
        hit = jnp.where(inner[:tiles] == near[None], one[:tiles], zero[:tiles])
        return hit.reshape(count, GROUP)

    def member(r):
        spans = [slice(j, j + GROUP) for j in range(0, keep_n, GROUP)]
        high = [ladder(high_ids[r : r + 1, span], groups) for span in spans]
        low = [ladder(low_ids[r : r + 1, span], GROUP) for span in spans]
        return lax.dot_general(
            jnp.concatenate(high, axis=1), jnp.concatenate(low, axis=1),
            (((1,), (1,)), ((), ())), preferred_element_type=F32,
        )

    root = member(levels - 1)
    root_b = root.astype(BF16)
    before = onehot(iota((GROUP, GROUP), 0) < iota((GROUP, GROUP), 1))
    inside = jnp.dot(root_b, before, preferred_element_type=F32)
    total = jnp.dot(root_b, jnp.ones((GROUP, GROUP), BF16), preferred_element_type=F32)
    above = onehot(iota((groups, groups), 1) < iota((groups, groups), 0))
    start = jnp.dot(above, total.astype(BF16), preferred_element_type=F32)
    rank = start + inside
    starts[...] = start.astype(jnp.int32)
    rooted[...] = jnp.where(root > 0.5, rank, -1.0)

    keep = member(0)
    sent[...] = keep
    for r in range(1, levels - 1):
        keep = keep * member(r)
    kept[...] = jnp.where(keep * root > 0.5, rank, -1.0)

    chip_ranks = rooted[pl.ds(chip, 1), :]
    column[...] = jnp.transpose(jnp.broadcast_to(chip_ranks, (GROUP, GROUP)))
    own_rows = pl.ds(pl.multiple_of(c * 64, 64), 64)
    half = column[own_rows, :]
    pltpu.make_async_copy(raw, raw, raw_sem).wait()
    raw_b[...] = raw[:, 1:].astype(BF16)
    mine_at = [at[order[0]] for order in STATE_ORDERS]
    master0[mine_at[0], own_rows, :] = raw[c, 0]
    for a in (1, 2):
        moment0[a - 1, mine_at[a], own_rows, :] = raw_b[c, a - 1]

    for h in range(2):
        new_master, _, _ = adamw(raw[h, 0], raw[h, 1], raw[h, 2], 0.0)
        weights[x, z, y, c, h] = jnp.where(half < 0.0, new_master, 0.0).astype(BF16)
    acc[...] = jnp.zeros_like(acc)
    diagonal = iota((GROUP, GROUP), 0) == iota((GROUP, GROUP), 1)

    def pack(i):
        for go in loads(i):
            go.wait()
        each_row = []
        for j in range(CHUNK // GROUP):
            g = i * (CHUNK // GROUP) + j
            span = pl.ds(pl.multiple_of(g * GROUP, GROUP), GROUP)
            value = grad[span, :].astype(F32) + err[0, span, :]
            value_b[j * GROUP : (j + 1) * GROUP, :] = value.astype(BF16)
            each_row.append(kept[pl.ds(g, 1), :])
        for q in range(keep_n // SPAN):
            hits = []
            for row in each_row:
                hits.append(ladder(jnp.clip(row - q * SPAN, -1.0, SPAN), SPAN))
            acc[q * SPAN : (q + 1) * SPAN, :] += jnp.dot(
                jnp.concatenate(hits, axis=1), value_b[...], preferred_element_type=F32
            )

    def settle(i, _):
        for j in range(CHUNK // GROUP):
            g = i * (CHUNK // GROUP) + j
            span = pl.ds(pl.multiple_of(g * GROUP, GROUP), GROUP)
            stays = 1.0 - sent[pl.ds(g, 1), :]
            mask = jnp.dot(
                jnp.where(diagonal, stays, 0.0).astype(BF16),
                jnp.ones((GROUP, err.shape[2]), BF16),
                preferred_element_type=F32,
            )
            err[0, span, :] = (grad[span, :].astype(F32) + err[0, span, :]) * mask
        return 0

    pack(0)
    pl.semaphore_wait(barrier, 10)
    greet(round_z, line["z"])

    raw_swaps = [
        copy(
            raw.at[1 - c, 0], state[0].at[mine_at[0], own_rows],
            raw_send, raw_recv, sibling,
        )
    ]
    for a in (1, 2):
        raw_swaps.append(
            copy(
                raw_b.at[1 - c, a - 1], state[a].at[mine_at[a], own_rows],
                rawb_send.at[a - 1], rawb_recv.at[a - 1], sibling,
            )
        )
    for go in raw_swaps:
        go.start()

    spread(0)
    mine = weights.at[x, z, y, c]
    copy(mine, mine, f_send, f_recv, sibling).start()

    pack(1)

    for go in raw_swaps:
        go.wait_recv()
    for a, order in enumerate(STATE_ORDERS):
        block = state[a].at[mine_at[a]]
        for k in (1, 2, 3):
            copy(
                block, block, s_send.at[a], s_recv.at[a], along(order[0], k)
            ).start()

    pl.semaphore_wait(round_z, 3)
    greet(round_x, line["x"])
    pack(2)

    arrive(0)
    spread(1)
    forward(0)
    pack(3)

    def place(a):
        order = STATE_ORDERS[a]
        bytes_of(state[a].at[pl.ds(0, 3)], s_send.at[a], s_recv.at[a]).wait_recv()
        shifts = {"x": 8, "z": 6, "y": 4}
        units = {"x": 16, "z": 4, "y": 1}
        hits = []
        for k in range(4):
            source = chip + (k - at[order[0]]) * units[order[0]]
            ranks = rooted[pl.ds(source, 1), :].astype(jnp.int32)
            first, second, third = ((ranks >> shifts[axis]) & 3 for axis in order)
            here = (ranks >= 0) & (first == at[order[0]])
            spot = second * (4 * UNIT) + third * UNIT + (ranks & (UNIT - 1))
            row = jnp.where(here, spot, -1).astype(F32)
            hits.append(ladder(row, 16 * UNIT))
        hits = jnp.concatenate(hits, axis=1)
        whole = state[a][...].reshape(4 * GROUP, 128)
        if a:
            split = whole
        else:
            high = whole.astype(BF16)
            rest = whole - high.astype(F32)
            middle = rest.astype(BF16)
            low = (rest - middle.astype(F32)).astype(BF16)
            split = jnp.concatenate([high, middle, low], axis=1)
        moved = jnp.dot(hits, split, preferred_element_type=F32)
        if not a:
            moved = (moved[:, :128] + moved[:, 128:256]) + moved[:, 256:]
        state1[a][...] = moved.astype(state1[a].dtype).reshape(state1[a].shape)

    def state_phase(phase, source, target):
        for a, order in enumerate(STATE_ORDERS):
            axis = order[phase]
            n = phase * 3 + a
            for k in (1, 2, 3):
                copy(
                    source[a].at[(at[axis] + k) % 4], target[a].at[k - 1],
                    s_send.at[n], s_recv.at[n], along(axis, k),
                ).start()

    def state_bytes(phase, target, a):
        n = phase * 3 + a
        return bytes_of(target[a], s_send.at[n], s_recv.at[n])

    def state_sum(phase, source, target, total):
        for a in range(3):
            state_bytes(phase, target, a).wait_recv()
        for a, order in enumerate(STATE_ORDERS):
            value = source[a][at[order[phase]]].astype(F32)
            for k in range(3):
                value = value + target[a][k].astype(F32)
            total[a][...] = value.astype(total[a].dtype)

    half_chips = chips // 2
    swaps = []
    for p in range(2):
        ranks = slice(p * keep_n // 2, (p + 1) * keep_n // 2)
        span = pl.ds(p * half_chips, half_chips)
        for h in range(2):
            packed[h, span] = (
                acc[ranks, h * 128 : (h + 1) * 128]
                .astype(BF16)
                .reshape(half_chips, UNIT, 128)
            )
        swap = copy(
            packed.at[1 - c, span], from_core.at[span],
            core_send.at[p], core_recv.at[p], sibling,
        )
        swap.start()
        swaps.append(swap)

    for a in range(3):
        place(a)
    state_phase(1, state1, sgot2)
    pl.semaphore_wait(round_x, 3)


    def scatter(k):
        other, peer = far(k)
        return copy(part.at[other], got.at[k - 1], rs_send, rs_recv, peer)

    for p in range(2):
        swaps[p].wait_recv()
        span = pl.ds(p * half_chips, half_chips)
        part[span] = (packed[c, span].astype(F32) + from_core[span].astype(F32)).astype(
            BF16
        )

    each(lambda k: scatter(k).start())
    own = packed[c, chip].astype(F32) + from_core[chip].astype(F32)

    state_sum(1, state1, sgot2, state2)
    state_phase(2, state2, sgot3)

    arrive(1)
    spread(2)
    forward(1)

    for k in range(keep_n // GROUP):
        lanes = (iota((64, GROUP), 1) + k * GROUP).astype(F32)
        expand[:, k * GROUP : (k + 1) * GROUP] = onehot(half == lanes)

    state_sum(2, state2, sgot3, state3)
    scattered = bytes_of(got, rs_send, rs_recv)
    scattered.wait_recv()
    summed = (own + jnp.sum(got[...].astype(F32), axis=0)).astype(BF16)
    new_master, _, _ = adamw(*(ref[...].astype(F32) for ref in state3), summed.astype(F32))
    result[c, chip, 0] = summed
    result[c, chip, 1] = new_master.astype(BF16)

    plane = chips // 4

    def gather(k):
        unit = result.at[c, chip]
        return copy(unit, unit, ag_send, ag_recv.at[x], far(k)[1])

    def pass_on(q):
        block = result.at[c, pl.ds(q * plane, plane)]
        return copy(block, block, half_send, half_recv, sibling)

    each(lambda k: gather(k).start())
    arrive(2)
    spread(3)
    forward(2)
    lax.fori_loop(0, chunks, settle, 0)

    for k in (3, 2, 1):
        q = (x + k) % 4
        block = result.at[c, pl.ds(q * plane, plane)]
        bytes_of(block, ag_send, ag_recv.at[q]).wait_recv()
        pass_on(q).start()
    bytes_of(result.at[c, pl.ds(0, plane - 1)], ag_send, ag_recv.at[x]).wait_recv()
    pass_on(x).start()

    arrive(3)
    forward(3)

    scattered.wait_send()
    bytes_of(result.at[c, pl.ds(0, chips - 1)], ag_send, ag_recv.at[x]).wait_send()
    for go in raw_swaps:
        go.wait_send()
    for go in swaps:
        go.wait_send()
    for a in range(3):
        bytes_of(state[a].at[pl.ds(0, 3)], s_send.at[a], s_recv.at[a]).wait_send()
        state_bytes(1, sgot2, a).wait_send()
        state_bytes(2, sgot3, a).wait_send()
    for stage in range(4):
        stage_bytes(stage, w_send, w_recv).wait_send()
    bytes_of(weights.at[:, :, :, c], f_send, f_recv).wait()
    bytes_of(result.at[c], half_send, half_recv).wait()


def finish_kernel(
    err, weights, result, expand, rooted, starts_v, master, first, second,
    err_hbm, out_hbm, new_master, new_first, new_second,
    out, starts, err_sem, out_sem, starts_sem,
):
    groups = rooted.shape[0]
    to_smem = pltpu.make_async_copy(starts_v, starts, starts_sem)
    to_smem.start()
    rows = err.shape[1]
    pieces = err_sem.shape[0]
    copies = []
    for i in range(pieces):
        span = pl.ds(i * (rows // pieces), rows // pieces)
        go = pltpu.make_async_copy(err.at[0, span], err_hbm.at[0, span], err_sem.at[i])
        go.start()
        copies.append(go)

    to_smem.wait()
    units = result.shape[1]
    window = GROUP // UNIT + 1
    batch = groups // out_sem.shape[0]

    def store(i):
        span = pl.ds(i * batch, batch)
        return pltpu.make_async_copy(out.at[span], out_hbm.at[span], out_sem.at[i])

    def fill(i, _):
        for j in range(batch):
            g = i * batch + j
            unit = jnp.minimum(starts[g, 0] // UNIT, units - window)
            near = rooted[pl.ds(g, 1), :] - (unit * UNIT).astype(F32)
            hits = onehot(iota((window * UNIT, GROUP), 0).astype(F32) == near)
            held = jnp.concatenate(
                [
                    result[h, pl.ds(unit, window), 1].reshape(window * UNIT, 128)
                    for h in range(2)
                ],
                axis=1,
            )
            moved = lax.dot_general(
                hits, held, (((0,), (0,)), ((), ())), preferred_element_type=F32
            ).astype(BF16)
            for c in range(2):
                span = slice(c * 64, c * 64 + 64)
                for h in range(2):
                    lanes = slice(h * 128, h * 128 + 128)
                    out[g, span, lanes] = weights[g, c, h] + moved[span, lanes]
        store(i).start()
        return 0

    steps = out_sem.shape[0]
    lax.fori_loop(0, steps, fill, 0)
    total = jnp.concatenate(
        [
            jnp.dot(
                expand[...], result[h, :, 0].reshape(-1, 128),
                preferred_element_type=F32,
            )
            for h in range(2)
        ],
        axis=1,
    )
    new_master[...], new_first[...], new_second[...] = adamw(
        master[...], first[...], second[...], total
    )

    for go in copies:
        go.wait()
    lax.fori_loop(0, steps, lambda i, _: (store(i).wait(), 0)[1], 0)


def body(gradients, error_memory, block_lists, master, first_moment, second_moment):
    _, rows, width = gradients.shape
    owned = master.shape[0]
    levels, keep_n = block_lists.shape[1:]
    groups = rows // GROUP
    chunks = rows // CHUNK
    vmem = pl.BlockSpec(memory_space=pltpu.VMEM)
    anywhere = pl.BlockSpec(memory_space=pl.ANY)
    dma = pltpu.SemaphoreType.DMA

    err, weights, result, expand, rooted, starts = pl.pallas_call(
        merge_kernel,
        out_shape=(
            pltpu.VMEM((1, rows, width), F32),
            pltpu.VMEM((4, 4, 4, 2, 2, owned, 128), BF16),
            pltpu.VMEM((2, groups, 2, UNIT, 128), BF16),
            pltpu.VMEM((owned, keep_n), BF16),
            pltpu.VMEM((groups, GROUP), F32),
            pltpu.VMEM((groups, GROUP), jnp.int32),
        ),
        in_specs=[anywhere] * 6,
        out_specs=(vmem,) * 6,
        scratch_shapes=[
            pltpu.VMEM((rows, width), BF16),
            pltpu.VMEM((levels, keep_n), jnp.int32),
            pltpu.VMEM((2, 3, owned, 128), F32),
            pltpu.VMEM((2, 2, owned, 128), BF16),
            pltpu.VMEM((keep_n, width), F32),
            pltpu.VMEM((groups, GROUP), F32),
            pltpu.VMEM((groups, GROUP), F32),
            pltpu.VMEM((GROUP, GROUP), F32),
            pltpu.VMEM((CHUNK, width), BF16),
            pltpu.VMEM((2, groups, UNIT, 128), BF16),
            pltpu.VMEM((groups, UNIT, 128), BF16),
            pltpu.VMEM((groups, UNIT, 128), BF16),
            pltpu.VMEM((groups - 1, UNIT, 128), BF16),
            *(
                pltpu.VMEM((*lead, *shape, 128), kind)
                for lead, kind in (((), F32), ((2,), BF16))
                for shape in (
                    (4, GROUP), (4, 4, UNIT), (4, UNIT), (UNIT,),
                    (3, 4, UNIT), (3, UNIT),
                )
            ),
            dma((chunks,)), dma((chunks,)), dma, dma,
            dma((2,)), dma((2,)), dma, dma, dma((2,)), dma((2,)),
            dma, dma, dma, dma((4,)), dma, dma,
            dma((9,)), dma((9,)),
            dma((4,)), dma((4,)), dma, dma,
            pltpu.SemaphoreType.REGULAR, pltpu.SemaphoreType.REGULAR,
        ],
        compiler_params=pltpu.CompilerParams(
            collective_id=0, has_side_effects=True, vmem_limit_bytes=46 * MIB
        ),
        name="merge",
    )(gradients, error_memory, block_lists, master, first_moment, second_moment)

    new_errors, out, new_master, new_first, new_second = pl.pallas_call(
        finish_kernel,
        out_shape=(
            jax.ShapeDtypeStruct((1, rows, width), F32),
            jax.ShapeDtypeStruct((groups, GROUP, width), BF16),
            jax.ShapeDtypeStruct((owned, width), F32),
            jax.ShapeDtypeStruct((owned, width), F32),
            jax.ShapeDtypeStruct((owned, width), F32),
        ),
        in_specs=[vmem] * 9,
        out_specs=(anywhere, anywhere, vmem, vmem, vmem),
        scratch_shapes=[
            pltpu.VMEM((groups, GROUP, width), BF16),
            pltpu.SMEM((groups, GROUP), jnp.int32),
            dma((4,)), dma((8,)), dma,
        ],
        compiler_params=pltpu.CompilerParams(vmem_limit_bytes=32 * MIB),
        name="finish",
    )(
        err, weights.reshape(groups, 2, 2, owned, 128), result, expand, rooted, starts,
        master, first_moment, second_moment,
    )
    return new_errors, new_master, new_first, new_second, out.reshape(rows, width)


def solution(mesh):
    in_specs = (
        P("dp", None, None),
        P("dp", None, None),
        P("dp", None, None),
        P("dp", None),
        P("dp", None),
        P("dp", None),
    )
    out_specs = (P("dp", None, None), P("dp", None), P("dp", None), P("dp", None), P())
    return jax.shard_map(
        body, mesh=mesh, in_specs=in_specs, out_specs=out_specs, check_vma=False
    )
```

```python
import jax
import jax.numpy as jnp
from jax import lax
from jax.experimental import pallas as pl
from jax.experimental.pallas import tpu as pltpu
from jax.sharding import PartitionSpec as P

FIRST_BIAS = 0.9999734386011124
SECOND_BIAS = 0.09520785288629036
MESH = pl.DeviceIdType.MESH
F32 = jnp.float32
BF16 = jnp.bfloat16
MIB = 1 << 20

GROUP = 128
CHUNK = 2048
UNIT = 16
SPAN = 256

ORDERS = ("xzy", "zyx", "yxz")
STATE_ORDERS = ("zyx", "xzy")


def iota(shape, dim):
    return lax.broadcasted_iota(jnp.int32, shape, dim)


def onehot(hits):
    return jnp.where(hits, 1.0, 0.0).astype(BF16)


def adamw(master, first, second, summed):
    new_first = 0.9 * first + 0.1 * summed
    new_second = 0.999 * second + 0.001 * summed * summed
    first_hat = new_first / FIRST_BIAS
    second_hat = new_second / SECOND_BIAS
    new_master = master - 0.001 * (
        first_hat / (jnp.sqrt(second_hat) + 1e-08) + 0.1 * master
    )
    return new_master, new_first, new_second


def merge_kernel(
    grad_hbm, err_hbm, lists_hbm, master_hbm, first_hbm, second_hbm,
    err, weights, result, expand, rooted, starts,
    grad, lists, raw, raw_b, acc, sent, kept, column, value_b,
    packed, from_core, part, got,
    master0, master1, master2, master3, mgot2, mgot3,
    moment0, moment1, moment2, moment3, vgot2, vgot3,
    grad_sem, err_sem, list_sem, raw_sem,
    core_send, core_recv, raw_send, raw_recv, rawb_send, rawb_recv,
    rs_send, rs_recv, ag_send, ag_recv, half_send, half_recv,
    s_send, s_recv, w_send, w_recv, f_send, f_recv, round_z, round_x,
):
    rows = grad.shape[0]
    groups = rows // GROUP
    chunks = rows // CHUNK
    levels, keep_n = lists.shape
    me = lax.axis_index("dp")
    c = me % 2
    y = (me // 2) % 4
    z = (me // 8) % 4
    x = me // 32
    chip = me // 2
    chips = groups
    sibling = me + 1 - 2 * c
    at = {"x": x, "z": z, "y": y}
    strides = {"x": 32, "z": 8, "y": 2}

    def far(k):
        other = (chip + k) % chips
        return other, 2 * other + c

    def along(axis, k):
        return me + ((at[axis] + k) % 4 - at[axis]) * strides[axis]

    def copy(src, dst, send, recv, peer):
        return pltpu.make_async_remote_copy(
            src_ref=src, dst_ref=dst, send_sem=send, recv_sem=recv,
            device_id=(peer,), device_id_type=MESH,
        )

    def each(act):
        def some(i, _):
            for j in range(21):
                act(i * 21 + j + 1)
            return 0

        lax.fori_loop(0, (chips - 1) // 21, some, 0)

    def bytes_of(ref, send, recv):
        return copy(ref, ref, send, recv, sibling)

    state = master0, moment0
    state1 = master1, moment1
    state2 = master2, moment2
    state3 = master3, moment3
    sgot2 = mgot2, vgot2
    sgot3 = mgot3, vgot3

    def greet(semaphore, peers):
        for peer in peers:
            pl.semaphore_signal(
                semaphore, inc=1, device_id=(peer,), device_id_type=MESH
            )

    line = {axis: [along(axis, k) for k in (1, 2, 3)] for axis in "xzy"}
    barrier = pltpu.get_barrier_semaphore()
    greet(barrier, [sibling, *line["y"], *line["z"], *line["x"]])

    list_load = pltpu.make_async_copy(lists_hbm.at[0], lists, list_sem)
    list_load.start()
    for a, source in enumerate((master_hbm, first_hbm, second_hbm)):
        for h in range(2):
            go = pltpu.make_async_copy(
                source.at[:, pl.ds(h * 128, 128)], raw.at[h, a], raw_sem
            )
            go.start()

    def loads(i):
        span = pl.ds(pl.multiple_of(i * CHUNK, CHUNK), CHUNK)
        return (
            pltpu.make_async_copy(grad_hbm.at[0, span], grad.at[span], grad_sem.at[i]),
            pltpu.make_async_copy(err_hbm.at[0, span], err.at[0, span], err_sem.at[i]),
        )

    def load(i, _):
        for go in loads(i):
            go.start()
        return 0

    lax.fori_loop(0, chunks, load, 0)

    parts = (
        ((0,), pl.ds(0, 48)),
        ((1,), pl.ds(0, 48)),
        ((pl.ds(0, 2),), pl.ds(48, 16)),
    )

    def region(s, stage, place, half=None):
        cols, span = parts[s]
        taken = ORDERS[s][: min(stage, 2)]
        index = [pl.ds(0, 4) if axis in taken else place[axis] for axis in "xzy"]
        if half is not None:
            index["xzy".index(taken[0])] = pl.ds(2 * half, 2)
        return weights.at[(*index, c, *cols, span)]

    def stage_bytes(stage, sends, recvs):
        same = (
            weights.at[0, 0, pl.ds(0, 3), c],
            weights.at[0, pl.ds(0, 3), :, c],
            weights.at[pl.ds(0, 2), :, :, c],
            weights.at[0, :, :, c],
        )
        return bytes_of(same[stage], sends.at[stage], recvs.at[stage])

    def spread(stage):
        for s, order in enumerate(ORDERS):
            axis = order[min(stage, 2)]
            for k in (1, 2, 3) if stage < 2 else (1, 3):
                if stage < 3:
                    block = region(s, stage, at)
                else:
                    origin = {**at, axis: (at[axis] + 4 - k) % 4}
                    block = region(s, stage, origin, k // 2)
                copy(
                    block, block, w_send.at[stage], w_recv.at[stage], along(axis, k)
                ).start()

    def arrive(stage):
        stage_bytes(stage, w_send, w_recv).wait_recv()

    def forward(stage):
        for s, order in enumerate(ORDERS):
            axis = order[min(stage, 2)]
            for k in ((1, 2, 3), (1, 2, 3), (1, 3), (2,))[stage]:
                block = region(s, stage, {**at, axis: (at[axis] + k) % 4})
                copy(block, block, f_send, f_recv, sibling).start()

    list_load.wait()

    ids = lists[...]
    high_ids = (ids >> 7).astype(F32)
    low_ids = (ids & 127).astype(F32)

    inner = iota((SPAN // 16, 16, GROUP), 0) * 16 + iota((SPAN // 16, 16, GROUP), 1)
    inner = inner.astype(F32).astype(BF16)
    one = jnp.ones((SPAN // 16, 16, GROUP), BF16)
    zero = jnp.zeros((SPAN // 16, 16, GROUP), BF16)

    def ladder(row, count):
        tiles = count // 16
        near = jnp.broadcast_to(row, (16, GROUP)).astype(BF16)
        hit = jnp.where(inner[:tiles] == near[None], one[:tiles], zero[:tiles])
        return hit.reshape(count, GROUP)

    def member(r):
        spans = [slice(j, j + GROUP) for j in range(0, keep_n, GROUP)]
        high = [ladder(high_ids[r : r + 1, span], groups) for span in spans]
        low = [ladder(low_ids[r : r + 1, span], GROUP) for span in spans]
        return lax.dot_general(
            jnp.concatenate(high, axis=1), jnp.concatenate(low, axis=1),
            (((1,), (1,)), ((), ())), preferred_element_type=F32,
        )

    root = member(levels - 1)
    root_b = root.astype(BF16)
    before = onehot(iota((GROUP, GROUP), 0) < iota((GROUP, GROUP), 1))
    inside = jnp.dot(root_b, before, preferred_element_type=F32)
    total = jnp.dot(root_b, jnp.ones((GROUP, GROUP), BF16), preferred_element_type=F32)
    above = onehot(iota((groups, groups), 1) < iota((groups, groups), 0))
    start = jnp.dot(above, total.astype(BF16), preferred_element_type=F32)
    rank = start + inside
    starts[...] = start.astype(jnp.int32)
    rooted[...] = jnp.where(root > 0.5, rank, -1.0)

    keep = member(0)
    sent[...] = keep
    for r in range(1, levels - 1):
        keep = keep * member(r)
    kept[...] = jnp.where(keep * root > 0.5, rank, -1.0)

    chip_ranks = rooted[pl.ds(chip, 1), :]
    column[...] = jnp.transpose(jnp.broadcast_to(chip_ranks, (GROUP, GROUP)))
    own_rows = pl.ds(pl.multiple_of(c * 64, 64), 64)
    half = column[own_rows, :]
    pltpu.make_async_copy(raw, raw, raw_sem).wait()
    for a in range(2):
        raw_b[:, :, a * 128 : (a + 1) * 128] = raw[:, 1 + a].astype(BF16)
    mine_at = [at[order[0]] for order in STATE_ORDERS]
    master0[mine_at[0], own_rows, :] = raw[c, 0]
    moment0[mine_at[1], own_rows, :] = raw_b[c]

    for h in range(2):
        new_master, _, _ = adamw(raw[h, 0], raw[h, 1], raw[h, 2], 0.0)
        weights[x, z, y, c, h] = jnp.where(half < 0.0, new_master, 0.0).astype(BF16)
    acc[...] = jnp.zeros_like(acc)
    diagonal = iota((GROUP, GROUP), 0) == iota((GROUP, GROUP), 1)

    def pack(i):
        for go in loads(i):
            go.wait()
        each_row = []
        for j in range(CHUNK // GROUP):
            g = i * (CHUNK // GROUP) + j
            span = pl.ds(pl.multiple_of(g * GROUP, GROUP), GROUP)
            value = grad[span, :].astype(F32) + err[0, span, :]
            value_b[j * GROUP : (j + 1) * GROUP, :] = value.astype(BF16)
            each_row.append(kept[pl.ds(g, 1), :])
        for q in range(keep_n // SPAN):
            hits = []
            for row in each_row:
                hits.append(ladder(jnp.clip(row - q * SPAN, -1.0, SPAN), SPAN))
            acc[q * SPAN : (q + 1) * SPAN, :] += jnp.dot(
                jnp.concatenate(hits, axis=1), value_b[...], preferred_element_type=F32
            )

    def settle(i, _):
        for j in range(CHUNK // GROUP):
            g = i * (CHUNK // GROUP) + j
            span = pl.ds(pl.multiple_of(g * GROUP, GROUP), GROUP)
            stays = 1.0 - sent[pl.ds(g, 1), :]
            mask = jnp.dot(
                jnp.where(diagonal, stays, 0.0).astype(BF16),
                jnp.ones((GROUP, err.shape[2]), BF16),
                preferred_element_type=F32,
            )
            err[0, span, :] = (grad[span, :].astype(F32) + err[0, span, :]) * mask
        return 0

    pl.semaphore_wait(barrier, 10)
    greet(round_z, line["z"])

    raw_swaps = [
        copy(
            raw.at[1 - c, 0], state[0].at[mine_at[0], own_rows],
            raw_send, raw_recv, sibling,
        ),
        copy(
            raw_b.at[1 - c], state[1].at[mine_at[1], own_rows],
            rawb_send, rawb_recv, sibling,
        ),
    ]
    for go in raw_swaps:
        go.start()

    pack(0)

    for go in raw_swaps:
        go.wait_recv()
    for a, order in enumerate(STATE_ORDERS):
        block = state[a].at[mine_at[a]]
        for k in (1, 2, 3):
            copy(
                block, block, s_send.at[a], s_recv.at[a], along(order[0], k)
            ).start()

    pl.semaphore_wait(round_z, 3)
    greet(round_x, line["x"])
    spread(0)
    mine = weights.at[x, z, y, c]
    copy(mine, mine, f_send, f_recv, sibling).start()

    pack(1)
    pack(2)
    pack(3)

    def place(a):
        order = STATE_ORDERS[a]
        bytes_of(state[a].at[pl.ds(0, 3)], s_send.at[a], s_recv.at[a]).wait_recv()
        shifts = {"x": 8, "z": 6, "y": 4}
        units = {"x": 16, "z": 4, "y": 1}
        hits = []
        for k in range(4):
            source = chip + (k - at[order[0]]) * units[order[0]]
            ranks = rooted[pl.ds(source, 1), :].astype(jnp.int32)
            first, second, third = ((ranks >> shifts[axis]) & 3 for axis in order)
            here = (ranks >= 0) & (first == at[order[0]])
            spot = second * (4 * UNIT) + third * UNIT + (ranks & (UNIT - 1))
            row = jnp.where(here, spot, -1).astype(F32)
            hits.append(ladder(row, 16 * UNIT))
        hits = jnp.concatenate(hits, axis=1)
        whole = state[a][...].reshape(4 * GROUP, -1)
        if a:
            split = whole
        else:
            high = whole.astype(BF16)
            rest = whole - high.astype(F32)
            middle = rest.astype(BF16)
            low = (rest - middle.astype(F32)).astype(BF16)
            split = jnp.concatenate([high, middle, low], axis=1)
        moved = jnp.dot(hits, split, preferred_element_type=F32)
        if not a:
            moved = (moved[:, :128] + moved[:, 128:256]) + moved[:, 256:]
        state1[a][...] = moved.astype(state1[a].dtype).reshape(state1[a].shape)

    def state_phase(phase, source, target):
        for a, order in enumerate(STATE_ORDERS):
            axis = order[phase]
            n = phase * 2 + a
            for k in (1, 2, 3):
                copy(
                    source[a].at[(at[axis] + k) % 4], target[a].at[k - 1],
                    s_send.at[n], s_recv.at[n], along(axis, k),
                ).start()

    def state_bytes(phase, target, a):
        n = phase * 2 + a
        return bytes_of(target[a], s_send.at[n], s_recv.at[n])

    def state_sum(phase, source, target, total):
        for a in range(2):
            state_bytes(phase, target, a).wait_recv()
        for a, order in enumerate(STATE_ORDERS):
            value = source[a][at[order[phase]]].astype(F32)
            for k in range(3):
                value = value + target[a][k].astype(F32)
            total[a][...] = value.astype(total[a].dtype)

    half_chips = chips // 2
    swaps = []
    for p in range(2):
        ranks = slice(p * keep_n // 2, (p + 1) * keep_n // 2)
        span = pl.ds(p * half_chips, half_chips)
        for h in range(2):
            packed[h, span] = (
                acc[ranks, h * 128 : (h + 1) * 128]
                .astype(BF16)
                .reshape(half_chips, UNIT, 128)
            )
        swap = copy(
            packed.at[1 - c, span], from_core.at[span],
            core_send.at[p], core_recv.at[p], sibling,
        )
        swap.start()
        swaps.append(swap)

    arrive(0)
    spread(1)
    for a in range(2):
        place(a)
    state_phase(1, state1, sgot2)
    pl.semaphore_wait(round_x, 3)


    def scatter(k):
        other, peer = far(k)
        return copy(part.at[other], got.at[k - 1], rs_send, rs_recv, peer)

    for p in range(2):
        swaps[p].wait_recv()
        span = pl.ds(p * half_chips, half_chips)
        part[span] = (packed[c, span].astype(F32) + from_core[span].astype(F32)).astype(
            BF16
        )

    each(lambda k: scatter(k).start())
    own = packed[c, chip].astype(F32) + from_core[chip].astype(F32)
    forward(0)

    state_sum(1, state1, sgot2, state2)
    state_phase(2, state2, sgot3)

    arrive(1)
    spread(2)
    forward(1)

    for k in range(keep_n // GROUP):
        lanes = (iota((64, GROUP), 1) + k * GROUP).astype(F32)
        expand[:, k * GROUP : (k + 1) * GROUP] = onehot(half == lanes)

    state_sum(2, state2, sgot3, state3)
    scattered = bytes_of(got, rs_send, rs_recv)
    scattered.wait_recv()
    summed = (own + jnp.sum(got[...].astype(F32), axis=0)).astype(BF16)
    new_master, _, _ = adamw(
        master3[...], moment3[:, :128].astype(F32), moment3[:, 128:].astype(F32),
        summed.astype(F32),
    )
    result[c, chip, 0] = summed
    result[c, chip, 1] = new_master.astype(BF16)

    plane = chips // 4

    def gather(k):
        unit = result.at[c, chip]
        return copy(unit, unit, ag_send, ag_recv.at[x], far(k)[1])

    def pass_on(q):
        block = result.at[c, pl.ds(q * plane, plane)]
        return copy(block, block, half_send, half_recv, sibling)

    each(lambda k: gather(k).start())
    arrive(2)
    spread(3)
    forward(2)
    lax.fori_loop(0, chunks, settle, 0)

    for k in (3, 2, 1):
        q = (x + k) % 4
        block = result.at[c, pl.ds(q * plane, plane)]
        bytes_of(block, ag_send, ag_recv.at[q]).wait_recv()
        pass_on(q).start()
    bytes_of(result.at[c, pl.ds(0, plane - 1)], ag_send, ag_recv.at[x]).wait_recv()
    pass_on(x).start()

    arrive(3)
    forward(3)

    scattered.wait_send()
    bytes_of(result.at[c, pl.ds(0, chips - 1)], ag_send, ag_recv.at[x]).wait_send()
    for go in raw_swaps:
        go.wait_send()
    for go in swaps:
        go.wait_send()
    for a in range(2):
        bytes_of(state[a].at[pl.ds(0, 3)], s_send.at[a], s_recv.at[a]).wait_send()
        state_bytes(1, sgot2, a).wait_send()
        state_bytes(2, sgot3, a).wait_send()
    for stage in range(4):
        stage_bytes(stage, w_send, w_recv).wait_send()
    bytes_of(weights.at[:, :, :, c], f_send, f_recv).wait()
    bytes_of(result.at[c], half_send, half_recv).wait()


def finish_kernel(
    err, weights, result, expand, rooted, starts_v, master, first, second,
    err_hbm, out_hbm, new_master, new_first, new_second,
    out, starts, err_sem, out_sem, starts_sem,
):
    groups = rooted.shape[0]
    to_smem = pltpu.make_async_copy(starts_v, starts, starts_sem)
    to_smem.start()
    rows = err.shape[1]
    pieces = err_sem.shape[0]
    copies = []
    for i in range(pieces):
        span = pl.ds(i * (rows // pieces), rows // pieces)
        go = pltpu.make_async_copy(err.at[0, span], err_hbm.at[0, span], err_sem.at[i])
        go.start()
        copies.append(go)

    to_smem.wait()
    units = result.shape[1]
    window = GROUP // UNIT + 1
    batch = groups // out_sem.shape[0]

    def store(i):
        span = pl.ds(i * batch, batch)
        return pltpu.make_async_copy(out.at[span], out_hbm.at[span], out_sem.at[i])

    def fill(i, _):
        for j in range(batch):
            g = i * batch + j
            unit = jnp.minimum(starts[g, 0] // UNIT, units - window)
            near = rooted[pl.ds(g, 1), :] - (unit * UNIT).astype(F32)
            hits = onehot(iota((window * UNIT, GROUP), 0).astype(F32) == near)
            held = jnp.concatenate(
                [
                    result[h, pl.ds(unit, window), 1].reshape(window * UNIT, 128)
                    for h in range(2)
                ],
                axis=1,
            )
            moved = lax.dot_general(
                hits, held, (((0,), (0,)), ((), ())), preferred_element_type=F32
            ).astype(BF16)
            for c in range(2):
                span = slice(c * 64, c * 64 + 64)
                for h in range(2):
                    lanes = slice(h * 128, h * 128 + 128)
                    out[g, span, lanes] = weights[g, c, h] + moved[span, lanes]
        store(i).start()
        return 0

    steps = out_sem.shape[0]
    lax.fori_loop(0, steps, fill, 0)
    total = jnp.concatenate(
        [
            jnp.dot(
                expand[...], result[h, :, 0].reshape(-1, 128),
                preferred_element_type=F32,
            )
            for h in range(2)
        ],
        axis=1,
    )
    new_master[...], new_first[...], new_second[...] = adamw(
        master[...], first[...], second[...], total
    )

    for go in copies:
        go.wait()
    lax.fori_loop(0, steps, lambda i, _: (store(i).wait(), 0)[1], 0)


def body(gradients, error_memory, block_lists, master, first_moment, second_moment):
    _, rows, width = gradients.shape
    owned = master.shape[0]
    levels, keep_n = block_lists.shape[1:]
    groups = rows // GROUP
    chunks = rows // CHUNK
    vmem = pl.BlockSpec(memory_space=pltpu.VMEM)
    anywhere = pl.BlockSpec(memory_space=pl.ANY)
    dma = pltpu.SemaphoreType.DMA

    err, weights, result, expand, rooted, starts = pl.pallas_call(
        merge_kernel,
        out_shape=(
            pltpu.VMEM((1, rows, width), F32),
            pltpu.VMEM((4, 4, 4, 2, 2, owned, 128), BF16),
            pltpu.VMEM((2, groups, 2, UNIT, 128), BF16),
            pltpu.VMEM((owned, keep_n), BF16),
            pltpu.VMEM((groups, GROUP), F32),
            pltpu.VMEM((groups, GROUP), jnp.int32),
        ),
        in_specs=[anywhere] * 6,
        out_specs=(vmem,) * 6,
        scratch_shapes=[
            pltpu.VMEM((rows, width), BF16),
            pltpu.VMEM((levels, keep_n), jnp.int32),
            pltpu.VMEM((2, 3, owned, 128), F32),
            pltpu.VMEM((2, owned, 256), BF16),
            pltpu.VMEM((keep_n, width), F32),
            pltpu.VMEM((groups, GROUP), F32),
            pltpu.VMEM((groups, GROUP), F32),
            pltpu.VMEM((GROUP, GROUP), F32),
            pltpu.VMEM((CHUNK, width), BF16),
            pltpu.VMEM((2, groups, UNIT, 128), BF16),
            pltpu.VMEM((groups, UNIT, 128), BF16),
            pltpu.VMEM((groups, UNIT, 128), BF16),
            pltpu.VMEM((groups - 1, UNIT, 128), BF16),
            *(
                pltpu.VMEM((*shape, lanes), kind)
                for lanes, kind in ((128, F32), (256, BF16))
                for shape in (
                    (4, GROUP), (4, 4, UNIT), (4, UNIT), (UNIT,),
                    (3, 4, UNIT), (3, UNIT),
                )
            ),
            dma((chunks,)), dma((chunks,)), dma, dma,
            dma((2,)), dma((2,)), dma, dma, dma, dma,
            dma, dma, dma, dma((4,)), dma, dma,
            dma((6,)), dma((6,)),
            dma((4,)), dma((4,)), dma, dma,
            pltpu.SemaphoreType.REGULAR, pltpu.SemaphoreType.REGULAR,
        ],
        compiler_params=pltpu.CompilerParams(
            collective_id=0, has_side_effects=True, vmem_limit_bytes=46 * MIB
        ),
        name="merge",
    )(gradients, error_memory, block_lists, master, first_moment, second_moment)

    new_errors, out, new_master, new_first, new_second = pl.pallas_call(
        finish_kernel,
        out_shape=(
            jax.ShapeDtypeStruct((1, rows, width), F32),
            jax.ShapeDtypeStruct((groups, GROUP, width), BF16),
            jax.ShapeDtypeStruct((owned, width), F32),
            jax.ShapeDtypeStruct((owned, width), F32),
            jax.ShapeDtypeStruct((owned, width), F32),
        ),
        in_specs=[vmem] * 9,
        out_specs=(anywhere, anywhere, vmem, vmem, vmem),
        scratch_shapes=[
            pltpu.VMEM((groups, GROUP, width), BF16),
            pltpu.SMEM((groups, GROUP), jnp.int32),
            dma((4,)), dma((8,)), dma,
        ],
        compiler_params=pltpu.CompilerParams(vmem_limit_bytes=32 * MIB),
        name="finish",
    )(
        err, weights.reshape(groups, 2, 2, owned, 128), result, expand, rooted, starts,
        master, first_moment, second_moment,
    )
    return new_errors, new_master, new_first, new_second, out.reshape(rows, width)


def solution(mesh):
    in_specs = (
        P("dp", None, None),
        P("dp", None, None),
        P("dp", None, None),
        P("dp", None),
        P("dp", None),
        P("dp", None),
    )
    out_specs = (P("dp", None, None), P("dp", None), P("dp", None), P("dp", None), P())
    return jax.shard_map(
        body, mesh=mesh, in_specs=in_specs, out_specs=out_specs, check_vma=False
    )
```

```python
import jax
import jax.numpy as jnp
from jax import lax
from jax.experimental import pallas as pl
from jax.experimental.pallas import tpu as pltpu
from jax.sharding import PartitionSpec as P

FIRST_BIAS = 0.9999734386011124
SECOND_BIAS = 0.09520785288629036
MESH = pl.DeviceIdType.MESH
F32 = jnp.float32
BF16 = jnp.bfloat16
MIB = 1 << 20

GROUP = 128
CHUNK = 2048
UNIT = 16
SPAN = 256

ORDERS = ("xzy", "zyx", "yxz")
STATE_ORDERS = ("zyx", "xzy")


def iota(shape, dim):
    return lax.broadcasted_iota(jnp.int32, shape, dim)


def onehot(hits):
    return jnp.where(hits, 1.0, 0.0).astype(BF16)


def adamw(master, first, second, summed):
    new_first = 0.9 * first + 0.1 * summed
    new_second = 0.999 * second + 0.001 * summed * summed
    first_hat = new_first / FIRST_BIAS
    second_hat = new_second / SECOND_BIAS
    new_master = master - 0.001 * (
        first_hat / (jnp.sqrt(second_hat) + 1e-08) + 0.1 * master
    )
    return new_master, new_first, new_second


def merge_kernel(
    grad_hbm, err_hbm, lists_hbm, master_hbm, first_hbm, second_hbm,
    err, weights, result, expand, rooted, starts,
    grad, lists, raw, raw_b, acc, sent, kept, column, value_b,
    packed, from_core, part, got,
    master0, master1, master2, master3, mgot2, mgot3,
    moment0, moment1, moment2, moment3, vgot2, vgot3,
    grad_sem, err_sem, list_sem, raw_sem,
    core_send, core_recv, raw_send, raw_recv, rawb_send, rawb_recv,
    rs_send, rs_recv, ag_send, ag_recv, half_send, half_recv,
    s_send, s_recv, w_send, w_recv, f_send, f_recv, round_z, round_x,
):
    rows = grad.shape[0]
    groups = rows // GROUP
    chunks = rows // CHUNK
    levels, keep_n = lists.shape
    me = lax.axis_index("dp")
    c = me % 2
    y = (me // 2) % 4
    z = (me // 8) % 4
    x = me // 32
    chip = me // 2
    chips = groups
    sibling = me + 1 - 2 * c
    at = {"x": x, "z": z, "y": y}
    strides = {"x": 32, "z": 8, "y": 2}

    def far(k):
        other = (chip + k) % chips
        return other, 2 * other + c

    def along(axis, k):
        return me + ((at[axis] + k) % 4 - at[axis]) * strides[axis]

    def copy(src, dst, send, recv, peer):
        return pltpu.make_async_remote_copy(
            src_ref=src, dst_ref=dst, send_sem=send, recv_sem=recv,
            device_id=(peer,), device_id_type=MESH,
        )

    def each(act):
        def some(i, _):
            for j in range(21):
                act(i * 21 + j + 1)
            return 0

        lax.fori_loop(0, (chips - 1) // 21, some, 0)

    def bytes_of(ref, send, recv):
        return copy(ref, ref, send, recv, sibling)

    state = master0, moment0
    state1 = master1, moment1
    state2 = master2, moment2
    state3 = master3, moment3
    sgot2 = mgot2, vgot2
    sgot3 = mgot3, vgot3

    def greet(semaphore, peers):
        for peer in peers:
            pl.semaphore_signal(
                semaphore, inc=1, device_id=(peer,), device_id_type=MESH
            )

    line = {axis: [along(axis, k) for k in (1, 2, 3)] for axis in "xzy"}
    barrier = pltpu.get_barrier_semaphore()
    greet(barrier, [sibling, *line["y"], *line["z"], *line["x"]])

    list_load = pltpu.make_async_copy(lists_hbm.at[0], lists, list_sem)
    list_load.start()
    for a, source in enumerate((master_hbm, first_hbm, second_hbm)):
        for h in range(2):
            go = pltpu.make_async_copy(
                source.at[:, pl.ds(h * 128, 128)], raw.at[h, a], raw_sem
            )
            go.start()

    def loads(i):
        span = pl.ds(pl.multiple_of(i * CHUNK, CHUNK), CHUNK)
        return (
            pltpu.make_async_copy(grad_hbm.at[0, span], grad.at[span], grad_sem.at[i]),
            pltpu.make_async_copy(err_hbm.at[0, span], err.at[0, span], err_sem.at[i]),
        )

    def load(i, _):
        for go in loads(i):
            go.start()
        return 0

    lax.fori_loop(0, chunks, load, 0)

    parts = (
        ((0,), pl.ds(0, 48)),
        ((1,), pl.ds(0, 48)),
        ((pl.ds(0, 2),), pl.ds(48, 16)),
    )

    def region(s, stage, place, half=None):
        cols, span = parts[s]
        taken = ORDERS[s][: min(stage, 2)]
        index = [pl.ds(0, 4) if axis in taken else place[axis] for axis in "xzy"]
        if half is not None:
            index["xzy".index(taken[0])] = pl.ds(2 * half, 2)
        return weights.at[(*index, c, *cols, span)]

    def stage_bytes(stage, sends, recvs):
        same = (
            weights.at[0, 0, pl.ds(0, 3), c],
            weights.at[0, pl.ds(0, 3), :, c],
            weights.at[pl.ds(0, 2), :, :, c],
            weights.at[0, :, :, c],
        )
        return bytes_of(same[stage], sends.at[stage], recvs.at[stage])

    def spread(stage):
        for s, order in enumerate(ORDERS):
            axis = order[min(stage, 2)]
            for k in (1, 2, 3) if stage < 2 else (1, 3):
                if stage < 3:
                    block = region(s, stage, at)
                else:
                    origin = {**at, axis: (at[axis] + 4 - k) % 4}
                    block = region(s, stage, origin, k // 2)
                copy(
                    block, block, w_send.at[stage], w_recv.at[stage], along(axis, k)
                ).start()

    def arrive(stage):
        stage_bytes(stage, w_send, w_recv).wait_recv()

    def forward(stage):
        for s, order in enumerate(ORDERS):
            axis = order[min(stage, 2)]
            for k in ((1, 2, 3), (1, 2, 3), (1, 3), (2,))[stage]:
                block = region(s, stage, {**at, axis: (at[axis] + k) % 4})
                copy(block, block, f_send, f_recv, sibling).start()

    list_load.wait()

    ids = lists[...]
    high_ids = (ids >> 7).astype(F32)
    low_ids = (ids & 127).astype(F32)

    inner = iota((SPAN // 16, 16, GROUP), 0) * 16 + iota((SPAN // 16, 16, GROUP), 1)
    inner = inner.astype(F32).astype(BF16)
    one = jnp.ones((SPAN // 16, 16, GROUP), BF16)
    zero = jnp.zeros((SPAN // 16, 16, GROUP), BF16)

    def ladder(row, count):
        tiles = count // 16
        near = jnp.broadcast_to(row, (16, GROUP)).astype(BF16)
        hit = jnp.where(inner[:tiles] == near[None], one[:tiles], zero[:tiles])
        return hit.reshape(count, GROUP)

    def member(r):
        spans = [slice(j, j + GROUP) for j in range(0, keep_n, GROUP)]
        high = [ladder(high_ids[r : r + 1, span], groups) for span in spans]
        low = [ladder(low_ids[r : r + 1, span], GROUP) for span in spans]
        return lax.dot_general(
            jnp.concatenate(high, axis=1), jnp.concatenate(low, axis=1),
            (((1,), (1,)), ((), ())), preferred_element_type=F32,
        )

    root = member(levels - 1)
    root_b = root.astype(BF16)
    before = onehot(iota((GROUP, GROUP), 0) < iota((GROUP, GROUP), 1))
    inside = jnp.dot(root_b, before, preferred_element_type=F32)
    total = jnp.dot(root_b, jnp.ones((GROUP, GROUP), BF16), preferred_element_type=F32)
    above = onehot(iota((groups, groups), 1) < iota((groups, groups), 0))
    start = jnp.dot(above, total.astype(BF16), preferred_element_type=F32)
    rank = start + inside
    starts[...] = start.astype(jnp.int32)
    rooted[...] = jnp.where(root > 0.5, rank, -1.0)

    keep = member(0)
    sent[...] = keep
    for r in range(1, levels - 1):
        keep = keep * member(r)
    kept[...] = jnp.where(keep * root > 0.5, rank, -1.0)

    chip_ranks = rooted[pl.ds(chip, 1), :]
    column[...] = jnp.transpose(jnp.broadcast_to(chip_ranks, (GROUP, GROUP)))
    own_rows = pl.ds(pl.multiple_of(c * 64, 64), 64)
    half = column[own_rows, :]
    pltpu.make_async_copy(raw, raw, raw_sem).wait()
    for a in range(2):
        raw_b[:, :, a * 128 : (a + 1) * 128] = raw[:, 1 + a].astype(BF16)
    mine_at = [at[order[0]] for order in STATE_ORDERS]
    master0[mine_at[0], own_rows, :] = raw[c, 0]
    moment0[mine_at[1], own_rows, :] = raw_b[c]

    for h in range(2):
        new_master, _, _ = adamw(raw[h, 0], raw[h, 1], raw[h, 2], 0.0)
        weights[x, z, y, c, h] = jnp.where(half < 0.0, new_master, 0.0).astype(BF16)
    acc[...] = jnp.zeros_like(acc)
    diagonal = iota((GROUP, GROUP), 0) == iota((GROUP, GROUP), 1)

    def pack(i):
        for go in loads(i):
            go.wait()
        each_row = []
        for j in range(CHUNK // GROUP):
            g = i * (CHUNK // GROUP) + j
            span = pl.ds(pl.multiple_of(g * GROUP, GROUP), GROUP)
            value = grad[span, :].astype(F32) + err[0, span, :]
            value_b[j * GROUP : (j + 1) * GROUP, :] = value.astype(BF16)
            each_row.append(kept[pl.ds(g, 1), :])
        for q in range(keep_n // SPAN):
            hits = []
            for row in each_row:
                hits.append(ladder(jnp.clip(row - q * SPAN, -1.0, SPAN), SPAN))
            acc[q * SPAN : (q + 1) * SPAN, :] += jnp.dot(
                jnp.concatenate(hits, axis=1), value_b[...], preferred_element_type=F32
            )

    def settle(i, _):
        for j in range(CHUNK // GROUP):
            g = i * (CHUNK // GROUP) + j
            span = pl.ds(pl.multiple_of(g * GROUP, GROUP), GROUP)
            stays = 1.0 - sent[pl.ds(g, 1), :]
            mask = jnp.dot(
                jnp.where(diagonal, stays, 0.0).astype(BF16),
                jnp.ones((GROUP, err.shape[2]), BF16),
                preferred_element_type=F32,
            )
            err[0, span, :] = (grad[span, :].astype(F32) + err[0, span, :]) * mask
        return 0

    pl.semaphore_wait(barrier, 10)
    greet(round_z, line["z"])

    raw_swaps = [
        copy(
            raw.at[1 - c, 0], state[0].at[mine_at[0], own_rows],
            raw_send, raw_recv, sibling,
        ),
        copy(
            raw_b.at[1 - c], state[1].at[mine_at[1], own_rows],
            rawb_send, rawb_recv, sibling,
        ),
    ]
    for go in raw_swaps:
        go.start()

    spread(0)
    mine = weights.at[x, z, y, c]
    copy(mine, mine, f_send, f_recv, sibling).start()

    pack(0)

    for go in raw_swaps:
        go.wait_recv()
    for a, order in enumerate(STATE_ORDERS):
        block = state[a].at[mine_at[a]]
        for k in (1, 2, 3):
            copy(
                block, block, s_send.at[a], s_recv.at[a], along(order[0], k)
            ).start()

    pl.semaphore_wait(round_z, 3)
    greet(round_x, line["x"])
    pack(1)
    pack(2)

    arrive(0)
    spread(1)
    pack(3)

    def place(a):
        order = STATE_ORDERS[a]
        bytes_of(state[a].at[pl.ds(0, 3)], s_send.at[a], s_recv.at[a]).wait_recv()
        shifts = {"x": 8, "z": 6, "y": 4}
        units = {"x": 16, "z": 4, "y": 1}
        hits = []
        for k in range(4):
            source = chip + (k - at[order[0]]) * units[order[0]]
            ranks = rooted[pl.ds(source, 1), :].astype(jnp.int32)
            first, second, third = ((ranks >> shifts[axis]) & 3 for axis in order)
            here = (ranks >= 0) & (first == at[order[0]])
            spot = second * (4 * UNIT) + third * UNIT + (ranks & (UNIT - 1))
            row = jnp.where(here, spot, -1).astype(F32)
            hits.append(ladder(row, 16 * UNIT))
        hits = jnp.concatenate(hits, axis=1)
        whole = state[a][...].reshape(4 * GROUP, -1)
        if a:
            split = whole
        else:
            high = whole.astype(BF16)
            rest = whole - high.astype(F32)
            middle = rest.astype(BF16)
            low = (rest - middle.astype(F32)).astype(BF16)
            split = jnp.concatenate([high, middle, low], axis=1)
        moved = jnp.dot(hits, split, preferred_element_type=F32)
        if not a:
            moved = (moved[:, :128] + moved[:, 128:256]) + moved[:, 256:]
        state1[a][...] = moved.astype(state1[a].dtype).reshape(state1[a].shape)

    def state_phase(phase, source, target):
        for a, order in enumerate(STATE_ORDERS):
            axis = order[phase]
            n = phase * 2 + a
            for k in (1, 2, 3):
                copy(
                    source[a].at[(at[axis] + k) % 4], target[a].at[k - 1],
                    s_send.at[n], s_recv.at[n], along(axis, k),
                ).start()

    def state_bytes(phase, target, a):
        n = phase * 2 + a
        return bytes_of(target[a], s_send.at[n], s_recv.at[n])

    def state_sum(phase, source, target, total):
        for a in range(2):
            state_bytes(phase, target, a).wait_recv()
        for a, order in enumerate(STATE_ORDERS):
            value = source[a][at[order[phase]]].astype(F32)
            for k in range(3):
                value = value + target[a][k].astype(F32)
            total[a][...] = value.astype(total[a].dtype)

    half_chips = chips // 2
    swaps = []
    for p in range(2):
        ranks = slice(p * keep_n // 2, (p + 1) * keep_n // 2)
        span = pl.ds(p * half_chips, half_chips)
        for h in range(2):
            packed[h, span] = (
                acc[ranks, h * 128 : (h + 1) * 128]
                .astype(BF16)
                .reshape(half_chips, UNIT, 128)
            )
        swap = copy(
            packed.at[1 - c, span], from_core.at[span],
            core_send.at[p], core_recv.at[p], sibling,
        )
        swap.start()
        swaps.append(swap)

    for a in range(2):
        place(a)
    state_phase(1, state1, sgot2)
    pl.semaphore_wait(round_x, 3)


    def scatter(k):
        other, peer = far(k)
        return copy(part.at[other], got.at[k - 1], rs_send, rs_recv, peer)

    for p in range(2):
        swaps[p].wait_recv()
        span = pl.ds(p * half_chips, half_chips)
        part[span] = (packed[c, span].astype(F32) + from_core[span].astype(F32)).astype(
            BF16
        )

    each(lambda k: scatter(k).start())
    own = packed[c, chip].astype(F32) + from_core[chip].astype(F32)
    forward(0)

    state_sum(1, state1, sgot2, state2)
    state_phase(2, state2, sgot3)

    arrive(1)
    spread(2)
    forward(1)

    for k in range(keep_n // GROUP):
        lanes = (iota((64, GROUP), 1) + k * GROUP).astype(F32)
        expand[:, k * GROUP : (k + 1) * GROUP] = onehot(half == lanes)

    state_sum(2, state2, sgot3, state3)
    scattered = bytes_of(got, rs_send, rs_recv)
    scattered.wait_recv()
    summed = (own + jnp.sum(got[...].astype(F32), axis=0)).astype(BF16)
    new_master, _, _ = adamw(
        master3[...], moment3[:, :128].astype(F32), moment3[:, 128:].astype(F32),
        summed.astype(F32),
    )
    result[c, chip, 0] = summed
    result[c, chip, 1] = new_master.astype(BF16)

    plane = chips // 4

    def gather(k):
        unit = result.at[c, chip]
        return copy(unit, unit, ag_send, ag_recv.at[x], far(k)[1])

    def pass_on(q):
        block = result.at[c, pl.ds(q * plane, plane)]
        return copy(block, block, half_send, half_recv, sibling)

    each(lambda k: gather(k).start())
    arrive(2)
    spread(3)
    forward(2)
    lax.fori_loop(0, chunks, settle, 0)

    for k in (3, 2, 1):
        q = (x + k) % 4
        block = result.at[c, pl.ds(q * plane, plane)]
        bytes_of(block, ag_send, ag_recv.at[q]).wait_recv()
        pass_on(q).start()
    bytes_of(result.at[c, pl.ds(0, plane - 1)], ag_send, ag_recv.at[x]).wait_recv()
    pass_on(x).start()

    arrive(3)
    forward(3)

    scattered.wait_send()
    bytes_of(result.at[c, pl.ds(0, chips - 1)], ag_send, ag_recv.at[x]).wait_send()
    for go in raw_swaps:
        go.wait_send()
    for go in swaps:
        go.wait_send()
    for a in range(2):
        bytes_of(state[a].at[pl.ds(0, 3)], s_send.at[a], s_recv.at[a]).wait_send()
        state_bytes(1, sgot2, a).wait_send()
        state_bytes(2, sgot3, a).wait_send()
    for stage in range(4):
        stage_bytes(stage, w_send, w_recv).wait_send()
    bytes_of(weights.at[:, :, :, c], f_send, f_recv).wait()
    bytes_of(result.at[c], half_send, half_recv).wait()


def finish_kernel(
    err, weights, result, expand, rooted, starts_v, master, first, second,
    err_hbm, out_hbm, new_master, new_first, new_second,
    out, starts, err_sem, out_sem, starts_sem,
):
    groups = rooted.shape[0]
    to_smem = pltpu.make_async_copy(starts_v, starts, starts_sem)
    to_smem.start()
    rows = err.shape[1]
    pieces = err_sem.shape[0]
    copies = []
    for i in range(pieces):
        span = pl.ds(i * (rows // pieces), rows // pieces)
        go = pltpu.make_async_copy(err.at[0, span], err_hbm.at[0, span], err_sem.at[i])
        go.start()
        copies.append(go)

    to_smem.wait()
    units = result.shape[1]
    window = GROUP // UNIT + 1
    batch = groups // out_sem.shape[0]

    def store(i):
        span = pl.ds(i * batch, batch)
        return pltpu.make_async_copy(out.at[span], out_hbm.at[span], out_sem.at[i])

    def fill(i, _):
        for j in range(batch):
            g = i * batch + j
            unit = jnp.minimum(starts[g, 0] // UNIT, units - window)
            near = rooted[pl.ds(g, 1), :] - (unit * UNIT).astype(F32)
            hits = onehot(iota((window * UNIT, GROUP), 0).astype(F32) == near)
            held = jnp.concatenate(
                [
                    result[h, pl.ds(unit, window), 1].reshape(window * UNIT, 128)
                    for h in range(2)
                ],
                axis=1,
            )
            moved = lax.dot_general(
                hits, held, (((0,), (0,)), ((), ())), preferred_element_type=F32
            ).astype(BF16)
            for c in range(2):
                span = slice(c * 64, c * 64 + 64)
                for h in range(2):
                    lanes = slice(h * 128, h * 128 + 128)
                    out[g, span, lanes] = weights[g, c, h] + moved[span, lanes]
        store(i).start()
        return 0

    steps = out_sem.shape[0]
    lax.fori_loop(0, steps, fill, 0)
    total = jnp.concatenate(
        [
            jnp.dot(
                expand[...], result[h, :, 0].reshape(-1, 128),
                preferred_element_type=F32,
            )
            for h in range(2)
        ],
        axis=1,
    )
    new_master[...], new_first[...], new_second[...] = adamw(
        master[...], first[...], second[...], total
    )

    for go in copies:
        go.wait()
    lax.fori_loop(0, steps, lambda i, _: (store(i).wait(), 0)[1], 0)


def body(gradients, error_memory, block_lists, master, first_moment, second_moment):
    _, rows, width = gradients.shape
    owned = master.shape[0]
    levels, keep_n = block_lists.shape[1:]
    groups = rows // GROUP
    chunks = rows // CHUNK
    vmem = pl.BlockSpec(memory_space=pltpu.VMEM)
    anywhere = pl.BlockSpec(memory_space=pl.ANY)
    dma = pltpu.SemaphoreType.DMA

    err, weights, result, expand, rooted, starts = pl.pallas_call(
        merge_kernel,
        out_shape=(
            pltpu.VMEM((1, rows, width), F32),
            pltpu.VMEM((4, 4, 4, 2, 2, owned, 128), BF16),
            pltpu.VMEM((2, groups, 2, UNIT, 128), BF16),
            pltpu.VMEM((owned, keep_n), BF16),
            pltpu.VMEM((groups, GROUP), F32),
            pltpu.VMEM((groups, GROUP), jnp.int32),
        ),
        in_specs=[anywhere] * 6,
        out_specs=(vmem,) * 6,
        scratch_shapes=[
            pltpu.VMEM((rows, width), BF16),
            pltpu.VMEM((levels, keep_n), jnp.int32),
            pltpu.VMEM((2, 3, owned, 128), F32),
            pltpu.VMEM((2, owned, 256), BF16),
            pltpu.VMEM((keep_n, width), F32),
            pltpu.VMEM((groups, GROUP), F32),
            pltpu.VMEM((groups, GROUP), F32),
            pltpu.VMEM((GROUP, GROUP), F32),
            pltpu.VMEM((CHUNK, width), BF16),
            pltpu.VMEM((2, groups, UNIT, 128), BF16),
            pltpu.VMEM((groups, UNIT, 128), BF16),
            pltpu.VMEM((groups, UNIT, 128), BF16),
            pltpu.VMEM((groups - 1, UNIT, 128), BF16),
            *(
                pltpu.VMEM((*shape, lanes), kind)
                for lanes, kind in ((128, F32), (256, BF16))
                for shape in (
                    (4, GROUP), (4, 4, UNIT), (4, UNIT), (UNIT,),
                    (3, 4, UNIT), (3, UNIT),
                )
            ),
            dma((chunks,)), dma((chunks,)), dma, dma,
            dma((2,)), dma((2,)), dma, dma, dma, dma,
            dma, dma, dma, dma((4,)), dma, dma,
            dma((6,)), dma((6,)),
            dma((4,)), dma((4,)), dma, dma,
            pltpu.SemaphoreType.REGULAR, pltpu.SemaphoreType.REGULAR,
        ],
        compiler_params=pltpu.CompilerParams(
            collective_id=0, has_side_effects=True, vmem_limit_bytes=46 * MIB
        ),
        name="merge",
    )(gradients, error_memory, block_lists, master, first_moment, second_moment)

    new_errors, out, new_master, new_first, new_second = pl.pallas_call(
        finish_kernel,
        out_shape=(
            jax.ShapeDtypeStruct((1, rows, width), F32),
            jax.ShapeDtypeStruct((groups, GROUP, width), BF16),
            jax.ShapeDtypeStruct((owned, width), F32),
            jax.ShapeDtypeStruct((owned, width), F32),
            jax.ShapeDtypeStruct((owned, width), F32),
        ),
        in_specs=[vmem] * 9,
        out_specs=(anywhere, anywhere, vmem, vmem, vmem),
        scratch_shapes=[
            pltpu.VMEM((groups, GROUP, width), BF16),
            pltpu.SMEM((groups, GROUP), jnp.int32),
            dma((4,)), dma((8,)), dma,
        ],
        compiler_params=pltpu.CompilerParams(vmem_limit_bytes=32 * MIB),
        name="finish",
    )(
        err, weights.reshape(groups, 2, 2, owned, 128), result, expand, rooted, starts,
        master, first_moment, second_moment,
    )
    return new_errors, new_master, new_first, new_second, out.reshape(rows, width)


def solution(mesh):
    in_specs = (
        P("dp", None, None),
        P("dp", None, None),
        P("dp", None, None),
        P("dp", None),
        P("dp", None),
        P("dp", None),
    )
    out_specs = (P("dp", None, None), P("dp", None), P("dp", None), P("dp", None), P())
    return jax.shard_map(
        body, mesh=mesh, in_specs=in_specs, out_specs=out_specs, check_vma=False
    )
```

```python
import jax
import jax.numpy as jnp
from jax import lax
from jax.experimental import pallas as pl
from jax.experimental.pallas import tpu as pltpu
from jax.sharding import PartitionSpec as P

FIRST_BIAS = 0.9999734386011124
SECOND_BIAS = 0.09520785288629036
MESH = pl.DeviceIdType.MESH
F32 = jnp.float32
BF16 = jnp.bfloat16
MIB = 1 << 20

GROUP = 128
CHUNK = 2048
UNIT = 16
SPAN = 256

ORDERS = ("xzy", "zyx", "yxz")
STATE_ORDERS = ("zyx", "xzy")


def iota(shape, dim):
    return lax.broadcasted_iota(jnp.int32, shape, dim)


def onehot(hits):
    return jnp.where(hits, 1.0, 0.0).astype(BF16)


def adamw(master, first, second, summed):
    new_first = 0.9 * first + 0.1 * summed
    new_second = 0.999 * second + 0.001 * summed * summed
    first_hat = new_first / FIRST_BIAS
    second_hat = new_second / SECOND_BIAS
    new_master = master - 0.001 * (
        first_hat / (jnp.sqrt(second_hat) + 1e-08) + 0.1 * master
    )
    return new_master, new_first, new_second


def merge_kernel(
    grad_hbm, err_hbm, lists_hbm, master_hbm, first_hbm, second_hbm,
    err, weights, result, expand, rooted, starts,
    grad, lists, raw, raw_b, acc, sent, kept, column, value_b,
    packed, from_core, part, got,
    master0, master1, master2, master3, mgot2, mgot3,
    moment0, moment1, moment2, moment3, vgot2, vgot3,
    grad_sem, err_sem, list_sem, raw_sem,
    core_send, core_recv, raw_send, raw_recv, rawb_send, rawb_recv,
    rs_send, rs_recv, ag_send, ag_recv, half_send, half_recv,
    s_send, s_recv, w_send, w_recv, f_send, f_recv, round_z, round_x,
):
    rows = grad.shape[0]
    groups = rows // GROUP
    chunks = rows // CHUNK
    levels, keep_n = lists.shape
    me = lax.axis_index("dp")
    c = me % 2
    y = (me // 2) % 4
    z = (me // 8) % 4
    x = me // 32
    chip = me // 2
    chips = groups
    sibling = me + 1 - 2 * c
    at = {"x": x, "z": z, "y": y}
    strides = {"x": 32, "z": 8, "y": 2}

    def far(k):
        other = (x + k // 16) % 4 * 16 + (z + k // 4 % 4) % 4 * 4 + (y + k % 4) % 4
        return other, 2 * other + c

    away = (2, 1, 3, 0)
    offsets = [16 * i + 4 * j + k for i in away for j in away for k in away][:-1]

    def along(axis, k):
        return me + ((at[axis] + k) % 4 - at[axis]) * strides[axis]

    def copy(src, dst, send, recv, peer):
        return pltpu.make_async_remote_copy(
            src_ref=src, dst_ref=dst, send_sem=send, recv_sem=recv,
            device_id=(peer,), device_id_type=MESH,
        )

    def each(act):
        for k in offsets:
            act(k)

    def bytes_of(ref, send, recv):
        return copy(ref, ref, send, recv, sibling)

    state = master0, moment0
    state1 = master1, moment1
    state2 = master2, moment2
    state3 = master3, moment3
    sgot2 = mgot2, vgot2
    sgot3 = mgot3, vgot3

    def greet(semaphore, peers):
        for peer in peers:
            pl.semaphore_signal(
                semaphore, inc=1, device_id=(peer,), device_id_type=MESH
            )

    line = {axis: [along(axis, k) for k in (1, 2, 3)] for axis in "xzy"}
    barrier = pltpu.get_barrier_semaphore()
    greet(barrier, [sibling, *line["y"], *line["z"], *line["x"]])

    list_load = pltpu.make_async_copy(lists_hbm.at[0], lists, list_sem)
    list_load.start()
    for a, source in enumerate((master_hbm, first_hbm, second_hbm)):
        for h in range(2):
            go = pltpu.make_async_copy(
                source.at[:, pl.ds(h * 128, 128)], raw.at[h, a], raw_sem
            )
            go.start()

    def loads(i):
        span = pl.ds(pl.multiple_of(i * CHUNK, CHUNK), CHUNK)
        return (
            pltpu.make_async_copy(grad_hbm.at[0, span], grad.at[span], grad_sem.at[i]),
            pltpu.make_async_copy(err_hbm.at[0, span], err.at[0, span], err_sem.at[i]),
        )

    def load(i, _):
        for go in loads(i):
            go.start()
        return 0

    lax.fori_loop(0, chunks, load, 0)

    parts = (
        ((0,), pl.ds(0, 48)),
        ((1,), pl.ds(0, 48)),
        ((pl.ds(0, 2),), pl.ds(48, 16)),
    )

    def region(s, stage, place, half=None):
        cols, span = parts[s]
        taken = ORDERS[s][: min(stage, 2)]
        index = [pl.ds(0, 4) if axis in taken else place[axis] for axis in "xzy"]
        if half is not None:
            index["xzy".index(taken[0])] = pl.ds(2 * half, 2)
        return weights.at[(*index, c, *cols, span)]

    def stage_bytes(stage, sends, recvs):
        same = (
            weights.at[0, 0, pl.ds(0, 3), c],
            weights.at[0, pl.ds(0, 3), :, c],
            weights.at[pl.ds(0, 2), :, :, c],
            weights.at[0, :, :, c],
        )
        return bytes_of(same[stage], sends.at[stage], recvs.at[stage])

    def spread(stage):
        for s, order in enumerate(ORDERS):
            axis = order[min(stage, 2)]
            for k in (1, 2, 3) if stage < 2 else (1, 3):
                if stage < 3:
                    block = region(s, stage, at)
                else:
                    origin = {**at, axis: (at[axis] + 4 - k) % 4}
                    block = region(s, stage, origin, k // 2)
                copy(
                    block, block, w_send.at[stage], w_recv.at[stage], along(axis, k)
                ).start()

    def arrive(stage):
        stage_bytes(stage, w_send, w_recv).wait_recv()

    def forward(stage):
        for s, order in enumerate(ORDERS):
            axis = order[min(stage, 2)]
            for k in ((1, 2, 3), (1, 2, 3), (1, 3), (2,))[stage]:
                block = region(s, stage, {**at, axis: (at[axis] + k) % 4})
                copy(block, block, f_send, f_recv, sibling).start()

    list_load.wait()

    ids = lists[...]
    high_ids = (ids >> 7).astype(F32)
    low_ids = (ids & 127).astype(F32)

    inner = iota((SPAN // 16, 16, GROUP), 0) * 16 + iota((SPAN // 16, 16, GROUP), 1)
    inner = inner.astype(F32).astype(BF16)
    one = jnp.ones((SPAN // 16, 16, GROUP), BF16)
    zero = jnp.zeros((SPAN // 16, 16, GROUP), BF16)

    def ladder(row, count):
        tiles = count // 16
        near = jnp.broadcast_to(row, (16, GROUP)).astype(BF16)
        hit = jnp.where(inner[:tiles] == near[None], one[:tiles], zero[:tiles])
        return hit.reshape(count, GROUP)

    def member(r):
        spans = [slice(j, j + GROUP) for j in range(0, keep_n, GROUP)]
        high = [ladder(high_ids[r : r + 1, span], groups) for span in spans]
        low = [ladder(low_ids[r : r + 1, span], GROUP) for span in spans]
        return lax.dot_general(
            jnp.concatenate(high, axis=1), jnp.concatenate(low, axis=1),
            (((1,), (1,)), ((), ())), preferred_element_type=F32,
        )

    root = member(levels - 1)
    root_b = root.astype(BF16)
    before = onehot(iota((GROUP, GROUP), 0) < iota((GROUP, GROUP), 1))
    inside = jnp.dot(root_b, before, preferred_element_type=F32)
    total = jnp.dot(root_b, jnp.ones((GROUP, GROUP), BF16), preferred_element_type=F32)
    above = onehot(iota((groups, groups), 1) < iota((groups, groups), 0))
    start = jnp.dot(above, total.astype(BF16), preferred_element_type=F32)
    rank = start + inside
    starts[...] = start.astype(jnp.int32)
    rooted[...] = jnp.where(root > 0.5, rank, -1.0)

    keep = member(0)
    sent[...] = keep
    for r in range(1, levels - 1):
        keep = keep * member(r)
    kept[...] = jnp.where(keep * root > 0.5, rank, -1.0)

    chip_ranks = rooted[pl.ds(chip, 1), :]
    column[...] = jnp.transpose(jnp.broadcast_to(chip_ranks, (GROUP, GROUP)))
    own_rows = pl.ds(pl.multiple_of(c * 64, 64), 64)
    half = column[own_rows, :]
    pltpu.make_async_copy(raw, raw, raw_sem).wait()
    for a in range(2):
        raw_b[:, :, a * 128 : (a + 1) * 128] = raw[:, 1 + a].astype(BF16)
    mine_at = [at[order[0]] for order in STATE_ORDERS]
    master0[mine_at[0], own_rows, :] = raw[c, 0]
    moment0[mine_at[1], own_rows, :] = raw_b[c]

    for h in range(2):
        new_master, _, _ = adamw(raw[h, 0], raw[h, 1], raw[h, 2], 0.0)
        weights[x, z, y, c, h] = jnp.where(half < 0.0, new_master, 0.0).astype(BF16)
    acc[...] = jnp.zeros_like(acc)
    diagonal = iota((GROUP, GROUP), 0) == iota((GROUP, GROUP), 1)

    def pack(i):
        for go in loads(i):
            go.wait()
        each_row = []
        for j in range(CHUNK // GROUP):
            g = i * (CHUNK // GROUP) + j
            span = pl.ds(pl.multiple_of(g * GROUP, GROUP), GROUP)
            value = grad[span, :].astype(F32) + err[0, span, :]
            value_b[j * GROUP : (j + 1) * GROUP, :] = value.astype(BF16)
            each_row.append(kept[pl.ds(g, 1), :])
        for q in range(keep_n // SPAN):
            hits = []
            for row in each_row:
                hits.append(ladder(jnp.clip(row - q * SPAN, -1.0, SPAN), SPAN))
            acc[q * SPAN : (q + 1) * SPAN, :] += jnp.dot(
                jnp.concatenate(hits, axis=1), value_b[...], preferred_element_type=F32
            )

    def settle(i, _):
        for j in range(CHUNK // GROUP):
            g = i * (CHUNK // GROUP) + j
            span = pl.ds(pl.multiple_of(g * GROUP, GROUP), GROUP)
            stays = 1.0 - sent[pl.ds(g, 1), :]
            mask = jnp.dot(
                jnp.where(diagonal, stays, 0.0).astype(BF16),
                jnp.ones((GROUP, err.shape[2]), BF16),
                preferred_element_type=F32,
            )
            err[0, span, :] = (grad[span, :].astype(F32) + err[0, span, :]) * mask
        return 0

    pl.semaphore_wait(barrier, 10)
    greet(round_z, line["z"])

    raw_swaps = [
        copy(
            raw.at[1 - c, 0], state[0].at[mine_at[0], own_rows],
            raw_send, raw_recv, sibling,
        ),
        copy(
            raw_b.at[1 - c], state[1].at[mine_at[1], own_rows],
            rawb_send, rawb_recv, sibling,
        ),
    ]
    for go in raw_swaps:
        go.start()

    spread(0)
    mine = weights.at[x, z, y, c]
    copy(mine, mine, f_send, f_recv, sibling).start()

    pack(0)

    for go in raw_swaps:
        go.wait_recv()
    for a, order in enumerate(STATE_ORDERS):
        block = state[a].at[mine_at[a]]
        for k in (1, 2, 3):
            copy(
                block, block, s_send.at[a], s_recv.at[a], along(order[0], k)
            ).start()

    pl.semaphore_wait(round_z, 3)
    greet(round_x, line["x"])
    pack(1)
    pack(2)

    arrive(0)
    spread(1)
    pack(3)

    def place(a):
        order = STATE_ORDERS[a]
        bytes_of(state[a].at[pl.ds(0, 3)], s_send.at[a], s_recv.at[a]).wait_recv()
        shifts = {"x": 8, "z": 6, "y": 4}
        units = {"x": 16, "z": 4, "y": 1}
        hits = []
        for k in range(4):
            source = chip + (k - at[order[0]]) * units[order[0]]
            ranks = rooted[pl.ds(source, 1), :].astype(jnp.int32)
            first, second, third = ((ranks >> shifts[axis]) & 3 for axis in order)
            here = (ranks >= 0) & (first == at[order[0]])
            spot = second * (4 * UNIT) + third * UNIT + (ranks & (UNIT - 1))
            row = jnp.where(here, spot, -1).astype(F32)
            hits.append(ladder(row, 16 * UNIT))
        hits = jnp.concatenate(hits, axis=1)
        whole = state[a][...].reshape(4 * GROUP, -1)
        if a:
            split = whole
        else:
            high = whole.astype(BF16)
            rest = whole - high.astype(F32)
            middle = rest.astype(BF16)
            low = (rest - middle.astype(F32)).astype(BF16)
            split = jnp.concatenate([high, middle, low], axis=1)
        moved = jnp.dot(hits, split, preferred_element_type=F32)
        if not a:
            moved = (moved[:, :128] + moved[:, 128:256]) + moved[:, 256:]
        state1[a][...] = moved.astype(state1[a].dtype).reshape(state1[a].shape)

    def state_phase(phase, source, target):
        for a, order in enumerate(STATE_ORDERS):
            axis = order[phase]
            n = phase * 2 + a
            for k in (1, 2, 3):
                copy(
                    source[a].at[(at[axis] + k) % 4], target[a].at[k - 1],
                    s_send.at[n], s_recv.at[n], along(axis, k),
                ).start()

    def state_bytes(phase, target, a):
        n = phase * 2 + a
        return bytes_of(target[a], s_send.at[n], s_recv.at[n])

    def state_sum(phase, source, target, total):
        for a in range(2):
            state_bytes(phase, target, a).wait_recv()
        for a, order in enumerate(STATE_ORDERS):
            value = source[a][at[order[phase]]].astype(F32)
            for k in range(3):
                value = value + target[a][k].astype(F32)
            total[a][...] = value.astype(total[a].dtype)

    half_chips = chips // 2
    swaps = []
    for p in range(2):
        ranks = slice(p * keep_n // 2, (p + 1) * keep_n // 2)
        span = pl.ds(p * half_chips, half_chips)
        for h in range(2):
            packed[h, span] = (
                acc[ranks, h * 128 : (h + 1) * 128]
                .astype(BF16)
                .reshape(half_chips, UNIT, 128)
            )
        swap = copy(
            packed.at[1 - c, span], from_core.at[span],
            core_send.at[p], core_recv.at[p], sibling,
        )
        swap.start()
        swaps.append(swap)

    for a in range(2):
        place(a)
    state_phase(1, state1, sgot2)
    pl.semaphore_wait(round_x, 3)


    def scatter(k):
        other, peer = far(k)
        return copy(part.at[other], got.at[k - 1], rs_send, rs_recv, peer)

    for p in range(2):
        swaps[p].wait_recv()
        span = pl.ds(p * half_chips, half_chips)
        part[span] = (packed[c, span].astype(F32) + from_core[span].astype(F32)).astype(
            BF16
        )

    each(lambda k: scatter(k).start())
    own = packed[c, chip].astype(F32) + from_core[chip].astype(F32)
    forward(0)

    state_sum(1, state1, sgot2, state2)
    state_phase(2, state2, sgot3)

    arrive(1)
    spread(2)
    forward(1)

    for k in range(keep_n // GROUP):
        lanes = (iota((64, GROUP), 1) + k * GROUP).astype(F32)
        expand[:, k * GROUP : (k + 1) * GROUP] = onehot(half == lanes)

    state_sum(2, state2, sgot3, state3)
    scattered = bytes_of(got, rs_send, rs_recv)
    scattered.wait_recv()
    summed = (own + jnp.sum(got[...].astype(F32), axis=0)).astype(BF16)
    new_master, _, _ = adamw(
        master3[...], moment3[:, :128].astype(F32), moment3[:, 128:].astype(F32),
        summed.astype(F32),
    )
    result[c, chip, 0] = summed
    result[c, chip, 1] = new_master.astype(BF16)

    plane = chips // 4

    def gather(k):
        unit = result.at[c, chip]
        return copy(unit, unit, ag_send, ag_recv.at[x], far(k)[1])

    def pass_on(q):
        block = result.at[c, pl.ds(q * plane, plane)]
        return copy(block, block, half_send, half_recv, sibling)

    each(lambda k: gather(k).start())
    lax.fori_loop(0, chunks // 2, settle, 0)
    arrive(2)
    spread(3)
    forward(2)
    lax.fori_loop(chunks // 2, chunks, settle, 0)

    for k in (3, 2, 1):
        q = (x + k) % 4
        block = result.at[c, pl.ds(q * plane, plane)]
        bytes_of(block, ag_send, ag_recv.at[q]).wait_recv()
        pass_on(q).start()
    bytes_of(result.at[c, pl.ds(0, plane - 1)], ag_send, ag_recv.at[x]).wait_recv()
    pass_on(x).start()

    arrive(3)
    forward(3)

    scattered.wait_send()
    bytes_of(result.at[c, pl.ds(0, chips - 1)], ag_send, ag_recv.at[x]).wait_send()
    for go in raw_swaps:
        go.wait_send()
    for go in swaps:
        go.wait_send()
    for a in range(2):
        bytes_of(state[a].at[pl.ds(0, 3)], s_send.at[a], s_recv.at[a]).wait_send()
        state_bytes(1, sgot2, a).wait_send()
        state_bytes(2, sgot3, a).wait_send()
    for stage in range(4):
        stage_bytes(stage, w_send, w_recv).wait_send()
    bytes_of(weights.at[:, :, :, c], f_send, f_recv).wait()
    bytes_of(result.at[c], half_send, half_recv).wait()


def finish_kernel(
    err, weights, result, expand, rooted, starts_v, master, first, second,
    err_hbm, out_hbm, new_master, new_first, new_second,
    out, starts, err_sem, out_sem, starts_sem,
):
    groups = rooted.shape[0]
    to_smem = pltpu.make_async_copy(starts_v, starts, starts_sem)
    to_smem.start()
    rows = err.shape[1]
    pieces = err_sem.shape[0]
    copies = []
    for i in range(pieces):
        span = pl.ds(i * (rows // pieces), rows // pieces)
        go = pltpu.make_async_copy(err.at[0, span], err_hbm.at[0, span], err_sem.at[i])
        go.start()
        copies.append(go)

    to_smem.wait()
    units = result.shape[1]
    window = GROUP // UNIT + 1
    batch = groups // out_sem.shape[0]

    def store(i):
        span = pl.ds(i * batch, batch)
        return pltpu.make_async_copy(out.at[span], out_hbm.at[span], out_sem.at[i])

    def fill(i, _):
        for j in range(batch):
            g = i * batch + j
            unit = jnp.minimum(starts[g, 0] // UNIT, units - window)
            near = rooted[pl.ds(g, 1), :] - (unit * UNIT).astype(F32)
            hits = onehot(iota((window * UNIT, GROUP), 0).astype(F32) == near)
            held = jnp.concatenate(
                [
                    result[h, pl.ds(unit, window), 1].reshape(window * UNIT, 128)
                    for h in range(2)
                ],
                axis=1,
            )
            moved = lax.dot_general(
                hits, held, (((0,), (0,)), ((), ())), preferred_element_type=F32
            ).astype(BF16)
            for c in range(2):
                span = slice(c * 64, c * 64 + 64)
                for h in range(2):
                    lanes = slice(h * 128, h * 128 + 128)
                    out[g, span, lanes] = weights[g, c, h] + moved[span, lanes]
        store(i).start()
        return 0

    steps = out_sem.shape[0]
    lax.fori_loop(0, steps, fill, 0)
    total = jnp.concatenate(
        [
            jnp.dot(
                expand[...], result[h, :, 0].reshape(-1, 128),
                preferred_element_type=F32,
            )
            for h in range(2)
        ],
        axis=1,
    )
    new_master[...], new_first[...], new_second[...] = adamw(
        master[...], first[...], second[...], total
    )

    for go in copies:
        go.wait()
    lax.fori_loop(0, steps, lambda i, _: (store(i).wait(), 0)[1], 0)


def body(gradients, error_memory, block_lists, master, first_moment, second_moment):
    _, rows, width = gradients.shape
    owned = master.shape[0]
    levels, keep_n = block_lists.shape[1:]
    groups = rows // GROUP
    chunks = rows // CHUNK
    vmem = pl.BlockSpec(memory_space=pltpu.VMEM)
    anywhere = pl.BlockSpec(memory_space=pl.ANY)
    dma = pltpu.SemaphoreType.DMA

    err, weights, result, expand, rooted, starts = pl.pallas_call(
        merge_kernel,
        out_shape=(
            pltpu.VMEM((1, rows, width), F32),
            pltpu.VMEM((4, 4, 4, 2, 2, owned, 128), BF16),
            pltpu.VMEM((2, groups, 2, UNIT, 128), BF16),
            pltpu.VMEM((owned, keep_n), BF16),
            pltpu.VMEM((groups, GROUP), F32),
            pltpu.VMEM((groups, GROUP), jnp.int32),
        ),
        in_specs=[anywhere] * 6,
        out_specs=(vmem,) * 6,
        scratch_shapes=[
            pltpu.VMEM((rows, width), BF16),
            pltpu.VMEM((levels, keep_n), jnp.int32),
            pltpu.VMEM((2, 3, owned, 128), F32),
            pltpu.VMEM((2, owned, 256), BF16),
            pltpu.VMEM((keep_n, width), F32),
            pltpu.VMEM((groups, GROUP), F32),
            pltpu.VMEM((groups, GROUP), F32),
            pltpu.VMEM((GROUP, GROUP), F32),
            pltpu.VMEM((CHUNK, width), BF16),
            pltpu.VMEM((2, groups, UNIT, 128), BF16),
            pltpu.VMEM((groups, UNIT, 128), BF16),
            pltpu.VMEM((groups, UNIT, 128), BF16),
            pltpu.VMEM((groups - 1, UNIT, 128), BF16),
            *(
                pltpu.VMEM((*shape, lanes), kind)
                for lanes, kind in ((128, F32), (256, BF16))
                for shape in (
                    (4, GROUP), (4, 4, UNIT), (4, UNIT), (UNIT,),
                    (3, 4, UNIT), (3, UNIT),
                )
            ),
            dma((chunks,)), dma((chunks,)), dma, dma,
            dma((2,)), dma((2,)), dma, dma, dma, dma,
            dma, dma, dma, dma((4,)), dma, dma,
            dma((6,)), dma((6,)),
            dma((4,)), dma((4,)), dma, dma,
            pltpu.SemaphoreType.REGULAR, pltpu.SemaphoreType.REGULAR,
        ],
        compiler_params=pltpu.CompilerParams(
            collective_id=0, has_side_effects=True, vmem_limit_bytes=46 * MIB
        ),
        name="merge",
    )(gradients, error_memory, block_lists, master, first_moment, second_moment)

    new_errors, out, new_master, new_first, new_second = pl.pallas_call(
        finish_kernel,
        out_shape=(
            jax.ShapeDtypeStruct((1, rows, width), F32),
            jax.ShapeDtypeStruct((groups, GROUP, width), BF16),
            jax.ShapeDtypeStruct((owned, width), F32),
            jax.ShapeDtypeStruct((owned, width), F32),
            jax.ShapeDtypeStruct((owned, width), F32),
        ),
        in_specs=[vmem] * 9,
        out_specs=(anywhere, anywhere, vmem, vmem, vmem),
        scratch_shapes=[
            pltpu.VMEM((groups, GROUP, width), BF16),
            pltpu.SMEM((groups, GROUP), jnp.int32),
            dma((4,)), dma((8,)), dma,
        ],
        compiler_params=pltpu.CompilerParams(vmem_limit_bytes=32 * MIB),
        name="finish",
    )(
        err, weights.reshape(groups, 2, 2, owned, 128), result, expand, rooted, starts,
        master, first_moment, second_moment,
    )
    return new_errors, new_master, new_first, new_second, out.reshape(rows, width)


def solution(mesh):
    in_specs = (
        P("dp", None, None),
        P("dp", None, None),
        P("dp", None, None),
        P("dp", None),
        P("dp", None),
        P("dp", None),
    )
    out_specs = (P("dp", None, None), P("dp", None), P("dp", None), P("dp", None), P())
    return jax.shard_map(
        body, mesh=mesh, in_specs=in_specs, out_specs=out_specs, check_vma=False
    )
```

```python
import jax
import jax.numpy as jnp
from jax import lax
from jax.experimental import pallas as pl
from jax.experimental.pallas import tpu as pltpu
from jax.sharding import PartitionSpec as P

FIRST_BIAS = 0.9999734386011124
SECOND_BIAS = 0.09520785288629036
MESH = pl.DeviceIdType.MESH
F32 = jnp.float32
BF16 = jnp.bfloat16
MIB = 1 << 20

GROUP = 128
CHUNK = 2048
UNIT = 16
SPAN = 256

ORDERS = ("xzy", "zyx", "yxz")
STATE_ORDERS = ("zyx", "xzy")


def iota(shape, dim):
    return lax.broadcasted_iota(jnp.int32, shape, dim)


def onehot(hits):
    return jnp.where(hits, 1.0, 0.0).astype(BF16)


def adamw(master, first, second, summed):
    new_first = 0.9 * first + 0.1 * summed
    new_second = 0.999 * second + 0.001 * summed * summed
    first_hat = new_first / FIRST_BIAS
    second_hat = new_second / SECOND_BIAS
    new_master = master - 0.001 * (
        first_hat / (jnp.sqrt(second_hat) + 1e-08) + 0.1 * master
    )
    return new_master, new_first, new_second


def merge_kernel(
    grad_hbm, err_hbm, lists_hbm, master_hbm, first_hbm, second_hbm,
    err, weights, result, expand, rooted, starts,
    grad, lists, raw, raw_b, acc, sent, kept, column, value_b,
    packed, from_core, part, got,
    master0, master1, master2, master3, mgot2, mgot3,
    moment0, moment1, moment2, moment3, vgot2, vgot3,
    grad_sem, err_sem, list_sem, raw_sem,
    core_send, core_recv, raw_send, raw_recv, rawb_send, rawb_recv,
    rs_send, rs_recv, ag_send, ag_recv, half_send, half_recv,
    s_send, s_recv, w_send, w_recv, f_send, f_recv, round_z, round_x,
):
    rows = grad.shape[0]
    groups = rows // GROUP
    chunks = rows // CHUNK
    levels, keep_n = lists.shape
    me = lax.axis_index("dp")
    c = me % 2
    y = (me // 2) % 4
    z = (me // 8) % 4
    x = me // 32
    chip = me // 2
    chips = groups
    sibling = me + 1 - 2 * c
    at = {"x": x, "z": z, "y": y}
    strides = {"x": 32, "z": 8, "y": 2}

    def far(k):
        other = (x + k // 16) % 4 * 16 + (z + k // 4 % 4) % 4 * 4 + (y + k % 4) % 4
        return other, 2 * other + c

    away = (2, 1, 3, 0)
    offsets = [16 * i + 4 * j + k for i in away for j in away for k in away][:-1]

    def along(axis, k):
        return me + ((at[axis] + k) % 4 - at[axis]) * strides[axis]

    def copy(src, dst, send, recv, peer):
        return pltpu.make_async_remote_copy(
            src_ref=src, dst_ref=dst, send_sem=send, recv_sem=recv,
            device_id=(peer,), device_id_type=MESH,
        )

    def each(act):
        for k in offsets:
            act(k)

    def bytes_of(ref, send, recv):
        return copy(ref, ref, send, recv, sibling)

    state = master0, moment0
    state1 = master1, moment1
    state2 = master2, moment2
    state3 = master3, moment3
    sgot2 = mgot2, vgot2
    sgot3 = mgot3, vgot3

    def greet(semaphore, peers):
        for peer in peers:
            pl.semaphore_signal(
                semaphore, inc=1, device_id=(peer,), device_id_type=MESH
            )

    line = {axis: [along(axis, k) for k in (1, 2, 3)] for axis in "xzy"}
    barrier = pltpu.get_barrier_semaphore()
    greet(barrier, [sibling, *line["y"], *line["z"], *line["x"]])

    list_load = pltpu.make_async_copy(lists_hbm.at[0], lists, list_sem)
    list_load.start()
    for a, source in enumerate((master_hbm, first_hbm, second_hbm)):
        for h in range(2):
            go = pltpu.make_async_copy(
                source.at[:, pl.ds(h * 128, 128)], raw.at[h, a], raw_sem
            )
            go.start()

    def loads(i):
        span = pl.ds(pl.multiple_of(i * CHUNK, CHUNK), CHUNK)
        return (
            pltpu.make_async_copy(grad_hbm.at[0, span], grad.at[span], grad_sem.at[i]),
            pltpu.make_async_copy(err_hbm.at[0, span], err.at[0, span], err_sem.at[i]),
        )

    def load(i, _):
        for go in loads(i):
            go.start()
        return 0

    lax.fori_loop(0, chunks, load, 0)

    parts = (
        ((0,), pl.ds(0, 48)),
        ((1,), pl.ds(0, 48)),
        ((pl.ds(0, 2),), pl.ds(48, 16)),
    )

    def region(s, stage, place, half=None):
        cols, span = parts[s]
        taken = ORDERS[s][: min(stage, 2)]
        index = [pl.ds(0, 4) if axis in taken else place[axis] for axis in "xzy"]
        if half is not None:
            index["xzy".index(taken[0])] = pl.ds(2 * half, 2)
        return weights.at[(*index, c, *cols, span)]

    def stage_bytes(stage, sends, recvs):
        same = (
            weights.at[0, 0, pl.ds(0, 3), c],
            weights.at[0, pl.ds(0, 3), :, c],
            weights.at[pl.ds(0, 2), :, :, c],
            weights.at[0, :, :, c],
        )
        return bytes_of(same[stage], sends.at[stage], recvs.at[stage])

    def spread(stage):
        for s, order in enumerate(ORDERS):
            axis = order[min(stage, 2)]
            for k in (1, 2, 3) if stage < 2 else (1, 3):
                if stage < 3:
                    block = region(s, stage, at)
                else:
                    origin = {**at, axis: (at[axis] + 4 - k) % 4}
                    block = region(s, stage, origin, k // 2)
                copy(
                    block, block, w_send.at[stage], w_recv.at[stage], along(axis, k)
                ).start()

    def arrive(stage):
        stage_bytes(stage, w_send, w_recv).wait_recv()

    def forward(stage):
        for s, order in enumerate(ORDERS):
            axis = order[min(stage, 2)]
            for k in ((1, 2, 3), (1, 2, 3), (1, 3), (2,))[stage]:
                block = region(s, stage, {**at, axis: (at[axis] + k) % 4})
                copy(block, block, f_send, f_recv, sibling).start()

    list_load.wait()

    ids = lists[...]
    high_ids = (ids >> 7).astype(F32)
    low_ids = (ids & 127).astype(F32)

    inner = iota((SPAN // 16, 16, GROUP), 0) * 16 + iota((SPAN // 16, 16, GROUP), 1)
    inner = inner.astype(F32).astype(BF16)
    one = jnp.ones((SPAN // 16, 16, GROUP), BF16)
    zero = jnp.zeros((SPAN // 16, 16, GROUP), BF16)

    def ladder(row, count):
        tiles = count // 16
        near = jnp.broadcast_to(row, (16, GROUP)).astype(BF16)
        hit = jnp.where(inner[:tiles] == near[None], one[:tiles], zero[:tiles])
        return hit.reshape(count, GROUP)

    def member(r):
        spans = [slice(j, j + GROUP) for j in range(0, keep_n, GROUP)]
        high = [ladder(high_ids[r : r + 1, span], groups) for span in spans]
        low = [ladder(low_ids[r : r + 1, span], GROUP) for span in spans]
        return lax.dot_general(
            jnp.concatenate(high, axis=1), jnp.concatenate(low, axis=1),
            (((1,), (1,)), ((), ())), preferred_element_type=F32,
        )

    root = member(levels - 1)
    root_b = root.astype(BF16)
    before = onehot(iota((GROUP, GROUP), 0) < iota((GROUP, GROUP), 1))
    inside = jnp.dot(root_b, before, preferred_element_type=F32)
    total = jnp.dot(root_b, jnp.ones((GROUP, GROUP), BF16), preferred_element_type=F32)
    above = onehot(iota((groups, groups), 1) < iota((groups, groups), 0))
    start = jnp.dot(above, total.astype(BF16), preferred_element_type=F32)
    rank = start + inside
    starts[...] = start.astype(jnp.int32)
    rooted[...] = jnp.where(root > 0.5, rank, -1.0)

    keep = member(0)
    sent[...] = keep
    for r in range(1, levels - 1):
        keep = keep * member(r)
    kept[...] = jnp.where(keep * root > 0.5, rank, -1.0)

    chip_ranks = rooted[pl.ds(chip, 1), :]
    column[...] = jnp.transpose(jnp.broadcast_to(chip_ranks, (GROUP, GROUP)))
    own_rows = pl.ds(pl.multiple_of(c * 64, 64), 64)
    half = column[own_rows, :]
    pltpu.make_async_copy(raw, raw, raw_sem).wait()
    for a in range(2):
        raw_b[:, :, a * 128 : (a + 1) * 128] = raw[:, 1 + a].astype(BF16)
    mine_at = [at[order[0]] for order in STATE_ORDERS]
    master0[mine_at[0], own_rows, :] = raw[c, 0]
    moment0[mine_at[1], own_rows, :] = raw_b[c]

    for h in range(2):
        new_master, _, _ = adamw(raw[h, 0], raw[h, 1], raw[h, 2], 0.0)
        weights[x, z, y, c, h] = jnp.where(half < 0.0, new_master, 0.0).astype(BF16)
    acc[...] = jnp.zeros_like(acc)
    diagonal = iota((GROUP, GROUP), 0) == iota((GROUP, GROUP), 1)

    def pack(i):
        for go in loads(i):
            go.wait()
        each_row = []
        for j in range(CHUNK // GROUP):
            g = i * (CHUNK // GROUP) + j
            span = pl.ds(pl.multiple_of(g * GROUP, GROUP), GROUP)
            value = grad[span, :].astype(F32) + err[0, span, :]
            value_b[j * GROUP : (j + 1) * GROUP, :] = value.astype(BF16)
            each_row.append(kept[pl.ds(g, 1), :])
        for q in range(keep_n // SPAN):
            hits = []
            for row in each_row:
                hits.append(ladder(jnp.clip(row - q * SPAN, -1.0, SPAN), SPAN))
            acc[q * SPAN : (q + 1) * SPAN, :] += jnp.dot(
                jnp.concatenate(hits, axis=1), value_b[...], preferred_element_type=F32
            )

    def settle(i, _):
        for j in range(CHUNK // GROUP):
            g = i * (CHUNK // GROUP) + j
            span = pl.ds(pl.multiple_of(g * GROUP, GROUP), GROUP)
            stays = 1.0 - sent[pl.ds(g, 1), :]
            mask = jnp.dot(
                jnp.where(diagonal, stays, 0.0).astype(BF16),
                jnp.ones((GROUP, err.shape[2]), BF16),
                preferred_element_type=F32,
            )
            err[0, span, :] = (grad[span, :].astype(F32) + err[0, span, :]) * mask
        return 0

    pl.semaphore_wait(barrier, 10)
    greet(round_z, line["z"])

    raw_swaps = [
        copy(
            raw.at[1 - c, 0], state[0].at[mine_at[0], own_rows],
            raw_send, raw_recv, sibling,
        ),
        copy(
            raw_b.at[1 - c], state[1].at[mine_at[1], own_rows],
            rawb_send, rawb_recv, sibling,
        ),
    ]
    for go in raw_swaps:
        go.start()

    spread(0)
    mine = weights.at[x, z, y, c]
    copy(mine, mine, f_send, f_recv, sibling).start()

    pack(0)

    for go in raw_swaps:
        go.wait_recv()
    for a, order in enumerate(STATE_ORDERS):
        block = state[a].at[mine_at[a]]
        for k in (1, 2, 3):
            copy(
                block, block, s_send.at[a], s_recv.at[a], along(order[0], k)
            ).start()

    pl.semaphore_wait(round_z, 3)
    greet(round_x, line["x"])
    pack(1)
    pack(2)

    arrive(0)
    spread(1)
    pack(3)

    def place(a):
        order = STATE_ORDERS[a]
        bytes_of(state[a].at[pl.ds(0, 3)], s_send.at[a], s_recv.at[a]).wait_recv()
        shifts = {"x": 8, "z": 6, "y": 4}
        units = {"x": 16, "z": 4, "y": 1}
        hits = []
        for k in range(4):
            source = chip + (k - at[order[0]]) * units[order[0]]
            ranks = rooted[pl.ds(source, 1), :].astype(jnp.int32)
            first, second, third = ((ranks >> shifts[axis]) & 3 for axis in order)
            here = (ranks >= 0) & (first == at[order[0]])
            spot = second * (4 * UNIT) + third * UNIT + (ranks & (UNIT - 1))
            row = jnp.where(here, spot, -1).astype(F32)
            hits.append(ladder(row, 16 * UNIT))
        hits = jnp.concatenate(hits, axis=1)
        whole = state[a][...].reshape(4 * GROUP, -1)
        if a:
            split = whole
        else:
            high = whole.astype(BF16)
            rest = whole - high.astype(F32)
            middle = rest.astype(BF16)
            low = (rest - middle.astype(F32)).astype(BF16)
            split = jnp.concatenate([high, middle, low], axis=1)
        moved = jnp.dot(hits, split, preferred_element_type=F32)
        if not a:
            moved = (moved[:, :128] + moved[:, 128:256]) + moved[:, 256:]
        state1[a][...] = moved.astype(state1[a].dtype).reshape(state1[a].shape)

    def state_phase(phase, source, target):
        for a, order in enumerate(STATE_ORDERS):
            axis = order[phase]
            n = phase * 2 + a
            for k in (1, 2, 3):
                copy(
                    source[a].at[(at[axis] + k) % 4], target[a].at[k - 1],
                    s_send.at[n], s_recv.at[n], along(axis, k),
                ).start()

    def state_bytes(phase, target, a):
        n = phase * 2 + a
        return bytes_of(target[a], s_send.at[n], s_recv.at[n])

    def state_sum(phase, source, target, total):
        for a in range(2):
            state_bytes(phase, target, a).wait_recv()
        for a, order in enumerate(STATE_ORDERS):
            value = source[a][at[order[phase]]].astype(F32)
            for k in range(3):
                value = value + target[a][k].astype(F32)
            total[a][...] = value.astype(total[a].dtype)

    half_chips = chips // 2
    swaps = []
    for p in range(2):
        ranks = slice(p * keep_n // 2, (p + 1) * keep_n // 2)
        span = pl.ds(p * half_chips, half_chips)
        for h in range(2):
            packed[h, span] = (
                acc[ranks, h * 128 : (h + 1) * 128]
                .astype(BF16)
                .reshape(half_chips, UNIT, 128)
            )
        swap = copy(
            packed.at[1 - c, span], from_core.at[span],
            core_send.at[p], core_recv.at[p], sibling,
        )
        swap.start()
        swaps.append(swap)

    for a in range(2):
        place(a)
    state_phase(1, state1, sgot2)
    pl.semaphore_wait(round_x, 3)


    def scatter(k):
        other, peer = far(k)
        return copy(part.at[other], got.at[k - 1], rs_send, rs_recv, peer)

    for p in range(2):
        swaps[p].wait_recv()
        span = pl.ds(p * half_chips, half_chips)
        part[span] = (packed[c, span].astype(F32) + from_core[span].astype(F32)).astype(
            BF16
        )

    each(lambda k: scatter(k).start())
    own = packed[c, chip].astype(F32) + from_core[chip].astype(F32)
    forward(0)

    state_sum(1, state1, sgot2, state2)
    state_phase(2, state2, sgot3)

    arrive(1)
    spread(2)
    forward(1)

    for k in range(keep_n // GROUP):
        lanes = (iota((64, GROUP), 1) + k * GROUP).astype(F32)
        expand[:, k * GROUP : (k + 1) * GROUP] = onehot(half == lanes)

    state_sum(2, state2, sgot3, state3)
    scattered = bytes_of(got, rs_send, rs_recv)
    scattered.wait_recv()
    summed = (own + jnp.sum(got[...].astype(F32), axis=0)).astype(BF16)
    new_master, _, _ = adamw(
        master3[...], moment3[:, :128].astype(F32), moment3[:, 128:].astype(F32),
        summed.astype(F32),
    )
    result[c, chip, 0] = summed
    result[c, chip, 1] = new_master.astype(BF16)

    plane = chips // 4

    def gather(k):
        unit = result.at[c, chip]
        return copy(unit, unit, ag_send, ag_recv.at[x], far(k)[1])

    def pass_on(q):
        block = result.at[c, pl.ds(q * plane, plane)]
        return copy(block, block, half_send, half_recv, sibling)

    each(lambda k: gather(k).start())
    lax.fori_loop(0, chunks // 2, settle, 0)
    arrive(2)
    spread(3)
    forward(2)
    lax.fori_loop(chunks // 2, chunks, settle, 0)

    for k in (2, 3, 1):
        q = (x + k) % 4
        block = result.at[c, pl.ds(q * plane, plane)]
        bytes_of(block, ag_send, ag_recv.at[q]).wait_recv()
        pass_on(q).start()
    bytes_of(result.at[c, pl.ds(0, plane - 1)], ag_send, ag_recv.at[x]).wait_recv()
    pass_on(x).start()

    arrive(3)
    forward(3)

    scattered.wait_send()
    bytes_of(result.at[c, pl.ds(0, chips - 1)], ag_send, ag_recv.at[x]).wait_send()
    for go in raw_swaps:
        go.wait_send()
    for go in swaps:
        go.wait_send()
    for a in range(2):
        bytes_of(state[a].at[pl.ds(0, 3)], s_send.at[a], s_recv.at[a]).wait_send()
        state_bytes(1, sgot2, a).wait_send()
        state_bytes(2, sgot3, a).wait_send()
    for stage in range(4):
        stage_bytes(stage, w_send, w_recv).wait_send()
    bytes_of(weights.at[:, :, :, c], f_send, f_recv).wait()
    bytes_of(result.at[c], half_send, half_recv).wait()


def finish_kernel(
    err, weights, result, expand, rooted, starts_v, master, first, second,
    err_hbm, out_hbm, new_master, new_first, new_second,
    out, starts, err_sem, out_sem, starts_sem,
):
    groups = rooted.shape[0]
    to_smem = pltpu.make_async_copy(starts_v, starts, starts_sem)
    to_smem.start()
    rows = err.shape[1]
    pieces = err_sem.shape[0]
    copies = []
    for i in range(pieces):
        span = pl.ds(i * (rows // pieces), rows // pieces)
        go = pltpu.make_async_copy(err.at[0, span], err_hbm.at[0, span], err_sem.at[i])
        go.start()
        copies.append(go)

    to_smem.wait()
    units = result.shape[1]
    window = GROUP // UNIT + 1
    batch = groups // out_sem.shape[0]

    def store(i):
        span = pl.ds(i * batch, batch)
        return pltpu.make_async_copy(out.at[span], out_hbm.at[span], out_sem.at[i])

    def fill(i, _):
        for j in range(batch):
            g = i * batch + j
            unit = jnp.minimum(starts[g, 0] // UNIT, units - window)
            near = rooted[pl.ds(g, 1), :] - (unit * UNIT).astype(F32)
            hits = onehot(iota((window * UNIT, GROUP), 0).astype(F32) == near)
            held = jnp.concatenate(
                [
                    result[h, pl.ds(unit, window), 1].reshape(window * UNIT, 128)
                    for h in range(2)
                ],
                axis=1,
            )
            moved = lax.dot_general(
                hits, held, (((0,), (0,)), ((), ())), preferred_element_type=F32
            ).astype(BF16)
            for c in range(2):
                span = slice(c * 64, c * 64 + 64)
                for h in range(2):
                    lanes = slice(h * 128, h * 128 + 128)
                    out[g, span, lanes] = weights[g, c, h] + moved[span, lanes]
        store(i).start()
        return 0

    steps = out_sem.shape[0]
    lax.fori_loop(0, steps, fill, 0)
    total = jnp.concatenate(
        [
            jnp.dot(
                expand[...], result[h, :, 0].reshape(-1, 128),
                preferred_element_type=F32,
            )
            for h in range(2)
        ],
        axis=1,
    )
    new_master[...], new_first[...], new_second[...] = adamw(
        master[...], first[...], second[...], total
    )

    for go in copies:
        go.wait()
    lax.fori_loop(0, steps, lambda i, _: (store(i).wait(), 0)[1], 0)


def body(gradients, error_memory, block_lists, master, first_moment, second_moment):
    _, rows, width = gradients.shape
    owned = master.shape[0]
    levels, keep_n = block_lists.shape[1:]
    groups = rows // GROUP
    chunks = rows // CHUNK
    vmem = pl.BlockSpec(memory_space=pltpu.VMEM)
    anywhere = pl.BlockSpec(memory_space=pl.ANY)
    dma = pltpu.SemaphoreType.DMA

    err, weights, result, expand, rooted, starts = pl.pallas_call(
        merge_kernel,
        out_shape=(
            pltpu.VMEM((1, rows, width), F32),
            pltpu.VMEM((4, 4, 4, 2, 2, owned, 128), BF16),
            pltpu.VMEM((2, groups, 2, UNIT, 128), BF16),
            pltpu.VMEM((owned, keep_n), BF16),
            pltpu.VMEM((groups, GROUP), F32),
            pltpu.VMEM((groups, GROUP), jnp.int32),
        ),
        in_specs=[anywhere] * 6,
        out_specs=(vmem,) * 6,
        scratch_shapes=[
            pltpu.VMEM((rows, width), BF16),
            pltpu.VMEM((levels, keep_n), jnp.int32),
            pltpu.VMEM((2, 3, owned, 128), F32),
            pltpu.VMEM((2, owned, 256), BF16),
            pltpu.VMEM((keep_n, width), F32),
            pltpu.VMEM((groups, GROUP), F32),
            pltpu.VMEM((groups, GROUP), F32),
            pltpu.VMEM((GROUP, GROUP), F32),
            pltpu.VMEM((CHUNK, width), BF16),
            pltpu.VMEM((2, groups, UNIT, 128), BF16),
            pltpu.VMEM((groups, UNIT, 128), BF16),
            pltpu.VMEM((groups, UNIT, 128), BF16),
            pltpu.VMEM((groups - 1, UNIT, 128), BF16),
            *(
                pltpu.VMEM((*shape, lanes), kind)
                for lanes, kind in ((128, F32), (256, BF16))
                for shape in (
                    (4, GROUP), (4, 4, UNIT), (4, UNIT), (UNIT,),
                    (3, 4, UNIT), (3, UNIT),
                )
            ),
            dma((chunks,)), dma((chunks,)), dma, dma,
            dma((2,)), dma((2,)), dma, dma, dma, dma,
            dma, dma, dma, dma((4,)), dma, dma,
            dma((6,)), dma((6,)),
            dma((4,)), dma((4,)), dma, dma,
            pltpu.SemaphoreType.REGULAR, pltpu.SemaphoreType.REGULAR,
        ],
        compiler_params=pltpu.CompilerParams(
            collective_id=0, has_side_effects=True, vmem_limit_bytes=46 * MIB
        ),
        name="merge",
    )(gradients, error_memory, block_lists, master, first_moment, second_moment)

    new_errors, out, new_master, new_first, new_second = pl.pallas_call(
        finish_kernel,
        out_shape=(
            jax.ShapeDtypeStruct((1, rows, width), F32),
            jax.ShapeDtypeStruct((groups, GROUP, width), BF16),
            jax.ShapeDtypeStruct((owned, width), F32),
            jax.ShapeDtypeStruct((owned, width), F32),
            jax.ShapeDtypeStruct((owned, width), F32),
        ),
        in_specs=[vmem] * 9,
        out_specs=(anywhere, anywhere, vmem, vmem, vmem),
        scratch_shapes=[
            pltpu.VMEM((groups, GROUP, width), BF16),
            pltpu.SMEM((groups, GROUP), jnp.int32),
            dma((4,)), dma((8,)), dma,
        ],
        compiler_params=pltpu.CompilerParams(vmem_limit_bytes=32 * MIB),
        name="finish",
    )(
        err, weights.reshape(groups, 2, 2, owned, 128), result, expand, rooted, starts,
        master, first_moment, second_moment,
    )
    return new_errors, new_master, new_first, new_second, out.reshape(rows, width)


def solution(mesh):
    in_specs = (
        P("dp", None, None),
        P("dp", None, None),
        P("dp", None, None),
        P("dp", None),
        P("dp", None),
        P("dp", None),
    )
    out_specs = (P("dp", None, None), P("dp", None), P("dp", None), P("dp", None), P())
    return jax.shard_map(
        body, mesh=mesh, in_specs=in_specs, out_specs=out_specs, check_vma=False
    )
```

```python
import jax
import jax.numpy as jnp
from jax import lax
from jax.experimental import pallas as pl
from jax.experimental.pallas import tpu as pltpu
from jax.sharding import PartitionSpec as P

FIRST_BIAS = 0.9999734386011124
SECOND_BIAS = 0.09520785288629036
MESH = pl.DeviceIdType.MESH
F32 = jnp.float32
BF16 = jnp.bfloat16
MIB = 1 << 20

GROUP = 128
CHUNK = 2048
UNIT = 16
SPAN = 256

ORDERS = ("xzy", "zyx", "yxz")
STATE_ORDERS = ("zyx", "xzy")


def iota(shape, dim):
    return lax.broadcasted_iota(jnp.int32, shape, dim)


def onehot(hits):
    return jnp.where(hits, 1.0, 0.0).astype(BF16)


def adamw(master, first, second, summed):
    new_first = 0.9 * first + 0.1 * summed
    new_second = 0.999 * second + 0.001 * summed * summed
    first_hat = new_first / FIRST_BIAS
    second_hat = new_second / SECOND_BIAS
    new_master = master - 0.001 * (
        first_hat / (jnp.sqrt(second_hat) + 1e-08) + 0.1 * master
    )
    return new_master, new_first, new_second


def merge_kernel(
    grad_hbm, err_hbm, lists_hbm, master_hbm, first_hbm, second_hbm,
    err, weights, result, expand, rooted, starts,
    grad, lists, raw, raw_b, acc, sent, kept, column, value_b,
    packed, from_core, part, got,
    master0, master1, master2, master3, mgot2, mgot3,
    moment0, moment1, moment2, moment3, vgot2, vgot3,
    grad_sem, err_sem, list_sem, raw_sem,
    core_send, core_recv, raw_send, raw_recv, rawb_send, rawb_recv,
    rs_send, rs_recv, ag_send, ag_recv, half_send, half_recv,
    s_send, s_recv, w_send, w_recv, f_send, f_recv, round_z, round_x,
):
    rows = grad.shape[0]
    groups = rows // GROUP
    chunks = rows // CHUNK
    levels, keep_n = lists.shape
    me = lax.axis_index("dp")
    c = me % 2
    y = (me // 2) % 4
    z = (me // 8) % 4
    x = me // 32
    chip = me // 2
    chips = groups
    sibling = me + 1 - 2 * c
    at = {"x": x, "z": z, "y": y}
    strides = {"x": 32, "z": 8, "y": 2}

    def far(k):
        other = (x + k // 16) % 4 * 16 + (z + k // 4 % 4) % 4 * 4 + (y + k % 4) % 4
        return other, 2 * other + c

    away = (2, 1, 3, 0)
    offsets = [16 * i + 4 * j + k for i in away for j in away for k in away][:-1]

    def along(axis, k):
        return me + ((at[axis] + k) % 4 - at[axis]) * strides[axis]

    def copy(src, dst, send, recv, peer):
        return pltpu.make_async_remote_copy(
            src_ref=src, dst_ref=dst, send_sem=send, recv_sem=recv,
            device_id=(peer,), device_id_type=MESH,
        )

    def each(act):
        for k in offsets:
            act(k)

    def bytes_of(ref, send, recv):
        return copy(ref, ref, send, recv, sibling)

    state = master0, moment0
    state1 = master1, moment1
    state2 = master2, moment2
    state3 = master3, moment3
    sgot2 = mgot2, vgot2
    sgot3 = mgot3, vgot3

    def greet(semaphore, peers):
        for peer in peers:
            pl.semaphore_signal(
                semaphore, inc=1, device_id=(peer,), device_id_type=MESH
            )

    line = {axis: [along(axis, k) for k in (1, 2, 3)] for axis in "xzy"}
    barrier = pltpu.get_barrier_semaphore()
    greet(barrier, [sibling, *line["y"], *line["z"], *line["x"]])

    list_load = pltpu.make_async_copy(lists_hbm.at[0], lists, list_sem)
    list_load.start()
    for a, source in enumerate((master_hbm, first_hbm, second_hbm)):
        for h in range(2):
            go = pltpu.make_async_copy(
                source.at[:, pl.ds(h * 128, 128)], raw.at[h, a], raw_sem
            )
            go.start()

    def loads(i):
        span = pl.ds(pl.multiple_of(i * CHUNK, CHUNK), CHUNK)
        return (
            pltpu.make_async_copy(grad_hbm.at[0, span], grad.at[span], grad_sem.at[i]),
            pltpu.make_async_copy(err_hbm.at[0, span], err.at[0, span], err_sem.at[i]),
        )

    def load(i, _):
        for go in loads(i):
            go.start()
        return 0

    lax.fori_loop(0, chunks, load, 0)

    parts = (
        ((0,), pl.ds(0, 48)),
        ((1,), pl.ds(0, 48)),
        ((pl.ds(0, 2),), pl.ds(48, 16)),
    )

    def region(s, stage, place, half=None):
        cols, span = parts[s]
        taken = ORDERS[s][: min(stage, 2)]
        index = [pl.ds(0, 4) if axis in taken else place[axis] for axis in "xzy"]
        if half is not None:
            index["xzy".index(taken[0])] = pl.ds(2 * half, 2)
        return weights.at[(*index, c, *cols, span)]

    def stage_bytes(stage, sends, recvs):
        same = (
            weights.at[0, 0, pl.ds(0, 3), c],
            weights.at[0, pl.ds(0, 3), :, c],
            weights.at[pl.ds(0, 2), :, :, c],
            weights.at[0, :, :, c],
        )
        return bytes_of(same[stage], sends.at[stage], recvs.at[stage])

    def spread(stage):
        for s, order in enumerate(ORDERS):
            axis = order[min(stage, 2)]
            for k in (1, 2, 3) if stage < 2 else (1, 3):
                if stage < 3:
                    block = region(s, stage, at)
                else:
                    origin = {**at, axis: (at[axis] + 4 - k) % 4}
                    block = region(s, stage, origin, k // 2)
                copy(
                    block, block, w_send.at[stage], w_recv.at[stage], along(axis, k)
                ).start()

    def arrive(stage):
        stage_bytes(stage, w_send, w_recv).wait_recv()

    def forward(stage):
        for s, order in enumerate(ORDERS):
            axis = order[min(stage, 2)]
            for k in ((1, 2, 3), (1, 2, 3), (1, 3), (2,))[stage]:
                block = region(s, stage, {**at, axis: (at[axis] + k) % 4})
                copy(block, block, f_send, f_recv, sibling).start()

    list_load.wait()

    ids = lists[...]
    high_ids = (ids >> 7).astype(F32)
    low_ids = (ids & 127).astype(F32)

    inner = iota((SPAN // 16, 16, GROUP), 0) * 16 + iota((SPAN // 16, 16, GROUP), 1)
    inner = inner.astype(F32).astype(BF16)
    one = jnp.ones((SPAN // 16, 16, GROUP), BF16)
    zero = jnp.zeros((SPAN // 16, 16, GROUP), BF16)

    def ladder(row, count):
        tiles = count // 16
        near = jnp.broadcast_to(row, (16, GROUP)).astype(BF16)
        hit = jnp.where(inner[:tiles] == near[None], one[:tiles], zero[:tiles])
        return hit.reshape(count, GROUP)

    def member(r):
        spans = [slice(j, j + GROUP) for j in range(0, keep_n, GROUP)]
        high = [ladder(high_ids[r : r + 1, span], groups) for span in spans]
        low = [ladder(low_ids[r : r + 1, span], GROUP) for span in spans]
        return lax.dot_general(
            jnp.concatenate(high, axis=1), jnp.concatenate(low, axis=1),
            (((1,), (1,)), ((), ())), preferred_element_type=F32,
        )

    root = member(levels - 1)
    root_b = root.astype(BF16)
    before = onehot(iota((GROUP, GROUP), 0) < iota((GROUP, GROUP), 1))
    inside = jnp.dot(root_b, before, preferred_element_type=F32)
    total = jnp.dot(root_b, jnp.ones((GROUP, GROUP), BF16), preferred_element_type=F32)
    above = onehot(iota((groups, groups), 1) < iota((groups, groups), 0))
    start = jnp.dot(above, total.astype(BF16), preferred_element_type=F32)
    rank = start + inside
    starts[...] = start.astype(jnp.int32)
    rooted[...] = jnp.where(root > 0.5, rank, -1.0)

    keep = member(0)
    sent[...] = keep
    for r in range(1, levels - 1):
        keep = keep * member(r)
    kept[...] = jnp.where(keep * root > 0.5, rank, -1.0)

    chip_ranks = rooted[pl.ds(chip, 1), :]
    column[...] = jnp.transpose(jnp.broadcast_to(chip_ranks, (GROUP, GROUP)))
    own_rows = pl.ds(pl.multiple_of(c * 64, 64), 64)
    half = column[own_rows, :]
    pltpu.make_async_copy(raw, raw, raw_sem).wait()
    for a in range(2):
        raw_b[:, :, a * 128 : (a + 1) * 128] = raw[:, 1 + a].astype(BF16)
    mine_at = [at[order[0]] for order in STATE_ORDERS]
    master0[mine_at[0], own_rows, :] = raw[c, 0]
    moment0[mine_at[1], own_rows, :] = raw_b[c]

    for h in range(2):
        new_master, _, _ = adamw(raw[h, 0], raw[h, 1], raw[h, 2], 0.0)
        weights[x, z, y, c, h] = jnp.where(half < 0.0, new_master, 0.0).astype(BF16)
    acc[...] = jnp.zeros_like(acc)
    diagonal = iota((GROUP, GROUP), 0) == iota((GROUP, GROUP), 1)

    def pack(i):
        for go in loads(i):
            go.wait()
        each_row = []
        for j in range(CHUNK // GROUP):
            g = i * (CHUNK // GROUP) + j
            span = pl.ds(pl.multiple_of(g * GROUP, GROUP), GROUP)
            value = grad[span, :].astype(F32) + err[0, span, :]
            value_b[j * GROUP : (j + 1) * GROUP, :] = value.astype(BF16)
            each_row.append(kept[pl.ds(g, 1), :])
        for q in range(keep_n // SPAN):
            hits = []
            for row in each_row:
                hits.append(ladder(jnp.clip(row - q * SPAN, -1.0, SPAN), SPAN))
            acc[q * SPAN : (q + 1) * SPAN, :] += jnp.dot(
                jnp.concatenate(hits, axis=1), value_b[...], preferred_element_type=F32
            )

    def settle(i, _):
        for j in range(CHUNK // GROUP):
            g = i * (CHUNK // GROUP) + j
            span = pl.ds(pl.multiple_of(g * GROUP, GROUP), GROUP)
            stays = 1.0 - sent[pl.ds(g, 1), :]
            mask = jnp.dot(
                jnp.where(diagonal, stays, 0.0).astype(BF16),
                jnp.ones((GROUP, err.shape[2]), BF16),
                preferred_element_type=F32,
            )
            err[0, span, :] = (grad[span, :].astype(F32) + err[0, span, :]) * mask
        return 0

    pl.semaphore_wait(barrier, 10)
    greet(round_z, line["z"])

    raw_swaps = [
        copy(
            raw.at[1 - c, 0], state[0].at[mine_at[0], own_rows],
            raw_send, raw_recv, sibling,
        ),
        copy(
            raw_b.at[1 - c], state[1].at[mine_at[1], own_rows],
            rawb_send, rawb_recv, sibling,
        ),
    ]
    for go in raw_swaps:
        go.start()

    spread(0)
    mine = weights.at[x, z, y, c]
    copy(mine, mine, f_send, f_recv, sibling).start()

    pack(0)

    for go in raw_swaps:
        go.wait_recv()
    for a, order in enumerate(STATE_ORDERS):
        block = state[a].at[mine_at[a]]
        for k in (1, 2, 3):
            copy(
                block, block, s_send.at[a], s_recv.at[a], along(order[0], k)
            ).start()

    pl.semaphore_wait(round_z, 3)
    greet(round_x, line["x"])
    pack(1)
    pack(2)

    arrive(0)
    spread(1)
    pack(3)

    def place(a):
        order = STATE_ORDERS[a]
        bytes_of(state[a].at[pl.ds(0, 3)], s_send.at[a], s_recv.at[a]).wait_recv()
        shifts = {"x": 8, "z": 6, "y": 4}
        units = {"x": 16, "z": 4, "y": 1}
        hits = []
        for k in range(4):
            source = chip + (k - at[order[0]]) * units[order[0]]
            ranks = rooted[pl.ds(source, 1), :].astype(jnp.int32)
            first, second, third = ((ranks >> shifts[axis]) & 3 for axis in order)
            here = (ranks >= 0) & (first == at[order[0]])
            spot = second * (4 * UNIT) + third * UNIT + (ranks & (UNIT - 1))
            row = jnp.where(here, spot, -1).astype(F32)
            hits.append(ladder(row, 16 * UNIT))
        hits = jnp.concatenate(hits, axis=1)
        whole = state[a][...].reshape(4 * GROUP, -1)
        if a:
            split = whole
        else:
            high = whole.astype(BF16)
            rest = whole - high.astype(F32)
            middle = rest.astype(BF16)
            low = (rest - middle.astype(F32)).astype(BF16)
            split = jnp.concatenate([high, middle, low], axis=1)
        moved = jnp.dot(hits, split, preferred_element_type=F32)
        if not a:
            moved = (moved[:, :128] + moved[:, 128:256]) + moved[:, 256:]
        state1[a][...] = moved.astype(state1[a].dtype).reshape(state1[a].shape)

    def state_phase(phase, source, target):
        for a, order in enumerate(STATE_ORDERS):
            axis = order[phase]
            n = phase * 2 + a
            for k in (1, 2, 3):
                copy(
                    source[a].at[(at[axis] + k) % 4], target[a].at[k - 1],
                    s_send.at[n], s_recv.at[n], along(axis, k),
                ).start()

    def state_bytes(phase, target, a):
        n = phase * 2 + a
        return bytes_of(target[a], s_send.at[n], s_recv.at[n])

    def state_sum(phase, source, target, total):
        for a in range(2):
            state_bytes(phase, target, a).wait_recv()
        for a, order in enumerate(STATE_ORDERS):
            value = source[a][at[order[phase]]].astype(F32)
            for k in range(3):
                value = value + target[a][k].astype(F32)
            total[a][...] = value.astype(total[a].dtype)

    half_chips = chips // 2
    swaps = []
    for p in range(2):
        ranks = slice(p * keep_n // 2, (p + 1) * keep_n // 2)
        span = pl.ds(p * half_chips, half_chips)
        for h in range(2):
            packed[h, span] = (
                acc[ranks, h * 128 : (h + 1) * 128]
                .astype(BF16)
                .reshape(half_chips, UNIT, 128)
            )
        swap = copy(
            packed.at[1 - c, span], from_core.at[span],
            core_send.at[p], core_recv.at[p], sibling,
        )
        swap.start()
        swaps.append(swap)

    for a in range(2):
        place(a)
    state_phase(1, state1, sgot2)
    pl.semaphore_wait(round_x, 3)


    def scatter(k):
        other, peer = far(k)
        return copy(part.at[other], got.at[k - 1], rs_send, rs_recv, peer)

    for p in range(2):
        swaps[p].wait_recv()
        span = pl.ds(p * half_chips, half_chips)
        part[span] = (packed[c, span].astype(F32) + from_core[span].astype(F32)).astype(
            BF16
        )

    each(lambda k: scatter(k).start())
    own = packed[c, chip].astype(F32) + from_core[chip].astype(F32)
    forward(0)

    state_sum(1, state1, sgot2, state2)
    state_phase(2, state2, sgot3)

    arrive(1)
    spread(2)
    forward(1)

    state_sum(2, state2, sgot3, state3)
    scattered = bytes_of(got, rs_send, rs_recv)
    scattered.wait_recv()
    summed = (own + jnp.sum(got[...].astype(F32), axis=0)).astype(BF16)
    new_master, _, _ = adamw(
        master3[...], moment3[:, :128].astype(F32), moment3[:, 128:].astype(F32),
        summed.astype(F32),
    )
    result[c, chip, 0] = summed
    result[c, chip, 1] = new_master.astype(BF16)

    plane = chips // 4

    def gather(k):
        unit = result.at[c, chip]
        return copy(unit, unit, ag_send, ag_recv.at[x], far(k)[1])

    def pass_on(q):
        block = result.at[c, pl.ds(q * plane, plane)]
        return copy(block, block, half_send, half_recv, sibling)

    each(lambda k: gather(k).start())
    for k in range(keep_n // GROUP):
        lanes = (iota((64, GROUP), 1) + k * GROUP).astype(F32)
        expand[:, k * GROUP : (k + 1) * GROUP] = onehot(half == lanes)

    lax.fori_loop(0, chunks // 2, settle, 0)
    arrive(2)
    spread(3)
    forward(2)
    lax.fori_loop(chunks // 2, chunks, settle, 0)

    for k in (2, 3, 1):
        q = (x + k) % 4
        block = result.at[c, pl.ds(q * plane, plane)]
        bytes_of(block, ag_send, ag_recv.at[q]).wait_recv()
        pass_on(q).start()
    bytes_of(result.at[c, pl.ds(0, plane - 1)], ag_send, ag_recv.at[x]).wait_recv()
    pass_on(x).start()

    arrive(3)
    forward(3)

    scattered.wait_send()
    bytes_of(result.at[c, pl.ds(0, chips - 1)], ag_send, ag_recv.at[x]).wait_send()
    for go in raw_swaps:
        go.wait_send()
    for go in swaps:
        go.wait_send()
    for a in range(2):
        bytes_of(state[a].at[pl.ds(0, 3)], s_send.at[a], s_recv.at[a]).wait_send()
        state_bytes(1, sgot2, a).wait_send()
        state_bytes(2, sgot3, a).wait_send()
    for stage in range(4):
        stage_bytes(stage, w_send, w_recv).wait_send()
    bytes_of(weights.at[:, :, :, c], f_send, f_recv).wait()
    bytes_of(result.at[c], half_send, half_recv).wait()


def finish_kernel(
    err, weights, result, expand, rooted, starts_v, master, first, second,
    err_hbm, out_hbm, new_master, new_first, new_second,
    out, starts, err_sem, out_sem, starts_sem,
):
    groups = rooted.shape[0]
    to_smem = pltpu.make_async_copy(starts_v, starts, starts_sem)
    to_smem.start()
    rows = err.shape[1]
    pieces = err_sem.shape[0]
    copies = []
    for i in range(pieces):
        span = pl.ds(i * (rows // pieces), rows // pieces)
        go = pltpu.make_async_copy(err.at[0, span], err_hbm.at[0, span], err_sem.at[i])
        go.start()
        copies.append(go)

    to_smem.wait()
    units = result.shape[1]
    window = GROUP // UNIT + 1
    batch = groups // out_sem.shape[0]

    def store(i):
        span = pl.ds(i * batch, batch)
        return pltpu.make_async_copy(out.at[span], out_hbm.at[span], out_sem.at[i])

    def fill(i, _):
        for j in range(batch):
            g = i * batch + j
            unit = jnp.minimum(starts[g, 0] // UNIT, units - window)
            near = rooted[pl.ds(g, 1), :] - (unit * UNIT).astype(F32)
            hits = onehot(iota((window * UNIT, GROUP), 0).astype(F32) == near)
            held = jnp.concatenate(
                [
                    result[h, pl.ds(unit, window), 1].reshape(window * UNIT, 128)
                    for h in range(2)
                ],
                axis=1,
            )
            moved = lax.dot_general(
                hits, held, (((0,), (0,)), ((), ())), preferred_element_type=F32
            ).astype(BF16)
            for c in range(2):
                span = slice(c * 64, c * 64 + 64)
                for h in range(2):
                    lanes = slice(h * 128, h * 128 + 128)
                    out[g, span, lanes] = weights[g, c, h] + moved[span, lanes]
        store(i).start()
        return 0

    steps = out_sem.shape[0]
    lax.fori_loop(0, steps, fill, 0)
    total = jnp.concatenate(
        [
            jnp.dot(
                expand[...], result[h, :, 0].reshape(-1, 128),
                preferred_element_type=F32,
            )
            for h in range(2)
        ],
        axis=1,
    )
    new_master[...], new_first[...], new_second[...] = adamw(
        master[...], first[...], second[...], total
    )

    for go in copies:
        go.wait()
    lax.fori_loop(0, steps, lambda i, _: (store(i).wait(), 0)[1], 0)


def body(gradients, error_memory, block_lists, master, first_moment, second_moment):
    _, rows, width = gradients.shape
    owned = master.shape[0]
    levels, keep_n = block_lists.shape[1:]
    groups = rows // GROUP
    chunks = rows // CHUNK
    vmem = pl.BlockSpec(memory_space=pltpu.VMEM)
    anywhere = pl.BlockSpec(memory_space=pl.ANY)
    dma = pltpu.SemaphoreType.DMA

    err, weights, result, expand, rooted, starts = pl.pallas_call(
        merge_kernel,
        out_shape=(
            pltpu.VMEM((1, rows, width), F32),
            pltpu.VMEM((4, 4, 4, 2, 2, owned, 128), BF16),
            pltpu.VMEM((2, groups, 2, UNIT, 128), BF16),
            pltpu.VMEM((owned, keep_n), BF16),
            pltpu.VMEM((groups, GROUP), F32),
            pltpu.VMEM((groups, GROUP), jnp.int32),
        ),
        in_specs=[anywhere] * 6,
        out_specs=(vmem,) * 6,
        scratch_shapes=[
            pltpu.VMEM((rows, width), BF16),
            pltpu.VMEM((levels, keep_n), jnp.int32),
            pltpu.VMEM((2, 3, owned, 128), F32),
            pltpu.VMEM((2, owned, 256), BF16),
            pltpu.VMEM((keep_n, width), F32),
            pltpu.VMEM((groups, GROUP), F32),
            pltpu.VMEM((groups, GROUP), F32),
            pltpu.VMEM((GROUP, GROUP), F32),
            pltpu.VMEM((CHUNK, width), BF16),
            pltpu.VMEM((2, groups, UNIT, 128), BF16),
            pltpu.VMEM((groups, UNIT, 128), BF16),
            pltpu.VMEM((groups, UNIT, 128), BF16),
            pltpu.VMEM((groups - 1, UNIT, 128), BF16),
            *(
                pltpu.VMEM((*shape, lanes), kind)
                for lanes, kind in ((128, F32), (256, BF16))
                for shape in (
                    (4, GROUP), (4, 4, UNIT), (4, UNIT), (UNIT,),
                    (3, 4, UNIT), (3, UNIT),
                )
            ),
            dma((chunks,)), dma((chunks,)), dma, dma,
            dma((2,)), dma((2,)), dma, dma, dma, dma,
            dma, dma, dma, dma((4,)), dma, dma,
            dma((6,)), dma((6,)),
            dma((4,)), dma((4,)), dma, dma,
            pltpu.SemaphoreType.REGULAR, pltpu.SemaphoreType.REGULAR,
        ],
        compiler_params=pltpu.CompilerParams(
            collective_id=0, has_side_effects=True, vmem_limit_bytes=46 * MIB
        ),
        name="merge",
    )(gradients, error_memory, block_lists, master, first_moment, second_moment)

    new_errors, out, new_master, new_first, new_second = pl.pallas_call(
        finish_kernel,
        out_shape=(
            jax.ShapeDtypeStruct((1, rows, width), F32),
            jax.ShapeDtypeStruct((groups, GROUP, width), BF16),
            jax.ShapeDtypeStruct((owned, width), F32),
            jax.ShapeDtypeStruct((owned, width), F32),
            jax.ShapeDtypeStruct((owned, width), F32),
        ),
        in_specs=[vmem] * 9,
        out_specs=(anywhere, anywhere, vmem, vmem, vmem),
        scratch_shapes=[
            pltpu.VMEM((groups, GROUP, width), BF16),
            pltpu.SMEM((groups, GROUP), jnp.int32),
            dma((4,)), dma((8,)), dma,
        ],
        compiler_params=pltpu.CompilerParams(vmem_limit_bytes=32 * MIB),
        name="finish",
    )(
        err, weights.reshape(groups, 2, 2, owned, 128), result, expand, rooted, starts,
        master, first_moment, second_moment,
    )
    return new_errors, new_master, new_first, new_second, out.reshape(rows, width)


def solution(mesh):
    in_specs = (
        P("dp", None, None),
        P("dp", None, None),
        P("dp", None, None),
        P("dp", None),
        P("dp", None),
        P("dp", None),
    )
    out_specs = (P("dp", None, None), P("dp", None), P("dp", None), P("dp", None), P())
    return jax.shard_map(
        body, mesh=mesh, in_specs=in_specs, out_specs=out_specs, check_vma=False
    )
```
